512 devices in a mesh: site: 32 (over x, z), sp: 16 (over y, core).
Axes of the slice: x: 4, y: 8, z: 8, core: 2. Of those that a mesh axis runs over, the one named last changes fastest.
Arguments:
- presence: int32 [114688, 2048], P('site', 'sp'), may hold values 0 or 1
- utility_noise: bfloat16 [114688, 2048], P('site', 'sp'), may hold values from -5 to 5
- factors: float32 [16, 114688], P(None, 'site'), may hold values from -6 to 6
- loadings: float32 [16, 2048], P(None, 'sp'), may hold values from -0.3 to 0.3
- loading_precision: float32 [16, 2048], P(None, 'sp'), may hold values from 0.5 to 229376
- neighbours: int32 [15, 114688], P(None, 'site'), may hold values from -1 to 114686, as said below
- neighbour_weights: float32 [15, 114688], P(None, 'site'), may hold values from 0 to 0.1
- conditional_variance: float32 [114688], P('site'), may hold values from 0.1 to 1
- factor_noise: float32 [16, 114688], P(None, 'site'), may hold values from -5 to 5
Outputs:
- utilities: bfloat16 [114688, 2048], P('site', 'sp')
- new_loadings: float32 [16, 2048], P(None, 'sp')
- new_factors: float32 [16, 114688], P(None, 'site')
The draws below stay inside these ranges and needn't reach their ends.
Inputs may be any that keep to these rules, and one draw needn't show every extreme that they name: The k-th neighbour of site i (k from 0) is i - o with k * 96 + 1 <= o <= (k + 1) * 96, or -1 where that index would be negative; so all neighbours of a site are distinct, earlier, and at most 1440 sites before it. Every seventh site's last neighbour, where it is not -1, lies exactly 1440 sites before it, and the last site's first neighbour is the site just before it.
All inputs are finite; a program needn't handle non-finite values. No bound on the sum of `presence` on one device may be relied on, other than what follows from the above.
Results may differ from the reference program's by a relative error of at most 0.001.
Values sent between devices are 32-bit elements; how exact they have to be, the bound alone decides.
A program may use at most 128 MiB of HBM per device.

```python
import math
import jax
import jax.numpy as jnp
from jax import lax

S = 2048
K = 16
NBR = 15
REACH = 1440
R = 3584
SITES = 114688
N_SITE = 32


def draw_neighbours(key, part):
    step_size = REACH // NBR
    site_ids = jnp.arange(SITES, dtype=jnp.int32)
    jitter = jax.random.randint(key, (NBR, SITES), 0, step_size, dtype=jnp.int32)
    offsets = jnp.arange(NBR, dtype=jnp.int32)[:, None] * step_size + 1 + jitter
    last_row = jnp.where(site_ids % 7 == 0, REACH, offsets[NBR - 1])
    offsets = offsets.at[NBR - 1].set(last_row)
    first_row = jnp.where(site_ids == SITES - 1, 1, offsets[0])
    offsets = offsets.at[0].set(first_row)
    ids = site_ids[None, :] - offsets
    return jnp.where(ids >= 0, ids, -1).astype(jnp.int32)


def plant(values, stream_key, least, largest):
    shape = values.shape
    place = [jax.random.randint(jax.random.fold_in(stream_key, axis), (), 0, shape[axis]) for axis in range(len(shape))]
    values = values.at[tuple(place)].set(least)
    longest = shape.index(max(shape))
    place[longest] = (place[longest] + 1) % shape[longest]
    return values.at[tuple(place)].set(largest)


def levels(key, shape, cuts, least, high):
    factor_of = 1.0
    for position, shards_of in cuts:
        heights = jax.random.uniform(jax.random.fold_in(jax.random.fold_in(key, 6), position), (shards_of,), jnp.float32, least / len(cuts), high / len(cuts))
        factor_of = factor_of * jnp.repeat(jnp.exp(heights), shape[position] // shards_of).reshape((-1,) + (1,) * (len(shape) - 1 - position))
    return factor_of


def normal_values(own_key, shape, deviation, most, pieces=(), kind=jnp.bfloat16):
    values = deviation * jax.random.normal(own_key, shape, jnp.float32)
    if pieces:
        values = values * levels(own_key, shape, pieces, -0.22, 0.18)
    return jnp.clip(values, -most, most).astype(kind)


def setup_inputs(seed: int = 0) -> dict:
    keys = jax.random.split(jax.random.key(seed), 10)
    presence = plant((jax.random.randint(keys[0], (SITES, S), 0, 3) < 1).astype(jnp.int32), jax.random.fold_in(keys[0], 1), 0, 1)
    utility_noise = normal_values(keys[1], (SITES, S), 1.0, 5.0, ((0, 32), (1, 16)))
    factors = normal_values(keys[2], (K, SITES), 1.0, 6.0, ((1, 32),), jnp.float32)
    loadings = normal_values(keys[3], (K, S), 0.05, 0.3, ((1, 16),), jnp.float32)
    loading_precision = jnp.clip(jnp.exp(math.log(229376.0) - 13.036265 * jax.random.uniform(keys[4], (K, S), jnp.float32) ** levels(keys[4], (K, S), ((1, 16),), -0.2, 0.2)), 0.5, 229376.0)
    neighbours = draw_neighbours(jax.random.fold_in(keys[9], 71), 0)
    neighbour_weights = jnp.clip(0.1 * jax.random.uniform(keys[6], (NBR, SITES), jnp.float32) ** levels(keys[6], (NBR, SITES), ((1, 32),), -0.2, 0.2), 0.0, 0.1)
    conditional_variance = jnp.clip(jnp.exp(math.log(1.0) - 2.3025851 * jax.random.uniform(keys[7], (SITES,), jnp.float32) ** levels(keys[7], (SITES,), ((0, 32),), -0.2, 0.2)), 0.1, 1.0)
    factor_noise = normal_values(keys[8], (K, SITES), 1.0, 5.0, ((1, 32),), jnp.float32)
    return dict(presence=presence, utility_noise=utility_noise, factors=factors, loadings=loadings, loading_precision=loading_precision, neighbours=neighbours, neighbour_weights=neighbour_weights, conditional_variance=conditional_variance, factor_noise=factor_noise)


HIGH = lax.Precision.HIGHEST
inv_root_two_pi = 0.3989422804014327
inv_root_two = 0.7071067811865476

def utilities_block(eta_block, loadings, presence, noise):
    mean = jnp.dot(eta_block.T, loadings, precision=HIGH, preferred_element_type=jnp.float32)
    signs = (2 * presence - 1).astype(jnp.float32)
    shifted = signs * mean
    ratio = jnp.exp(-0.5 * shifted * shifted) * inv_root_two_pi / (0.5 * lax.erfc(-shifted * inv_root_two))
    spread = 1.0 - ratio * (ratio + shifted)
    return mean + signs * ratio + jnp.sqrt(spread) * noise.astype(jnp.float32)

def cholesky_solve(base, extra, rhs, noise):
    count = base.shape[0]
    lower = {}
    for j in range(count):
        accum = base[j, j] + extra[j]
        for k in range(j):
            accum = accum - lower[j, k] * lower[j, k]
        pivot = jnp.sqrt(accum)
        lower[j, j] = pivot
        for i in range(j + 1, count):
            accum = base[i, j] + jnp.zeros_like(pivot)
            for k in range(j):
                accum = accum - lower[i, k] * lower[j, k]
            lower[i, j] = accum / pivot
    middle = []
    for i in range(count):
        accum = rhs[i]
        for k in range(i):
            accum = accum - lower[i, k] * middle[k]
        value = accum / lower[i, i]
        if noise is not None:
            value = value + noise[i]
        middle.append(value)
    result = [None] * count
    for i in range(count - 1, -1, -1):
        accum = middle[i]
        for k in range(i + 1, count):
            accum = accum - lower[k, i] * result[k]
        result[i] = accum / lower[i, i]
    return jnp.stack(result, axis=0)

def prior_mean(window, ids, weights, anchor):
    local = ids - anchor
    valid = ids >= 0
    local = jnp.where(valid, local, 0).astype(jnp.int32)
    picked = jnp.take(window, local, axis=1)
    scaled = jnp.where(valid, weights, jnp.float32(0.0))
    return lax.optimization_barrier(jnp.sum(picked * scaled[None, :, :], axis=1))

def site_update(lgram, variance, pull, prior, noise):
    inverse = 1.0 / variance
    extra = jnp.broadcast_to(inverse[None, :], pull.shape)
    return cholesky_solve(lgram, extra, pull + prior * inverse[None, :], noise)

def reference(presence, utility_noise, factors, loadings, loading_precision, neighbours, neighbour_weights, conditional_variance, factor_noise):
    blocks_y = presence.reshape(N_SITE, R, S)
    blocks_noise = utility_noise.reshape(N_SITE, R, S)
    blocks_eta = factors.reshape(K, N_SITE, R).transpose(1, 0, 2)

    def first_pass(items):
        eta_block, y_block, noise_block = items
        draw = utilities_block(eta_block, loadings, y_block, noise_block)
        cross = jnp.dot(eta_block, draw, precision=HIGH, preferred_element_type=jnp.float32)
        return (draw.astype(jnp.bfloat16), cross)
    drawn, crosses = lax.map(first_pass, (blocks_eta, blocks_y, blocks_noise))
    cross = lax.optimization_barrier(jnp.sum(crosses, axis=0))
    gram = jnp.dot(factors, factors.T, precision=HIGH, preferred_element_type=jnp.float32)
    new_loadings = cholesky_solve(gram, loading_precision, cross, None)

    def second_pass(items):
        eta_block, y_block, noise_block = items
        draw = utilities_block(eta_block, loadings, y_block, noise_block)
        return lax.dot_general(new_loadings, draw, (((1,), (1,)), ((), ())), precision=HIGH, preferred_element_type=jnp.float32)
    pulls = lax.map(second_pass, (blocks_eta, blocks_y, blocks_noise))
    pull = pulls.transpose(1, 0, 2).reshape(K, SITES)
    lgram = jnp.dot(new_loadings, new_loadings.T, precision=HIGH, preferred_element_type=jnp.float32)
    prior = prior_mean(factors, neighbours, neighbour_weights, 0)
    new_factors = site_update(lgram, conditional_variance, pull, prior, factor_noise)
    return (drawn.reshape(SITES, S), new_loadings, new_factors)
```

```python
import functools

import jax
import jax.numpy as jnp
from jax import lax
from jax.experimental import pallas as pl
from jax.experimental.pallas import tpu as pltpu
from jax.sharding import PartitionSpec as P

F32 = jnp.float32
BF16 = jnp.bfloat16
MESH = pl.DeviceIdType.MESH

Z = 8
CORES = 2
K = 16
NBR = 15
CHUNK = 256
RIM = 1536
WINDOW = RIM + CHUNK
HALF = 8
STEP = 96

N_COEF = (0.7978845828848753, 0.561783412736638, 0.19921040380039692, 0.039025408597369395, 0.0036777514496204662)
D_COEF = (1.0, 1.1595221251207712, 0.6411219754723788, 0.20649649681102156, 0.03902744122918637, 0.003677727281734947)
inv_root_two_pi = 0.3989422804014327


def poly(coef, u):
    acc = u * coef[-1] + coef[-2]
    for a in coef[-3::-1]:
        acc = acc * u + a
    return acc


def split(x):
    hi = x.astype(BF16)
    return hi, (x - hi.astype(F32)).astype(BF16)


def dot(a, b, dims):
    return lax.dot_general(a, b, (dims, ((), ())), preferred_element_type=F32)


def blocks_sum(p, rows, cols):
    return (p[:rows, :cols] + p[:rows, cols:]) + (p[rows:, :cols] + p[rows:, cols:])


def cholesky(base, extra):
    width = extra[0].shape[1]
    row = lax.broadcasted_iota(jnp.int32, (HALF, width), 0)
    top, bot = [], []
    for k in range(K):
        diag = jnp.where(row == k % HALF, extra[k], 0.0)
        column = base[:, k : k + 1]
        if k < HALF:
            top.append(column[:HALF] + diag)
            bot.append(column[HALF:] + jnp.zeros_like(diag))
        else:
            top.append(None)
            bot.append(column[HALF:] + diag)
    scales = []
    for j in range(K):
        d = top[j][j : j + 1] if j < HALF else bot[j][j - HALF : j - HALF + 1]
        r = lax.rsqrt(d)
        scales.append(r)
        bot[j] = bot[j] * r
        if j < HALF:
            top[j] = top[j] * r
        for k in range(j + 1, K):
            if k < HALF:
                s = top[j][k : k + 1]
                top[k] = top[k] - top[j] * s
                bot[k] = bot[k] - bot[j] * s
            else:
                bot[k] = bot[k] - bot[j] * bot[j][k - HALF : k - HALF + 1]
    return top, bot, scales


def solve(factor, rhs, noise):
    top, bot, scales = factor
    rt, rb = rhs[:HALF], rhs[HALF:]
    middle = []
    for j in range(K):
        y = (rt[j : j + 1] if j < HALF else rb[j - HALF : j - HALF + 1]) * scales[j]
        if noise is not None:
            y = y + noise[j : j + 1]
        middle.append(y)
        if j < HALF:
            rt = rt - top[j] * y
        rb = rb - bot[j] * y
    row = lax.broadcasted_iota(jnp.int32, rt.shape, 0)
    xt, xb = jnp.zeros_like(rt), jnp.zeros_like(rt)
    for j in range(K - 1, -1, -1):
        terms = bot[j] * xb
        if j < HALF:
            terms = terms + top[j] * xt
        x = (middle[j] - jnp.sum(terms, axis=0, keepdims=True)) * scales[j]
        if j < HALF:
            xt = jnp.where(row == j, x, xt)
        else:
            xb = jnp.where(row == j - HALF, x, xb)
    return jnp.concatenate([xt, xb], axis=0)


def kernel(
    n_site,
    n_sp,
    presence,
    noise,
    factors,
    loadings,
    precision,
    neighbours,
    weights,
    variance,
    factor_noise,
    utilities,
    new_loadings,
    new_factors,
    fs,
    draws,
    window,
    onehot,
    gram_z,
    gram_x,
    cross_z,
    cross_x,
    lgram_mine,
    lgram_pair,
    lgram_y,
    pull_out,
    pull_pair,
    pull_mine,
    pull_y,
    rim_sems,
    gz_sems,
    gx_sems,
    cz_sems,
    cx_sems,
    lp_sems,
    ly_sems,
    pp_sems,
    py_sems,
    fy_sems,
    fp_sems,
):
    nx = n_site // Z
    ny = n_sp // CORES
    busy = ny - 1
    rows = factors.shape[1]
    species = loadings.shape[1]
    steps = rows // CHUNK

    site = lax.axis_index("site")
    sp = lax.axis_index("sp")
    x, z = site // Z, site % Z
    y, core = sp // CORES, sp % CORES
    pair = y * CORES + (1 - core)
    ahead = (site + 1) % n_site
    behind = (site + n_site - 1) % n_site

    def z_peer(d):
        return x * Z + (z + d) % Z

    def x_peer(d):
        return ((x + d) % nx) * Z + z

    barrier = pltpu.get_barrier_semaphore()
    greeted = [{"site": z_peer(d)} for d in range(1, Z)]
    greeted += [{"site": x_peer(d)} for d in range(1, nx)]
    greeted += [{"site": ahead}, {"site": behind}]
    greeted += [{"sp": ((y + d) % ny) * CORES + core} for d in range(1, ny)]
    greeted += [{"sp": pair}]
    for peer in greeted:
        pl.semaphore_signal(barrier, inc=1, device_id=peer, device_id_type=MESH)

    def remote(src, dst, sems, send, recv, peer):
        return pltpu.make_async_remote_copy(
            src_ref=src,
            dst_ref=dst,
            send_sem=sems.at[0, send],
            recv_sem=sems.at[1, recv],
            device_id=peer,
            device_id_type=MESH,
        )

    def spread_z(buf, sems):
        copies = []
        for d in range(1, Z):
            copy = remote(buf.at[z], buf.at[z], sems, d, d, {"site": z_peer(d)})
            copy.start()
            copies.append(copy)
        return copies

    def spread_x(buf, sems):
        copies = []
        for d in range(1, nx):
            copy = remote(buf.at[x], buf.at[x], sems, d, d, {"site": x_peer(d)})
            copy.start()
            copies.append(copy)
        return copies

    def gather_z(buf, sems):
        for d in range(1, Z):
            s = (z + Z - d) % Z
            remote(buf.at[s], buf.at[s], sems, d, d, {"site": z_peer(d)}).wait_recv()
        acc = buf[0]
        for s in range(1, Z):
            acc = acc + buf[s]
        return acc

    def gather_x(buf, sems):
        for d in range(1, nx):
            s = (x + nx - d) % nx
            remote(buf.at[s], buf.at[s], sems, d, d, {"site": x_peer(d)}).wait_recv()
        acc = buf[0]
        for s in range(1, nx):
            acc = acc + buf[s]
        return acc

    started = []

    f = factors[...]
    hi, lo = split(f)
    fs[0:16, :] = hi
    fs[16:32, :] = lo
    fs[32:48, :] = hi
    window[:, RIM:] = f
    l_hi, l_lo = split(loadings[...])
    ls = jnp.concatenate([l_hi, l_hi, l_lo], axis=0)

    both = jnp.concatenate([hi, lo], axis=0)
    products = dot(both, both, ((1,), (1,)))
    gram_part = blocks_sum(products, K, K)
    zeros = jnp.zeros((K, species), F32)
    gram_z[z] = zeros
    gram_z[z, :, 0:K] = gram_part

    pl.semaphore_wait(barrier, len(greeted))

    rim = remote(
        factors.at[:, rows - RIM : rows],
        window.at[:, 0:RIM],
        rim_sems,
        0,
        0,
        {"site": ahead},
    )
    started += spread_z(gram_z, gz_sems)
    rim.start()
    started.append(rim)

    def draw_step(i, acc):
        r0 = pl.multiple_of(i * CHUNK, CHUNK)
        mean = dot(fs[:, pl.ds(r0, CHUNK)], ls, ((0,), (0,)))
        there = presence[pl.ds(r0, CHUNK), :] > 0
        t = jnp.where(there, mean, -mean)
        u = jnp.abs(t)
        density = jnp.exp(-0.5 * t * t) * inv_root_two_pi
        num = poly(N_COEF, u)
        den = poly(D_COEF, u)
        full = u * den + num
        negative = t < 0.0
        v = jnp.where(negative, num, density * full) / jnp.where(negative, den, full - density * den)
        s = v + jnp.maximum(t, 0.0)
        spread = jnp.maximum(1.0 - v * (v + u), 0.0)
        draw = jnp.where(there, s, -s) + jnp.sqrt(spread) * noise[pl.ds(r0, CHUNK), :].astype(F32)
        d_hi, d_lo = split(draw)
        utilities[pl.ds(r0, CHUNK), :] = d_hi
        pieces = jnp.concatenate([d_hi, d_lo], axis=1)
        draws[pl.ds(r0, CHUNK), :] = pieces
        return acc + dot(fs[0:32, pl.ds(r0, CHUNK)], pieces, ((1,), (0,)))

    acc = jnp.zeros((2 * K, 2 * species), F32)
    acc = lax.fori_loop(0, steps // 2, draw_step, acc)
    gram_x[x] = gather_z(gram_z, gz_sems)
    started += spread_x(gram_x, gx_sems)
    acc = lax.fori_loop(steps // 2, steps, draw_step, acc)
    cross_z[z] = blocks_sum(acc, K, species)
    started += spread_z(cross_z, cz_sems)

    gram = gather_x(gram_x, gx_sems)[:, 0:K]
    factor = cholesky(gram, [precision[k : k + 1, :] for k in range(K)])
    cross_x[x] = gather_z(cross_z, cz_sems)
    started += spread_x(cross_x, cx_sems)

    chunk = jnp.minimum(sp, CORES * busy - 1)
    c0 = pl.multiple_of(chunk * CHUNK, CHUNK)
    base = site * rows + chunk * CHUNK - RIM
    onehot[...] = jnp.zeros_like(onehot)
    iota = lax.broadcasted_iota(jnp.int32, (224, 128), 0)

    def mark(k, carry):
        ids = neighbours[pl.ds(k, 1), pl.ds(c0, CHUNK)]
        w = jnp.where(ids >= 0, weights[pl.ds(k, 1), pl.ds(c0, CHUNK)], 0.0)
        for q in range(CHUNK // 128):
            first = pl.multiple_of(RIM - STEP + 128 * q - STEP * k, 32)
            lanes = slice(128 * q, 128 * (q + 1))
            hit = iota == ids[:, lanes] - (base + first)
            onehot[pl.ds(first, 224), lanes] += jnp.where(hit, w[:, lanes], 0.0)
        return carry

    lax.fori_loop(0, NBR, mark, 0)
    rim.wait_recv()

    def gather_step(b, acc):
        r0 = pl.multiple_of(b * 256, 256)
        m_hi, m_lo = split(onehot[pl.ds(r0, 256), :])
        w_hi, w_lo = split(window[:, pl.ds(pl.multiple_of(c0 + r0, 256), 256)])
        return acc + dot(
            jnp.concatenate([w_hi, w_lo], axis=0),
            jnp.concatenate([m_hi, m_lo], axis=1),
            ((1,), (0,)),
        )

    prior = lax.fori_loop(0, WINDOW // 256, gather_step, jnp.zeros((2 * K, 2 * CHUNK), F32))
    prior = blocks_sum(prior, K, CHUNK)
    inverse = 1.0 / variance[:, pl.ds(c0, CHUNK)]
    shift = prior * inverse

    cross = gather_x(cross_x, cx_sems)
    fresh = solve(factor, cross, None)
    new_loadings[...] = fresh

    n_hi, n_lo = split(fresh)
    narrow = jnp.concatenate([n_hi, n_lo], axis=0)
    lgram_part = blocks_sum(dot(narrow, narrow, ((1,), (1,))), K, K)
    lgram_mine[...] = zeros
    lgram_mine[:, 0:K] = lgram_part
    copy = remote(lgram_mine, lgram_pair, lp_sems, 0, 0, {"sp": pair})
    copy.start()
    started.append(copy)

    zero = jnp.zeros_like(n_hi)
    wide = jnp.concatenate(
        [jnp.concatenate([n_hi, n_hi], axis=1), jnp.concatenate([n_lo, zero], axis=1)],
        axis=0,
    )

    def pull_of(t, c):
        r0 = pl.multiple_of((t * CORES + c) * CHUNK, CHUNK)
        p = dot(wide, draws[pl.ds(r0, CHUNK), :], ((1,), (1,)))
        return p[:K] + p[K:]

    for e in range(1, busy + 1):
        t = (y + e) % busy
        pull_out[e - 1] = pull_of(t, 1 - core)
        copy = remote(pull_out.at[e - 1], pull_pair.at[e - 1], pp_sems, e - 1, e - 1, {"sp": pair})
        copy.start()
        started.append(copy)

    remote(lgram_mine, lgram_pair, lp_sems, 0, 0, {"sp": pair}).wait_recv()
    lgram_y[y] = lgram_mine[...] + lgram_pair[...]
    for d in range(1, ny):
        peer = {"sp": ((y + d) % ny) * CORES + core}
        copy = remote(lgram_y.at[y], lgram_y.at[y], ly_sems, d, d, peer)
        copy.start()
        started.append(copy)

    for e in range(1, busy + 1):
        t = (y + e) % busy
        mine = pull_of(t, core)
        remote(pull_out.at[e - 1], pull_pair.at[e - 1], pp_sems, e - 1, e - 1, {"sp": pair}).wait_recv()
        pull_mine[e - 1] = mine + pull_pair[e - 1]
        copy = remote(pull_mine.at[e - 1], pull_y.at[y], py_sems, e, y, {"sp": t * CORES + core})
        if e < busy:
            copy.start()
            started.append(copy)
        else:

            @pl.when(y == busy)
            def _():
                copy.start()

            last_pull = copy

    for d in range(1, ny):
        s = (y + ny - d) % ny
        peer = {"sp": ((y + d) % ny) * CORES + core}
        remote(lgram_y.at[s], lgram_y.at[s], ly_sems, d, d, peer).wait_recv()

    def factors_to(sems, send, recv, index, peer):
        lanes = pl.ds(pl.multiple_of(index * CHUNK, CHUNK), CHUNK)
        return remote(new_factors.at[:, lanes], new_factors.at[:, lanes], sems, send, recv, peer)

    @pl.when(y < busy)
    def _():
        lgram = lgram_y[0]
        for s in range(1, ny):
            lgram = lgram + lgram_y[s]
        site_factor = cholesky(lgram[:, 0:K], [inverse] * K)
        total = pull_mine[busy - 1] + shift
        for d in range(1, ny):
            s = (y + d) % ny
            remote(pull_y.at[s], pull_y.at[s], py_sems, 0, s, {"sp": s * CORES + core}).wait_recv()
            total = total + pull_y[s]
        result = solve(site_factor, total, factor_noise[:, pl.ds(c0, CHUNK)])
        new_factors[:, pl.ds(c0, CHUNK)] = result
        for d in range(1, ny):
            t = (y + d) % ny
            factors_to(fy_sems, d, y, y * CORES + core, {"sp": t * CORES + core}).start()
        factors_to(fp_sems, y, y, y * CORES + core, {"sp": pair}).start()

    for e in range(1, busy + 1):
        s = (y + busy - e) % busy

        def hand_on():
            factors_to(fy_sems, 0, s, s * CORES + core, {"sp": s * CORES + core}).wait_recv()
            factors_to(fp_sems, s, s, s * CORES + core, {"sp": pair}).start()

        if e < busy:
            hand_on()
        else:
            pl.when(y == busy)(hand_on)

    for s in range(busy):
        factors_to(fp_sems, s, s, s * CORES + (1 - core), {"sp": pair}).wait_recv()

    for copy in started:
        copy.wait_send()
    for s in range(busy):
        factors_to(fp_sems, s, s, s * CORES + core, {"sp": pair}).wait_send()

    @pl.when(y == busy)
    def _():
        last_pull.wait_send()

    @pl.when(y < busy)
    def _():
        for d in range(1, ny):
            t = (y + d) % ny
            factors_to(fy_sems, d, y, y * CORES + core, {"sp": t * CORES + core}).wait_send()


def solution(mesh):
    n_site, n_sp = mesh.shape["site"], mesh.shape["sp"]
    nx, ny = n_site // Z, n_sp // CORES
    busy = ny - 1

    def shards(presence, noise, factors, loadings, precision, neighbours, weights, variance, factor_noise):
        rows, species = presence.shape
        assert rows == busy * CORES * CHUNK and species == 128
        vmem = pl.BlockSpec(memory_space=pltpu.VMEM)
        sems = pltpu.SemaphoreType.DMA
        return pl.pallas_call(
            functools.partial(kernel, n_site, n_sp),
            out_shape=(
                jax.ShapeDtypeStruct((rows, species), BF16),
                jax.ShapeDtypeStruct((K, species), F32),
                jax.ShapeDtypeStruct((K, rows), F32),
            ),
            in_specs=[vmem] * 9,
            out_specs=(vmem,) * 3,
            scratch_shapes=[
                pltpu.VMEM((3 * K, rows), BF16),
                pltpu.VMEM((rows, 2 * species), BF16),
                pltpu.VMEM((K, RIM + rows), F32),
                pltpu.VMEM((WINDOW, CHUNK), F32),
                pltpu.VMEM((Z, K, species), F32),
                pltpu.VMEM((nx, K, species), F32),
                pltpu.VMEM((Z, K, species), F32),
                pltpu.VMEM((nx, K, species), F32),
                pltpu.VMEM((K, species), F32),
                pltpu.VMEM((K, species), F32),
                pltpu.VMEM((ny, K, species), F32),
                pltpu.VMEM((busy, K, CHUNK), F32),
                pltpu.VMEM((busy, K, CHUNK), F32),
                pltpu.VMEM((busy, K, CHUNK), F32),
                pltpu.VMEM((ny, K, CHUNK), F32),
                sems((2, 1)),
                sems((2, Z)),
                sems((2, nx)),
                sems((2, Z)),
                sems((2, nx)),
                sems((2, 1)),
                sems((2, ny)),
                sems((2, busy)),
                sems((2, ny)),
                sems((2, ny)),
                sems((2, busy)),
            ],
            compiler_params=pltpu.CompilerParams(
                collective_id=0,
                has_side_effects=True,
                vmem_limit_bytes=40 * 1024 * 1024,
            ),
        )(presence, noise, factors, loadings, precision, neighbours, weights, variance.reshape(1, rows), factor_noise)

    in_specs = (
        P("site", "sp"),
        P("site", "sp"),
        P(None, "site"),
        P(None, "sp"),
        P(None, "sp"),
        P(None, "site"),
        P(None, "site"),
        P("site"),
        P(None, "site"),
    )
    out_specs = (P("site", "sp"), P(None, "sp"), P(None, "site"))
    return jax.shard_map(shards, mesh=mesh, in_specs=in_specs, out_specs=out_specs, check_vma=False)
```

```python
import functools

import jax
import jax.numpy as jnp
from jax import lax
from jax.experimental import pallas as pl
from jax.experimental.pallas import tpu as pltpu
from jax.sharding import PartitionSpec as P

F32 = jnp.float32
BF16 = jnp.bfloat16
MESH = pl.DeviceIdType.MESH

Z = 8
CORES = 2
K = 16
NBR = 15
CHUNK = 256
RIM = 1536
WINDOW = RIM + CHUNK
HALF = 8
STEP = 96

N_COEF = (0.7978845828848753, 0.561783412736638, 0.19921040380039692, 0.039025408597369395, 0.0036777514496204662)
D_COEF = (1.0, 1.1595221251207712, 0.6411219754723788, 0.20649649681102156, 0.03902744122918637, 0.003677727281734947)
inv_root_two_pi = 0.3989422804014327


def poly(coef, u):
    acc = u * coef[-1] + coef[-2]
    for a in coef[-3::-1]:
        acc = acc * u + a
    return acc


def split(x):
    hi = x.astype(BF16)
    return hi, (x - hi.astype(F32)).astype(BF16)


def dot(a, b, dims):
    return lax.dot_general(a, b, (dims, ((), ())), preferred_element_type=F32)


def blocks_sum(p, rows, cols):
    return (p[:rows, :cols] + p[:rows, cols:]) + (p[rows:, :cols] + p[rows:, cols:])


def cholesky(base, extra):
    width = extra[0].shape[1]
    row = lax.broadcasted_iota(jnp.int32, (HALF, width), 0)
    top, bot = [], []
    for k in range(K):
        diag = jnp.where(row == k % HALF, extra[k], 0.0)
        column = base[:, k : k + 1]
        if k < HALF:
            top.append(column[:HALF] + diag)
            bot.append(column[HALF:] + jnp.zeros_like(diag))
        else:
            top.append(None)
            bot.append(column[HALF:] + diag)
    scales = []
    for j in range(K):
        d = top[j][j : j + 1] if j < HALF else bot[j][j - HALF : j - HALF + 1]
        r = lax.rsqrt(d)
        scales.append(r)
        bot[j] = bot[j] * r
        if j < HALF:
            top[j] = top[j] * r
        for k in range(j + 1, K):
            if k < HALF:
                s = top[j][k : k + 1]
                top[k] = top[k] - top[j] * s
                bot[k] = bot[k] - bot[j] * s
            else:
                bot[k] = bot[k] - bot[j] * bot[j][k - HALF : k - HALF + 1]
    return top, bot, scales


def solve(factor, rhs, noise):
    top, bot, scales = factor
    rt, rb = rhs[:HALF], rhs[HALF:]
    middle = []
    for j in range(K):
        y = (rt[j : j + 1] if j < HALF else rb[j - HALF : j - HALF + 1]) * scales[j]
        if noise is not None:
            y = y + noise[j : j + 1]
        middle.append(y)
        if j < HALF:
            rt = rt - top[j] * y
        rb = rb - bot[j] * y
    row = lax.broadcasted_iota(jnp.int32, rt.shape, 0)
    xt, xb = jnp.zeros_like(rt), jnp.zeros_like(rt)
    for j in range(K - 1, -1, -1):
        terms = bot[j] * xb
        if j < HALF:
            terms = terms + top[j] * xt
        x = (middle[j] - jnp.sum(terms, axis=0, keepdims=True)) * scales[j]
        if j < HALF:
            xt = jnp.where(row == j, x, xt)
        else:
            xb = jnp.where(row == j - HALF, x, xb)
    return jnp.concatenate([xt, xb], axis=0)


def far_first(n):
    return sorted(range(1, n), key=lambda d: -min(d, n - d))


def kernel(
    n_site,
    n_sp,
    presence_hbm,
    noise_hbm,
    factors_hbm,
    loadings_hbm,
    precision_hbm,
    neighbours_hbm,
    weights_hbm,
    variance_hbm,
    factor_noise_hbm,
    utilities_hbm,
    new_loadings_hbm,
    new_factors_hbm,
    utilities,
    new_loadings,
    new_factors,
    out_sems,
    presence,
    noise,
    factors,
    loadings,
    precision,
    neighbours,
    weights,
    variance,
    factor_noise,
    in_sems,
    fs,
    draws,
    window,
    onehot,
    gram_z,
    gram_x,
    cross_z,
    cross_x,
    lgram_mine,
    lgram_pair,
    lgram_y,
    pull_out,
    pull_pair,
    pull_mine,
    pull_y,
    rim_sems,
    gz_sems,
    gx_sems,
    cz_sems,
    cx_sems,
    lp_sems,
    ly_sems,
    pp_sems,
    py_sems,
    fy_sems,
    fp_sems,
):
    nx = n_site // Z
    ny = n_sp // CORES
    busy = ny - 1
    rows = factors.shape[1]
    steps = rows // CHUNK
    cuts = (0, min(2, steps // 2) * CHUNK, steps // 2 * CHUNK, rows)
    species = loadings.shape[1]

    site = lax.axis_index("site")
    sp = lax.axis_index("sp")
    x, z = site // Z, site % Z
    y, core = sp // CORES, sp % CORES
    pair = y * CORES + (1 - core)
    ahead = (site + 1) % n_site
    behind = (site + n_site - 1) % n_site

    def z_peer(d):
        return x * Z + (z + d) % Z

    def x_peer(d):
        return ((x + d) % nx) * Z + z

    barrier = pltpu.get_barrier_semaphore()
    greeted = [{"site": z_peer(d)} for d in range(1, Z)]
    greeted += [{"site": x_peer(d)} for d in range(1, nx)]
    greeted += [{"site": ahead}, {"site": behind}]
    greeted += [{"sp": ((y + d) % ny) * CORES + core} for d in range(1, ny)]
    greeted += [{"sp": pair}]
    for peer in greeted:
        pl.semaphore_signal(barrier, inc=1, device_id=peer, device_id_type=MESH)

    def remote(src, dst, sems, send, recv, peer):
        return pltpu.make_async_remote_copy(
            src_ref=src,
            dst_ref=dst,
            send_sem=sems.at[0, send],
            recv_sem=sems.at[1, recv],
            device_id=peer,
            device_id_type=MESH,
        )

    def spread_z(buf, sems):
        copies = []
        for d in far_first(Z):
            copy = remote(buf.at[z], buf.at[z], sems, d, d, {"site": z_peer(d)})
            copy.start()
            copies.append(copy)
        return copies

    def spread_x(buf, sems):
        copies = []
        for d in far_first(nx):
            copy = remote(buf.at[x], buf.at[x], sems, d, d, {"site": x_peer(d)})
            copy.start()
            copies.append(copy)
        return copies

    def gather_z(buf, sems):
        for d in range(1, Z):
            s = (z + Z - d) % Z
            remote(buf.at[s], buf.at[s], sems, d, d, {"site": z_peer(d)}).wait_recv()
        acc = buf[0]
        for s in range(1, Z):
            acc = acc + buf[s]
        return acc

    def gather_x(buf, sems):
        for d in range(1, nx):
            s = (x + nx - d) % nx
            remote(buf.at[s], buf.at[s], sems, d, d, {"site": x_peer(d)}).wait_recv()
        acc = buf[0]
        for s in range(1, nx):
            acc = acc + buf[s]
        return acc

    chunk = jnp.minimum(sp, CORES * busy - 1)
    c0 = pl.multiple_of(chunk * CHUNK, CHUNK)
    mine = pl.ds(c0, CHUNK)
    loads = [(factors_hbm, factors), (loadings_hbm, loadings)]
    for a, b in zip(cuts, cuts[1:]):
        loads.append((presence_hbm.at[a:b], presence.at[a:b]))
        loads.append((noise_hbm.at[a:b], noise.at[a:b]))
    loads += [
        (neighbours_hbm.at[:, mine], neighbours),
        (weights_hbm.at[:, mine], weights),
        (precision_hbm, precision),
        (variance_hbm.at[:, mine], variance),
        (factor_noise_hbm.at[:, mine], factor_noise),
    ]
    loads = [pltpu.make_async_copy(a, b, in_sems.at[i]) for i, (a, b) in enumerate(loads)]
    for load in loads:
        load.start()
    started = []

    loads[0].wait()
    loads[1].wait()
    f = factors[...]
    hi, lo = split(f)
    fs[0:16, :] = hi
    fs[16:32, :] = lo
    fs[32:48, :] = hi
    window[:, RIM:] = f
    l_hi, l_lo = split(loadings[...])
    ls = jnp.concatenate([l_hi, l_hi, l_lo], axis=0)

    both = jnp.concatenate([hi, lo], axis=0)
    products = dot(both, both, ((1,), (1,)))
    gram_part = blocks_sum(products, K, K)
    zeros = jnp.zeros((K, species), F32)
    gram_z[z] = zeros
    gram_z[z, :, 0:K] = gram_part

    def draw_step(i, acc):
        r0 = pl.multiple_of(i * CHUNK, CHUNK)
        mean = dot(fs[:, pl.ds(r0, CHUNK)], ls, ((0,), (0,)))
        there = presence[pl.ds(r0, CHUNK), :] > 0
        t = jnp.where(there, mean, -mean)
        u = jnp.abs(t)
        density = jnp.exp(-0.5 * t * t) * inv_root_two_pi
        num = poly(N_COEF, u)
        den = poly(D_COEF, u)
        full = u * den + num
        negative = t < 0.0
        v = jnp.where(negative, num, density * full) / jnp.where(negative, den, full - density * den)
        s = v + jnp.maximum(t, 0.0)
        spread = jnp.maximum(1.0 - v * (v + u), 0.0)
        draw = jnp.where(there, s, -s) + jnp.sqrt(spread) * noise[pl.ds(r0, CHUNK), :].astype(F32)
        d_hi, d_lo = split(draw)
        utilities[pl.ds(r0, CHUNK), :] = d_hi
        pieces = jnp.concatenate([d_hi, d_lo], axis=1)
        draws[pl.ds(r0, CHUNK), :] = pieces
        return acc + dot(fs[0:32, pl.ds(r0, CHUNK)], pieces, ((1,), (0,)))

    acc = jnp.zeros((2 * K, 2 * species), F32)
    for piece in range(2):
        loads[2 + 2 * piece].wait()
        loads[3 + 2 * piece].wait()
        acc = lax.fori_loop(cuts[piece] // CHUNK, cuts[piece + 1] // CHUNK, draw_step, acc)

    pl.semaphore_wait(barrier, len(greeted))

    rim = remote(
        factors.at[:, rows - RIM : rows],
        window.at[:, 0:RIM],
        rim_sems,
        0,
        0,
        {"site": ahead},
    )
    started += spread_z(gram_z, gz_sems)
    rim.start()
    started.append(rim)

    loads[6].wait()
    loads[7].wait()
    acc = lax.fori_loop(cuts[2] // CHUNK, steps, draw_step, acc)
    cross_z[z] = blocks_sum(acc, K, species)
    started += spread_z(cross_z, cz_sems)
    stores = [pltpu.make_async_copy(utilities, utilities_hbm, out_sems.at[0])]
    stores[0].start()
    gram_x[x] = gather_z(gram_z, gz_sems)
    started += spread_x(gram_x, gx_sems)

    for load in loads[8:]:
        load.wait()
    base = site * rows + chunk * CHUNK - RIM
    onehot[...] = jnp.zeros_like(onehot)
    iota = lax.broadcasted_iota(jnp.int32, (224, 128), 0)

    def mark(k, carry):
        ids = neighbours[pl.ds(k, 1), :]
        w = jnp.where(ids >= 0, weights[pl.ds(k, 1), :], 0.0)
        for q in range(CHUNK // 128):
            first = pl.multiple_of(RIM - STEP + 128 * q - STEP * k, 32)
            lanes = slice(128 * q, 128 * (q + 1))
            hit = iota == ids[:, lanes] - (base + first)
            onehot[pl.ds(first, 224), lanes] += jnp.where(hit, w[:, lanes], 0.0)
        return carry

    lax.fori_loop(0, NBR, mark, 0)
    rim.wait_recv()

    def gather_step(b, acc):
        r0 = pl.multiple_of(b * 256, 256)
        m_hi, m_lo = split(onehot[pl.ds(r0, 256), :])
        w_hi, w_lo = split(window[:, pl.ds(pl.multiple_of(c0 + r0, 256), 256)])
        return acc + dot(
            jnp.concatenate([w_hi, w_lo], axis=0),
            jnp.concatenate([m_hi, m_lo], axis=1),
            ((1,), (0,)),
        )

    prior = lax.fori_loop(0, WINDOW // 256, gather_step, jnp.zeros((2 * K, 2 * CHUNK), F32))
    prior = blocks_sum(prior, K, CHUNK)
    inverse = 1.0 / variance[...]
    shift = prior * inverse

    cross_x[x] = gather_z(cross_z, cz_sems)
    started += spread_x(cross_x, cx_sems)

    gram = gather_x(gram_x, gx_sems)[:, 0:K]
    factor = cholesky(gram, [precision[k : k + 1, :] for k in range(K)])

    cross = gather_x(cross_x, cx_sems)
    fresh = solve(factor, cross, None)
    new_loadings[...] = fresh
    stores.append(pltpu.make_async_copy(new_loadings, new_loadings_hbm, out_sems.at[1]))
    stores[1].start()

    n_hi, n_lo = split(fresh)
    narrow = jnp.concatenate([n_hi, n_lo], axis=0)
    lgram_part = blocks_sum(dot(narrow, narrow, ((1,), (1,))), K, K)
    lgram_mine[...] = zeros
    lgram_mine[:, 0:K] = lgram_part
    copy = remote(lgram_mine, lgram_pair, lp_sems, 0, 0, {"sp": pair})
    copy.start()
    started.append(copy)

    zero = jnp.zeros_like(n_hi)
    wide = jnp.concatenate(
        [jnp.concatenate([n_hi, n_hi], axis=1), jnp.concatenate([n_lo, zero], axis=1)],
        axis=0,
    )

    def pull_of(t, c):
        r0 = pl.multiple_of((t * CORES + c) * CHUNK, CHUNK)
        p = dot(wide, draws[pl.ds(r0, CHUNK), :], ((1,), (1,)))
        return p[:K] + p[K:]

    order = far_first(ny)
    order.remove(busy)
    order.append(busy)
    for e in order:
        t = (y + e) % busy
        pull_out[e - 1] = pull_of(t, 1 - core)
        copy = remote(pull_out.at[e - 1], pull_pair.at[e - 1], pp_sems, e - 1, e - 1, {"sp": pair})
        copy.start()
        started.append(copy)

    remote(lgram_mine, lgram_pair, lp_sems, 0, 0, {"sp": pair}).wait_recv()
    lgram_y[y] = lgram_mine[...] + lgram_pair[...]
    for d in far_first(ny):
        peer = {"sp": ((y + d) % ny) * CORES + core}
        copy = remote(lgram_y.at[y], lgram_y.at[y], ly_sems, d, d, peer)
        copy.start()
        started.append(copy)

    for e in order:
        t = (y + e) % busy
        part = pull_of(t, core)
        remote(pull_out.at[e - 1], pull_pair.at[e - 1], pp_sems, e - 1, e - 1, {"sp": pair}).wait_recv()
        pull_mine[e - 1] = part + pull_pair[e - 1]
        copy = remote(pull_mine.at[e - 1], pull_y.at[y], py_sems, e, y, {"sp": t * CORES + core})
        if e < busy:
            copy.start()
            started.append(copy)
        else:

            @pl.when(y == busy)
            def _():
                copy.start()

            last_pull = copy

    for d in range(1, ny):
        s = (y + ny - d) % ny
        peer = {"sp": ((y + d) % ny) * CORES + core}
        remote(lgram_y.at[s], lgram_y.at[s], ly_sems, d, d, peer).wait_recv()

    def factors_to(sems, send, recv, index, peer):
        lanes = pl.ds(pl.multiple_of(index * CHUNK, CHUNK), CHUNK)
        return remote(new_factors.at[:, lanes], new_factors.at[:, lanes], sems, send, recv, peer)

    @pl.when(y < busy)
    def _():
        lgram = lgram_y[0]
        for s in range(1, ny):
            lgram = lgram + lgram_y[s]
        site_factor = cholesky(lgram[:, 0:K], [inverse] * K)
        total = pull_mine[busy - 1] + shift
        for d in range(1, ny):
            s = (y + d) % ny
            remote(pull_y.at[s], pull_y.at[s], py_sems, 0, s, {"sp": s * CORES + core}).wait_recv()
            total = total + pull_y[s]
        result = solve(site_factor, total, factor_noise[...])
        new_factors[:, pl.ds(c0, CHUNK)] = result
        for d in far_first(ny):
            t = (y + d) % ny
            factors_to(fy_sems, d, y, y * CORES + core, {"sp": t * CORES + core}).start()
        factors_to(fp_sems, y, y, y * CORES + core, {"sp": pair}).start()

    for e in order[busy - 2 :: -1] + [busy]:
        s = (y + busy - e) % busy

        def hand_on():
            factors_to(fy_sems, 0, s, s * CORES + core, {"sp": s * CORES + core}).wait_recv()
            factors_to(fp_sems, s, s, s * CORES + core, {"sp": pair}).start()

        if e < busy:
            hand_on()
        else:
            pl.when(y == busy)(hand_on)

    for s in range(busy):
        factors_to(fp_sems, s, s, s * CORES + (1 - core), {"sp": pair}).wait_recv()

    stores.append(pltpu.make_async_copy(new_factors, new_factors_hbm, out_sems.at[2]))
    stores[2].start()

    for copy in started:
        copy.wait_send()
    for s in range(busy):
        factors_to(fp_sems, s, s, s * CORES + core, {"sp": pair}).wait_send()

    @pl.when(y == busy)
    def _():
        last_pull.wait_send()

    @pl.when(y < busy)
    def _():
        for d in range(1, ny):
            t = (y + d) % ny
            factors_to(fy_sems, d, y, y * CORES + core, {"sp": t * CORES + core}).wait_send()

    for store in stores:
        store.wait()


def write_out(a, b, c, a_out, b_out, c_out, sems):
    cut = a.shape[0] // 4
    pairs = [(a.at[i * cut : (i + 1) * cut], a_out.at[i * cut : (i + 1) * cut]) for i in range(4)]
    pairs += [(b, b_out), (c, c_out)]
    copies = [pltpu.make_async_copy(src, dst, sems.at[i]) for i, (src, dst) in enumerate(pairs)]
    for copy in copies:
        copy.start()
    for copy in copies:
        copy.wait()


def solution(mesh):
    n_site, n_sp = mesh.shape["site"], mesh.shape["sp"]
    nx, ny = n_site // Z, n_sp // CORES
    busy = ny - 1

    def shards(presence, noise, factors, loadings, precision, neighbours, weights, variance, factor_noise):
        rows, species = presence.shape
        assert rows == busy * CORES * CHUNK and species == 128
        hbm = pl.BlockSpec(memory_space=pltpu.HBM)
        sems = pltpu.SemaphoreType.DMA
        out_shape = (
            jax.ShapeDtypeStruct((rows, species), BF16),
            jax.ShapeDtypeStruct((K, species), F32),
            jax.ShapeDtypeStruct((K, rows), F32),
        )
        results = pl.pallas_call(
            functools.partial(kernel, n_site, n_sp),
            out_shape=out_shape,
            in_specs=[hbm] * 9,
            out_specs=(hbm,) * 3,
            scratch_shapes=[
                pltpu.VMEM((rows, species), BF16),
                pltpu.VMEM((K, species), F32),
                pltpu.VMEM((K, rows), F32),
                sems((3,)),
                pltpu.VMEM((rows, species), jnp.int32),
                pltpu.VMEM((rows, species), BF16),
                pltpu.VMEM((K, rows), F32),
                pltpu.VMEM((K, species), F32),
                pltpu.VMEM((K, species), F32),
                pltpu.VMEM((NBR, CHUNK), jnp.int32),
                pltpu.VMEM((NBR, CHUNK), F32),
                pltpu.VMEM((1, CHUNK), F32),
                pltpu.VMEM((K, CHUNK), F32),
                sems((13,)),
                pltpu.VMEM((3 * K, rows), BF16),
                pltpu.VMEM((rows, 2 * species), BF16),
                pltpu.VMEM((K, RIM + rows), F32),
                pltpu.VMEM((WINDOW, CHUNK), F32),
                pltpu.VMEM((Z, K, species), F32),
                pltpu.VMEM((nx, K, species), F32),
                pltpu.VMEM((Z, K, species), F32),
                pltpu.VMEM((nx, K, species), F32),
                pltpu.VMEM((K, species), F32),
                pltpu.VMEM((K, species), F32),
                pltpu.VMEM((ny, K, species), F32),
                pltpu.VMEM((busy, K, CHUNK), F32),
                pltpu.VMEM((busy, K, CHUNK), F32),
                pltpu.VMEM((busy, K, CHUNK), F32),
                pltpu.VMEM((ny, K, CHUNK), F32),
                sems((2, 1)),
                sems((2, Z)),
                sems((2, nx)),
                sems((2, Z)),
                sems((2, nx)),
                sems((2, 1)),
                sems((2, ny)),
                sems((2, busy)),
                sems((2, ny)),
                sems((2, ny)),
                sems((2, busy)),
            ],
            compiler_params=pltpu.CompilerParams(
                collective_id=0,
                has_side_effects=True,
                vmem_limit_bytes=60 * 1024 * 1024,
            ),
        )(presence, noise, factors, loadings, precision, neighbours, weights, variance.reshape(1, rows), factor_noise)
        return pl.pallas_call(
            write_out,
            out_shape=out_shape,
            in_specs=[hbm] * 3,
            out_specs=(hbm,) * 3,
            scratch_shapes=[sems((6,))],
        )(*results)

    in_specs = (
        P("site", "sp"),
        P("site", "sp"),
        P(None, "site"),
        P(None, "sp"),
        P(None, "sp"),
        P(None, "site"),
        P(None, "site"),
        P("site"),
        P(None, "site"),
    )
    out_specs = (P("site", "sp"), P(None, "sp"), P(None, "site"))
    return jax.shard_map(shards, mesh=mesh, in_specs=in_specs, out_specs=out_specs, check_vma=False)
```

```python
import functools

import jax
import jax.numpy as jnp
from jax import lax
from jax.experimental import pallas as pl
from jax.experimental.pallas import tpu as pltpu
from jax.sharding import PartitionSpec as P

F32 = jnp.float32
BF16 = jnp.bfloat16
MESH = pl.DeviceIdType.MESH

Z = 8
CORES = 2
K = 16
NBR = 15
CHUNK = 256
RIM = 1536
WINDOW = RIM + CHUNK
HALF = 8
STEP = 96
PIECES = 4

N_COEF = (0.7978845828848753, 0.561783412736638, 0.19921040380039692, 0.039025408597369395, 0.0036777514496204662)
D_COEF = (1.0, 1.1595221251207712, 0.6411219754723788, 0.20649649681102156, 0.03902744122918637, 0.003677727281734947)
inv_root_two_pi = 0.3989422804014327


def poly(coef, u):
    acc = u * coef[-1] + coef[-2]
    for a in coef[-3::-1]:
        acc = acc * u + a
    return acc


def split(x):
    hi = x.astype(BF16)
    return hi, (x - hi.astype(F32)).astype(BF16)


def dot(a, b, dims):
    return lax.dot_general(a, b, (dims, ((), ())), preferred_element_type=F32)


def blocks_sum(p, rows, cols):
    return (p[:rows, :cols] + p[:rows, cols:]) + (p[rows:, :cols] + p[rows:, cols:])


def cholesky(base, extra):
    width = extra[0].shape[1]
    row = lax.broadcasted_iota(jnp.int32, (HALF, width), 0)
    top, bot = [], []
    for k in range(K):
        diag = jnp.where(row == k % HALF, extra[k], 0.0)
        column = base[:, k : k + 1]
        if k < HALF:
            top.append(column[:HALF] + diag)
            bot.append(column[HALF:] + jnp.zeros_like(diag))
        else:
            top.append(None)
            bot.append(column[HALF:] + diag)
    scales = []
    for j in range(K):
        d = top[j][j : j + 1] if j < HALF else bot[j][j - HALF : j - HALF + 1]
        r = lax.rsqrt(d)
        scales.append(r)
        bot[j] = bot[j] * r
        if j < HALF:
            top[j] = top[j] * r
        for k in range(j + 1, K):
            if k < HALF:
                s = top[j][k : k + 1]
                top[k] = top[k] - top[j] * s
                bot[k] = bot[k] - bot[j] * s
            else:
                bot[k] = bot[k] - bot[j] * bot[j][k - HALF : k - HALF + 1]
    return top, bot, scales


def solve(factor, rhs, noise):
    top, bot, scales = factor
    rt, rb = rhs[:HALF], rhs[HALF:]
    middle = []
    for j in range(K):
        y = (rt[j : j + 1] if j < HALF else rb[j - HALF : j - HALF + 1]) * scales[j]
        if noise is not None:
            y = y + noise[j : j + 1]
        middle.append(y)
        if j < HALF:
            rt = rt - top[j] * y
        rb = rb - bot[j] * y
    row = lax.broadcasted_iota(jnp.int32, rt.shape, 0)
    xt, xb = jnp.zeros_like(rt), jnp.zeros_like(rt)
    for j in range(K - 1, -1, -1):
        terms = bot[j] * xb
        if j < HALF:
            terms = terms + top[j] * xt
        x = (middle[j] - jnp.sum(terms, axis=0, keepdims=True)) * scales[j]
        if j < HALF:
            xt = jnp.where(row == j, x, xt)
        else:
            xb = jnp.where(row == j - HALF, x, xb)
    return jnp.concatenate([xt, xb], axis=0)


def far_first(n):
    return sorted(range(1, n), key=lambda d: -min(d, n - d))


def kernel(
    n_site,
    n_sp,
    presence_hbm,
    noise_hbm,
    factors_hbm,
    loadings_hbm,
    precision_hbm,
    neighbours_hbm,
    weights_hbm,
    variance_hbm,
    factor_noise_hbm,
    utilities_hbm,
    new_loadings_hbm,
    new_factors_hbm,
    utilities,
    new_loadings,
    new_factors,
    out_sems,
    presence,
    noise,
    factors,
    loadings,
    precision,
    neighbours,
    weights,
    variance,
    factor_noise,
    in_sems,
    fs,
    draws,
    window,
    onehot,
    gram_z,
    gram_x,
    cross_z,
    cross_x,
    lgram_mine,
    lgram_pair,
    lgram_y,
    pull_out,
    pull_pair,
    pull_mine,
    pull_y,
    rim_sems,
    gz_sems,
    gx_sems,
    cz_sems,
    cx_sems,
    lp_sems,
    ly_sems,
    pp_sems,
    py_sems,
    fy_sems,
    fp_sems,
):
    nx = n_site // Z
    ny = n_sp // CORES
    busy = ny - 1
    rows = factors.shape[1]
    steps = rows // CHUNK
    cuts = (0, min(2, steps // 2) * CHUNK, steps // 2 * CHUNK, rows)
    species = loadings.shape[1]

    site = lax.axis_index("site")
    sp = lax.axis_index("sp")
    x, z = site // Z, site % Z
    y, core = sp // CORES, sp % CORES
    pair = y * CORES + (1 - core)
    ahead = (site + 1) % n_site
    behind = (site + n_site - 1) % n_site

    def z_peer(d):
        return x * Z + (z + d) % Z

    def x_peer(d):
        return ((x + d) % nx) * Z + z

    barrier = pltpu.get_barrier_semaphore()
    greeted = [{"site": z_peer(d)} for d in range(1, Z)]
    greeted += [{"site": x_peer(d)} for d in range(1, nx)]
    greeted += [{"site": ahead}, {"site": behind}]
    greeted += [{"sp": ((y + d) % ny) * CORES + core} for d in range(1, ny)]
    greeted += [{"sp": pair}]
    for peer in greeted:
        pl.semaphore_signal(barrier, inc=1, device_id=peer, device_id_type=MESH)

    def remote(src, dst, sems, send, recv, peer):
        return pltpu.make_async_remote_copy(
            src_ref=src,
            dst_ref=dst,
            send_sem=sems.at[0, send],
            recv_sem=sems.at[1, recv],
            device_id=peer,
            device_id_type=MESH,
        )

    def spread_z(buf, sems):
        copies = []
        for d in far_first(Z):
            copy = remote(buf.at[z], buf.at[z], sems, d, d, {"site": z_peer(d)})
            copy.start()
            copies.append(copy)
        return copies

    def spread_x(buf, sems):
        copies = []
        for d in far_first(nx):
            copy = remote(buf.at[x], buf.at[x], sems, d, d, {"site": x_peer(d)})
            copy.start()
            copies.append(copy)
        return copies

    def gather_z(buf, sems):
        for d in range(1, Z):
            s = (z + Z - d) % Z
            remote(buf.at[s], buf.at[s], sems, d, d, {"site": z_peer(d)}).wait_recv()
        acc = buf[0]
        for s in range(1, Z):
            acc = acc + buf[s]
        return acc

    def gather_x(buf, sems):
        for d in range(1, nx):
            s = (x + nx - d) % nx
            remote(buf.at[s], buf.at[s], sems, d, d, {"site": x_peer(d)}).wait_recv()
        acc = buf[0]
        for s in range(1, nx):
            acc = acc + buf[s]
        return acc

    chunk = jnp.minimum(sp, CORES * busy - 1)
    c0 = pl.multiple_of(chunk * CHUNK, CHUNK)
    mine = pl.ds(c0, CHUNK)
    loads = [(factors_hbm, factors), (loadings_hbm, loadings)]
    for a, b in zip(cuts, cuts[1:]):
        loads.append((presence_hbm.at[a:b], presence.at[a:b]))
        loads.append((noise_hbm.at[a:b], noise.at[a:b]))
    loads += [
        (neighbours_hbm.at[:, mine], neighbours),
        (weights_hbm.at[:, mine], weights),
        (precision_hbm, precision),
        (variance_hbm, variance),
        (factor_noise_hbm.at[:, mine], factor_noise),
    ]
    loads = [pltpu.make_async_copy(a, b, in_sems.at[i]) for i, (a, b) in enumerate(loads)]
    for load in loads:
        load.start()
    started = []

    loads[0].wait()
    loads[1].wait()
    f = factors[...]
    hi, lo = split(f)
    fs[0:16, :] = hi
    fs[16:32, :] = lo
    fs[32:48, :] = hi
    window[:, RIM:] = f
    l_hi, l_lo = split(loadings[...])
    ls = jnp.concatenate([l_hi, l_hi, l_lo], axis=0)

    both = jnp.concatenate([hi, lo], axis=0)
    products = dot(both, both, ((1,), (1,)))
    gram_part = blocks_sum(products, K, K)
    zeros = jnp.zeros((K, species), F32)
    gram_z[z] = zeros
    gram_z[z, :, 0:K] = gram_part

    def draw_step(i, acc):
        r0 = pl.multiple_of(i * CHUNK, CHUNK)
        mean = dot(fs[:, pl.ds(r0, CHUNK)], ls, ((0,), (0,)))
        there = presence[pl.ds(r0, CHUNK), :] > 0
        t = jnp.where(there, mean, -mean)
        u = jnp.abs(t)
        density = jnp.exp(-0.5 * t * t) * inv_root_two_pi
        num = poly(N_COEF, u)
        den = poly(D_COEF, u)
        full = u * den + num
        negative = t < 0.0
        v = jnp.where(negative, num, density * full) / jnp.where(negative, den, full - density * den)
        s = v + jnp.maximum(t, 0.0)
        spread = jnp.maximum(1.0 - v * (v + u), 0.0)
        draw = jnp.where(there, s, -s) + jnp.sqrt(spread) * noise[pl.ds(r0, CHUNK), :].astype(F32)
        d_hi, d_lo = split(draw)
        utilities[pl.ds(r0, CHUNK), :] = d_hi
        pieces = jnp.concatenate([d_hi, d_lo], axis=1)
        draws[pl.ds(r0, CHUNK), :] = pieces
        return acc + dot(fs[0:32, pl.ds(r0, CHUNK)], pieces, ((1,), (0,)))

    acc = jnp.zeros((2 * K, 2 * species), F32)
    for piece in range(2):
        loads[2 + 2 * piece].wait()
        loads[3 + 2 * piece].wait()
        acc = lax.fori_loop(cuts[piece] // CHUNK, cuts[piece + 1] // CHUNK, draw_step, acc)

    pl.semaphore_wait(barrier, len(greeted))

    rim = remote(
        factors.at[:, rows - RIM : rows],
        window.at[:, 0:RIM],
        rim_sems,
        0,
        0,
        {"site": ahead},
    )
    started += spread_z(gram_z, gz_sems)
    rim.start()
    started.append(rim)

    loads[6].wait()
    loads[7].wait()
    acc = lax.fori_loop(cuts[2] // CHUNK, steps, draw_step, acc)
    cross_z[z] = blocks_sum(acc, K, species)
    started += spread_z(cross_z, cz_sems)
    stores = [pltpu.make_async_copy(utilities, utilities_hbm, out_sems.at[0])]
    stores[0].start()
    gram_x[x] = gather_z(gram_z, gz_sems)
    started += spread_x(gram_x, gx_sems)

    for load in loads[8:]:
        load.wait()
    base = site * rows + chunk * CHUNK - RIM
    onehot[...] = jnp.zeros_like(onehot)
    iota = lax.broadcasted_iota(jnp.int32, (224, 128), 0)

    def mark(k, carry):
        ids = neighbours[pl.ds(k, 1), :]
        w = jnp.where(ids >= 0, weights[pl.ds(k, 1), :], 0.0)
        for q in range(CHUNK // 128):
            first = pl.multiple_of(RIM - STEP + 128 * q - STEP * k, 32)
            lanes = slice(128 * q, 128 * (q + 1))
            hit = iota == ids[:, lanes] - (base + first)
            onehot[pl.ds(first, 224), lanes] += jnp.where(hit, w[:, lanes], 0.0)
        return carry

    lax.fori_loop(0, NBR, mark, 0)
    rim.wait_recv()

    def gather_step(b, acc):
        r0 = pl.multiple_of(b * 256, 256)
        m_hi, m_lo = split(onehot[pl.ds(r0, 256), :])
        w_hi, w_lo = split(window[:, pl.ds(pl.multiple_of(c0 + r0, 256), 256)])
        return acc + dot(
            jnp.concatenate([w_hi, w_lo], axis=0),
            jnp.concatenate([m_hi, m_lo], axis=1),
            ((1,), (0,)),
        )

    prior = lax.fori_loop(0, WINDOW // 256, gather_step, jnp.zeros((2 * K, 2 * CHUNK), F32))
    prior = blocks_sum(prior, K, CHUNK)
    inverse = 1.0 / variance[pl.ds(c0, CHUNK)].reshape(1, CHUNK)
    shift = prior * inverse

    cross_x[x] = gather_z(cross_z, cz_sems)
    started += spread_x(cross_x, cx_sems)

    gram = gather_x(gram_x, gx_sems)[:, 0:K]
    factor = cholesky(gram, [precision[k : k + 1, :] for k in range(K)])

    cross = gather_x(cross_x, cx_sems)
    fresh = solve(factor, cross, None)
    new_loadings[...] = fresh
    stores.append(pltpu.make_async_copy(new_loadings, new_loadings_hbm, out_sems.at[1]))
    stores[1].start()

    n_hi, n_lo = split(fresh)
    narrow = jnp.concatenate([n_hi, n_lo], axis=0)
    lgram_part = blocks_sum(dot(narrow, narrow, ((1,), (1,))), K, K)
    lgram_mine[...] = zeros
    lgram_mine[:, 0:K] = lgram_part
    copy = remote(lgram_mine, lgram_pair, lp_sems, 0, 0, {"sp": pair})
    copy.start()
    started.append(copy)

    zero = jnp.zeros_like(n_hi)
    wide = jnp.concatenate(
        [jnp.concatenate([n_hi, n_hi], axis=1), jnp.concatenate([n_lo, zero], axis=1)],
        axis=0,
    )

    def pull_of(t, c):
        r0 = pl.multiple_of((t * CORES + c) * CHUNK, CHUNK)
        p = dot(wide, draws[pl.ds(r0, CHUNK), :], ((1,), (1,)))
        return p[:K] + p[K:]

    order = far_first(ny)
    order.remove(busy)
    order.append(busy)
    for e in order:
        t = (y + e) % busy
        pull_out[e - 1] = pull_of(t, 1 - core)
        copy = remote(pull_out.at[e - 1], pull_pair.at[e - 1], pp_sems, e - 1, e - 1, {"sp": pair})
        copy.start()
        started.append(copy)

    remote(lgram_mine, lgram_pair, lp_sems, 0, 0, {"sp": pair}).wait_recv()
    lgram_y[y] = lgram_mine[...] + lgram_pair[...]
    for d in far_first(ny):
        peer = {"sp": ((y + d) % ny) * CORES + core}
        copy = remote(lgram_y.at[y], lgram_y.at[y], ly_sems, d, d, peer)
        copy.start()
        started.append(copy)

    for e in order:
        t = (y + e) % busy
        part = pull_of(t, core)
        remote(pull_out.at[e - 1], pull_pair.at[e - 1], pp_sems, e - 1, e - 1, {"sp": pair}).wait_recv()
        pull_mine[e - 1] = part + pull_pair[e - 1]
        copy = remote(pull_mine.at[e - 1], pull_y.at[y], py_sems, e, y, {"sp": t * CORES + core})
        if e < busy:
            copy.start()
            started.append(copy)
        else:

            @pl.when(y == busy)
            def _():
                copy.start()

            last_pull = copy

    for d in range(1, ny):
        s = (y + ny - d) % ny
        peer = {"sp": ((y + d) % ny) * CORES + core}
        remote(lgram_y.at[s], lgram_y.at[s], ly_sems, d, d, peer).wait_recv()

    def factors_to(sems, send, recv, index, peer):
        lanes = pl.ds(pl.multiple_of(index * CHUNK, CHUNK), CHUNK)
        return remote(new_factors.at[:, lanes], new_factors.at[:, lanes], sems, send, recv, peer)

    @pl.when(y < busy)
    def _():
        lgram = lgram_y[0]
        for s in range(1, ny):
            lgram = lgram + lgram_y[s]
        site_factor = cholesky(lgram[:, 0:K], [inverse] * K)
        total = pull_mine[busy - 1] + shift
        for d in range(1, ny):
            s = (y + d) % ny
            remote(pull_y.at[s], pull_y.at[s], py_sems, 0, s, {"sp": s * CORES + core}).wait_recv()
            total = total + pull_y[s]
        result = solve(site_factor, total, factor_noise[...])
        new_factors[:, pl.ds(c0, CHUNK)] = result
        for d in far_first(ny):
            t = (y + d) % ny
            factors_to(fy_sems, d, y, y * CORES + core, {"sp": t * CORES + core}).start()
        factors_to(fp_sems, y, y, y * CORES + core, {"sp": pair}).start()

    for e in order[busy - 2 :: -1] + [busy]:
        s = (y + busy - e) % busy

        def hand_on():
            factors_to(fy_sems, 0, s, s * CORES + core, {"sp": s * CORES + core}).wait_recv()
            factors_to(fp_sems, s, s, s * CORES + core, {"sp": pair}).start()

        if e < busy:
            hand_on()
        else:
            pl.when(y == busy)(hand_on)

    for s in range(busy):
        factors_to(fp_sems, s, s, s * CORES + (1 - core), {"sp": pair}).wait_recv()

    stores.append(pltpu.make_async_copy(new_factors, new_factors_hbm, out_sems.at[2]))
    stores[2].start()

    for copy in started:
        copy.wait_send()
    for s in range(busy):
        factors_to(fp_sems, s, s, s * CORES + core, {"sp": pair}).wait_send()

    @pl.when(y == busy)
    def _():
        last_pull.wait_send()

    @pl.when(y < busy)
    def _():
        for d in range(1, ny):
            t = (y + d) % ny
            factors_to(fy_sems, d, y, y * CORES + core, {"sp": t * CORES + core}).wait_send()

    for store in stores:
        store.wait()


def write_out(a, b, c, a_out, b_out, c_out, a_mid, b_mid, c_mid, sems):
    cut = a.shape[0] // PIECES
    rows = [slice(i * cut, (i + 1) * cut) for i in range(PIECES)]
    hops = [(c, c_mid, c_out), (b, b_mid, b_out)]
    hops += [(a.at[r], a_mid.at[r], a_out.at[r]) for r in rows]
    reads = [pltpu.make_async_copy(src, mid, sems.at[0, i]) for i, (src, mid, dst) in enumerate(hops)]
    writes = [pltpu.make_async_copy(mid, dst, sems.at[1, i]) for i, (src, mid, dst) in enumerate(hops)]
    for read in reads:
        read.start()
    for read, write in zip(reads, writes):
        read.wait()
        write.start()
    for write in writes:
        write.wait()


def solution(mesh):
    n_site, n_sp = mesh.shape["site"], mesh.shape["sp"]
    nx, ny = n_site // Z, n_sp // CORES
    busy = ny - 1

    def shards(presence, noise, factors, loadings, precision, neighbours, weights, variance, factor_noise):
        rows, species = presence.shape
        assert rows == busy * CORES * CHUNK and species == 128
        hbm = pl.BlockSpec(memory_space=pltpu.HBM)
        sems = pltpu.SemaphoreType.DMA
        out_shape = (
            jax.ShapeDtypeStruct((rows, species), BF16),
            jax.ShapeDtypeStruct((K, species), F32),
            jax.ShapeDtypeStruct((K, rows), F32),
        )
        results = pl.pallas_call(
            functools.partial(kernel, n_site, n_sp),
            out_shape=out_shape,
            in_specs=[hbm] * 9,
            out_specs=(hbm,) * 3,
            scratch_shapes=[
                pltpu.VMEM((rows, species), BF16),
                pltpu.VMEM((K, species), F32),
                pltpu.VMEM((K, rows), F32),
                sems((3,)),
                pltpu.VMEM((rows, species), jnp.int32),
                pltpu.VMEM((rows, species), BF16),
                pltpu.VMEM((K, rows), F32),
                pltpu.VMEM((K, species), F32),
                pltpu.VMEM((K, species), F32),
                pltpu.VMEM((NBR, CHUNK), jnp.int32),
                pltpu.VMEM((NBR, CHUNK), F32),
                pltpu.VMEM((rows,), F32),
                pltpu.VMEM((K, CHUNK), F32),
                sems((13,)),
                pltpu.VMEM((3 * K, rows), BF16),
                pltpu.VMEM((rows, 2 * species), BF16),
                pltpu.VMEM((K, RIM + rows), F32),
                pltpu.VMEM((WINDOW, CHUNK), F32),
                pltpu.VMEM((Z, K, species), F32),
                pltpu.VMEM((nx, K, species), F32),
                pltpu.VMEM((Z, K, species), F32),
                pltpu.VMEM((nx, K, species), F32),
                pltpu.VMEM((K, species), F32),
                pltpu.VMEM((K, species), F32),
                pltpu.VMEM((ny, K, species), F32),
                pltpu.VMEM((busy, K, CHUNK), F32),
                pltpu.VMEM((busy, K, CHUNK), F32),
                pltpu.VMEM((busy, K, CHUNK), F32),
                pltpu.VMEM((ny, K, CHUNK), F32),
                sems((2, 1)),
                sems((2, Z)),
                sems((2, nx)),
                sems((2, Z)),
                sems((2, nx)),
                sems((2, 1)),
                sems((2, ny)),
                sems((2, busy)),
                sems((2, ny)),
                sems((2, ny)),
                sems((2, busy)),
            ],
            compiler_params=pltpu.CompilerParams(
                collective_id=0,
                has_side_effects=True,
                vmem_limit_bytes=60 * 1024 * 1024,
            ),
        )(presence, noise, factors, loadings, precision, neighbours, weights, variance, factor_noise)
        return pl.pallas_call(
            write_out,
            out_shape=out_shape,
            in_specs=[hbm] * 3,
            out_specs=(hbm,) * 3,
            scratch_shapes=[pltpu.VMEM((rows, species), BF16), pltpu.VMEM((K, species), F32), pltpu.VMEM((K, rows), F32), sems((2, PIECES + 2))],
        )(*results)

    in_specs = (
        P("site", "sp"),
        P("site", "sp"),
        P(None, "site"),
        P(None, "sp"),
        P(None, "sp"),
        P(None, "site"),
        P(None, "site"),
        P("site"),
        P(None, "site"),
    )
    out_specs = (P("site", "sp"), P(None, "sp"), P(None, "site"))
    return jax.shard_map(shards, mesh=mesh, in_specs=in_specs, out_specs=out_specs, check_vma=False)
```

```python
import functools

import jax
import jax.numpy as jnp
from jax import lax
from jax.experimental import pallas as pl
from jax.experimental.pallas import tpu as pltpu
from jax.sharding import PartitionSpec as P

F32 = jnp.float32
BF16 = jnp.bfloat16
MESH = pl.DeviceIdType.MESH

Z = 8
CORES = 2
K = 16
NBR = 15
CHUNK = 256
RIM = 1536
WINDOW = RIM + CHUNK
HALF = 8
STEP = 96
PIECES = 4

N_COEF = (0.7978845828848753, 0.561783412736638, 0.19921040380039692, 0.039025408597369395, 0.0036777514496204662)
D_COEF = (1.0, 1.1595221251207712, 0.6411219754723788, 0.20649649681102156, 0.03902744122918637, 0.003677727281734947)
inv_root_two_pi = 0.3989422804014327


def poly(coef, u):
    acc = u * coef[-1] + coef[-2]
    for a in coef[-3::-1]:
        acc = acc * u + a
    return acc


def split(x):
    hi = x.astype(BF16)
    return hi, (x - hi.astype(F32)).astype(BF16)


def dot(a, b, dims):
    return lax.dot_general(a, b, (dims, ((), ())), preferred_element_type=F32)


def blocks_sum(p, rows, cols):
    return (p[:rows, :cols] + p[:rows, cols:]) + (p[rows:, :cols] + p[rows:, cols:])


def cholesky(base, extra):
    width = extra[0].shape[1]
    row = lax.broadcasted_iota(jnp.int32, (HALF, width), 0)
    top, bot = [], []
    for k in range(K):
        diag = jnp.where(row == k % HALF, extra[k], 0.0)
        column = base[:, k : k + 1]
        if k < HALF:
            top.append(column[:HALF] + diag)
            bot.append(column[HALF:] + jnp.zeros_like(diag))
        else:
            top.append(None)
            bot.append(column[HALF:] + diag)
    scales = []
    for j in range(K):
        d = top[j][j : j + 1] if j < HALF else bot[j][j - HALF : j - HALF + 1]
        r = lax.rsqrt(d)
        scales.append(r)
        bot[j] = bot[j] * r
        if j < HALF:
            top[j] = top[j] * r
        for k in range(j + 1, K):
            if k < HALF:
                s = top[j][k : k + 1]
                top[k] = top[k] - top[j] * s
                bot[k] = bot[k] - bot[j] * s
            else:
                bot[k] = bot[k] - bot[j] * bot[j][k - HALF : k - HALF + 1]
    return top, bot, scales


def solve(factor, rhs, noise):
    top, bot, scales = factor
    rt, rb = rhs[:HALF], rhs[HALF:]
    middle = []
    for j in range(K):
        y = (rt[j : j + 1] if j < HALF else rb[j - HALF : j - HALF + 1]) * scales[j]
        if noise is not None:
            y = y + noise[j : j + 1]
        middle.append(y)
        if j < HALF:
            rt = rt - top[j] * y
        rb = rb - bot[j] * y
    row = lax.broadcasted_iota(jnp.int32, rt.shape, 0)
    xt, xb = jnp.zeros_like(rt), jnp.zeros_like(rt)
    for j in range(K - 1, -1, -1):
        terms = bot[j] * xb
        if j < HALF:
            terms = terms + top[j] * xt
        x = (middle[j] - jnp.sum(terms, axis=0, keepdims=True)) * scales[j]
        if j < HALF:
            xt = jnp.where(row == j, x, xt)
        else:
            xb = jnp.where(row == j - HALF, x, xb)
    return jnp.concatenate([xt, xb], axis=0)


def far_first(n):
    return sorted(range(1, n), key=lambda d: -min(d, n - d))


def kernel(
    n_site,
    n_sp,
    presence_hbm,
    noise_hbm,
    factors_hbm,
    loadings_hbm,
    precision_hbm,
    neighbours_hbm,
    weights_hbm,
    variance_hbm,
    factor_noise_hbm,
    utilities,
    new_loadings,
    new_factors,
    presence,
    noise,
    factors,
    loadings,
    precision,
    neighbours,
    weights,
    variance,
    factor_noise,
    in_sems,
    fs,
    draws,
    window,
    onehot,
    gram_z,
    gram_x,
    cross_z,
    cross_x,
    lgram_mine,
    lgram_pair,
    lgram_y,
    pull_out,
    pull_pair,
    pull_mine,
    pull_y,
    rim_sems,
    gz_sems,
    gx_sems,
    cz_sems,
    cx_sems,
    lp_sems,
    ly_sems,
    pp_sems,
    py_sems,
    fy_sems,
    fp_sems,
):
    nx = n_site // Z
    ny = n_sp // CORES
    busy = ny - 1
    rows = factors.shape[1]
    steps = rows // CHUNK
    cuts = (0, min(2, steps // 2) * CHUNK, steps // 2 * CHUNK, rows)
    species = loadings.shape[1]

    site = lax.axis_index("site")
    sp = lax.axis_index("sp")
    x, z = site // Z, site % Z
    y, core = sp // CORES, sp % CORES
    pair = y * CORES + (1 - core)
    ahead = (site + 1) % n_site
    behind = (site + n_site - 1) % n_site

    def z_peer(d):
        return x * Z + (z + d) % Z

    def x_peer(d):
        return ((x + d) % nx) * Z + z

    barrier = pltpu.get_barrier_semaphore()
    greeted = [{"site": z_peer(d)} for d in range(1, Z)]
    greeted += [{"site": x_peer(d)} for d in range(1, nx)]
    greeted += [{"site": ahead}, {"site": behind}]
    greeted += [{"sp": ((y + d) % ny) * CORES + core} for d in range(1, ny)]
    greeted += [{"sp": pair}]
    for peer in greeted:
        pl.semaphore_signal(barrier, inc=1, device_id=peer, device_id_type=MESH)

    def remote(src, dst, sems, send, recv, peer):
        return pltpu.make_async_remote_copy(
            src_ref=src,
            dst_ref=dst,
            send_sem=sems.at[0, send],
            recv_sem=sems.at[1, recv],
            device_id=peer,
            device_id_type=MESH,
        )

    def spread_z(buf, sems):
        copies = []
        for d in far_first(Z):
            copy = remote(buf.at[z], buf.at[z], sems, d, d, {"site": z_peer(d)})
            copy.start()
            copies.append(copy)
        return copies

    def spread_x(buf, sems):
        copies = []
        for d in far_first(nx):
            copy = remote(buf.at[x], buf.at[x], sems, d, d, {"site": x_peer(d)})
            copy.start()
            copies.append(copy)
        return copies

    def gather_z(buf, sems):
        for d in range(1, Z):
            s = (z + Z - d) % Z
            remote(buf.at[s], buf.at[s], sems, d, d, {"site": z_peer(d)}).wait_recv()
        acc = buf[0]
        for s in range(1, Z):
            acc = acc + buf[s]
        return acc

    def gather_x(buf, sems):
        for d in range(1, nx):
            s = (x + nx - d) % nx
            remote(buf.at[s], buf.at[s], sems, d, d, {"site": x_peer(d)}).wait_recv()
        acc = buf[0]
        for s in range(1, nx):
            acc = acc + buf[s]
        return acc

    chunk = jnp.minimum(sp, CORES * busy - 1)
    c0 = pl.multiple_of(chunk * CHUNK, CHUNK)
    mine = pl.ds(c0, CHUNK)
    loads = [(factors_hbm, factors), (loadings_hbm, loadings)]
    for a, b in zip(cuts, cuts[1:]):
        loads.append((presence_hbm.at[a:b], presence.at[a:b]))
        loads.append((noise_hbm.at[a:b], noise.at[a:b]))
    loads += [
        (neighbours_hbm.at[:, mine], neighbours),
        (weights_hbm.at[:, mine], weights),
        (precision_hbm, precision),
        (variance_hbm, variance),
        (factor_noise_hbm.at[:, mine], factor_noise),
    ]
    loads = [pltpu.make_async_copy(a, b, in_sems.at[i]) for i, (a, b) in enumerate(loads)]
    for load in loads:
        load.start()
    started = []

    loads[0].wait()
    loads[1].wait()
    f = factors[...]
    hi, lo = split(f)
    fs[0:16, :] = hi
    fs[16:32, :] = lo
    fs[32:48, :] = hi
    window[:, RIM:] = f
    l_hi, l_lo = split(loadings[...])
    ls = jnp.concatenate([l_hi, l_hi, l_lo], axis=0)

    both = jnp.concatenate([hi, lo], axis=0)
    products = dot(both, both, ((1,), (1,)))
    gram_part = blocks_sum(products, K, K)
    zeros = jnp.zeros((K, species), F32)
    gram_z[z] = zeros
    gram_z[z, :, 0:K] = gram_part

    def draw_step(i, acc):
        r0 = pl.multiple_of(i * CHUNK, CHUNK)
        mean = dot(fs[:, pl.ds(r0, CHUNK)], ls, ((0,), (0,)))
        there = presence[pl.ds(r0, CHUNK), :] > 0
        t = jnp.where(there, mean, -mean)
        u = jnp.abs(t)
        density = jnp.exp(-0.5 * t * t) * inv_root_two_pi
        num = poly(N_COEF, u)
        den = poly(D_COEF, u)
        full = u * den + num
        negative = t < 0.0
        v = jnp.where(negative, num, density * full) / jnp.where(negative, den, full - density * den)
        s = v + jnp.maximum(t, 0.0)
        spread = jnp.maximum(1.0 - v * (v + u), 1e-30)
        draw = jnp.where(there, s, -s) + spread * lax.rsqrt(spread) * noise[pl.ds(r0, CHUNK), :].astype(F32)
        d_hi, d_lo = split(draw)
        utilities[pl.ds(r0, CHUNK), :] = d_hi
        pieces = jnp.concatenate([d_hi, d_lo], axis=1)
        draws[pl.ds(r0, CHUNK), :] = pieces
        return acc + dot(fs[0:32, pl.ds(r0, CHUNK)], pieces, ((1,), (0,)))

    acc = jnp.zeros((2 * K, 2 * species), F32)
    for piece in range(2):
        loads[2 + 2 * piece].wait()
        loads[3 + 2 * piece].wait()
        acc = lax.fori_loop(cuts[piece] // CHUNK, cuts[piece + 1] // CHUNK, draw_step, acc, unroll=True)

    pl.semaphore_wait(barrier, len(greeted))

    rim = remote(
        factors.at[:, rows - RIM : rows],
        window.at[:, 0:RIM],
        rim_sems,
        0,
        0,
        {"site": ahead},
    )
    started += spread_z(gram_z, gz_sems)
    rim.start()
    started.append(rim)

    loads[6].wait()
    loads[7].wait()
    acc = lax.fori_loop(cuts[2] // CHUNK, steps, draw_step, acc, unroll=True)
    cross_z[z] = blocks_sum(acc, K, species)
    started += spread_z(cross_z, cz_sems)
    gram_x[x] = gather_z(gram_z, gz_sems)
    started += spread_x(gram_x, gx_sems)

    for load in loads[8:]:
        load.wait()
    base = site * rows + chunk * CHUNK - RIM
    onehot[...] = jnp.zeros_like(onehot)
    iota = lax.broadcasted_iota(jnp.int32, (224, 128), 0)

    def mark(k, carry):
        ids = neighbours[pl.ds(k, 1), :]
        w = jnp.where(ids >= 0, weights[pl.ds(k, 1), :], 0.0)
        for q in range(CHUNK // 128):
            first = pl.multiple_of(RIM - STEP + 128 * q - STEP * k, 32)
            lanes = slice(128 * q, 128 * (q + 1))
            hit = iota == ids[:, lanes] - (base + first)
            onehot[pl.ds(first, 224), lanes] += jnp.where(hit, w[:, lanes], 0.0)
        return carry

    lax.fori_loop(0, NBR, mark, 0)
    rim.wait_recv()

    def gather_step(b, acc):
        r0 = pl.multiple_of(b * 256, 256)
        m_hi, m_lo = split(onehot[pl.ds(r0, 256), :])
        w_hi, w_lo = split(window[:, pl.ds(pl.multiple_of(c0 + r0, 256), 256)])
        return acc + dot(
            jnp.concatenate([w_hi, w_lo], axis=0),
            jnp.concatenate([m_hi, m_lo], axis=1),
            ((1,), (0,)),
        )

    prior = lax.fori_loop(0, WINDOW // 256, gather_step, jnp.zeros((2 * K, 2 * CHUNK), F32))
    prior = blocks_sum(prior, K, CHUNK)
    inverse = 1.0 / variance[pl.ds(c0, CHUNK)].reshape(1, CHUNK)
    shift = prior * inverse

    cross_x[x] = gather_z(cross_z, cz_sems)
    started += spread_x(cross_x, cx_sems)

    gram = gather_x(gram_x, gx_sems)[:, 0:K]
    factor = cholesky(gram, [precision[k : k + 1, :] for k in range(K)])

    cross = gather_x(cross_x, cx_sems)
    fresh = solve(factor, cross, None)
    new_loadings[...] = fresh

    n_hi, n_lo = split(fresh)
    narrow = jnp.concatenate([n_hi, n_lo], axis=0)
    lgram_part = blocks_sum(dot(narrow, narrow, ((1,), (1,))), K, K)
    lgram_mine[...] = zeros
    lgram_mine[:, 0:K] = lgram_part
    copy = remote(lgram_mine, lgram_pair, lp_sems, 0, 0, {"sp": pair})
    copy.start()
    started.append(copy)

    zero = jnp.zeros_like(n_hi)
    wide = jnp.concatenate(
        [jnp.concatenate([n_hi, n_hi], axis=1), jnp.concatenate([n_lo, zero], axis=1)],
        axis=0,
    )

    def pull_of(t, c):
        r0 = pl.multiple_of((t * CORES + c) * CHUNK, CHUNK)
        p = dot(wide, draws[pl.ds(r0, CHUNK), :], ((1,), (1,)))
        return p[:K] + p[K:]

    order = far_first(ny)
    order.remove(busy)
    order.append(busy)
    for e in order:
        t = (y + e) % busy
        pull_out[e - 1] = pull_of(t, 1 - core)
        copy = remote(pull_out.at[e - 1], pull_pair.at[e - 1], pp_sems, e - 1, e - 1, {"sp": pair})
        copy.start()
        started.append(copy)

    remote(lgram_mine, lgram_pair, lp_sems, 0, 0, {"sp": pair}).wait_recv()
    lgram_y[y] = lgram_mine[...] + lgram_pair[...]
    for d in far_first(ny):
        peer = {"sp": ((y + d) % ny) * CORES + core}
        copy = remote(lgram_y.at[y], lgram_y.at[y], ly_sems, d, d, peer)
        copy.start()
        started.append(copy)

    for e in order:
        t = (y + e) % busy
        part = pull_of(t, core)
        remote(pull_out.at[e - 1], pull_pair.at[e - 1], pp_sems, e - 1, e - 1, {"sp": pair}).wait_recv()
        pull_mine[e - 1] = part + pull_pair[e - 1]
        copy = remote(pull_mine.at[e - 1], pull_y.at[y], py_sems, e, y, {"sp": t * CORES + core})
        if e < busy:
            copy.start()
            started.append(copy)
        else:

            @pl.when(y == busy)
            def _():
                copy.start()

            last_pull = copy

    for d in range(1, ny):
        s = (y + ny - d) % ny
        peer = {"sp": ((y + d) % ny) * CORES + core}
        remote(lgram_y.at[s], lgram_y.at[s], ly_sems, d, d, peer).wait_recv()

    def factors_to(sems, send, recv, index, peer):
        lanes = pl.ds(pl.multiple_of(index * CHUNK, CHUNK), CHUNK)
        return remote(new_factors.at[:, lanes], new_factors.at[:, lanes], sems, send, recv, peer)

    @pl.when(y < busy)
    def _():
        lgram = lgram_y[0]
        for s in range(1, ny):
            lgram = lgram + lgram_y[s]
        site_factor = cholesky(lgram[:, 0:K], [inverse] * K)
        total = pull_mine[busy - 1] + shift
        for d in range(1, ny):
            s = (y + d) % ny
            remote(pull_y.at[s], pull_y.at[s], py_sems, 0, s, {"sp": s * CORES + core}).wait_recv()
            total = total + pull_y[s]
        result = solve(site_factor, total, factor_noise[...])
        new_factors[:, pl.ds(c0, CHUNK)] = result
        for d in far_first(ny):
            t = (y + d) % ny
            factors_to(fy_sems, d, y, y * CORES + core, {"sp": t * CORES + core}).start()
        factors_to(fp_sems, y, y, y * CORES + core, {"sp": pair}).start()

    for e in order[busy - 2 :: -1] + [busy]:
        s = (y + busy - e) % busy

        def hand_on():
            factors_to(fy_sems, 0, s, s * CORES + core, {"sp": s * CORES + core}).wait_recv()
            factors_to(fp_sems, s, s, s * CORES + core, {"sp": pair}).start()

        if e < busy:
            hand_on()
        else:
            pl.when(y == busy)(hand_on)

    for s in range(busy):
        factors_to(fp_sems, s, s, s * CORES + (1 - core), {"sp": pair}).wait_recv()

    for copy in started:
        copy.wait_send()
    for s in range(busy):
        factors_to(fp_sems, s, s, s * CORES + core, {"sp": pair}).wait_send()

    @pl.when(y == busy)
    def _():
        last_pull.wait_send()

    @pl.when(y < busy)
    def _():
        for d in range(1, ny):
            t = (y + d) % ny
            factors_to(fy_sems, d, y, y * CORES + core, {"sp": t * CORES + core}).wait_send()


def write_out(a, b, c, a_out, b_out, c_out, sems):
    cut = a.shape[0] // PIECES
    rows = [slice(i * cut, (i + 1) * cut) for i in range(PIECES)]
    pairs = [(c, c_out), (b, b_out)] + [(a.at[r], a_out.at[r]) for r in rows]
    writes = [pltpu.make_async_copy(src, dst, sems.at[i]) for i, (src, dst) in enumerate(pairs)]
    for write in writes:
        write.start()
    for write in writes:
        write.wait()


def solution(mesh):
    n_site, n_sp = mesh.shape["site"], mesh.shape["sp"]
    nx, ny = n_site // Z, n_sp // CORES
    busy = ny - 1

    def shards(presence, noise, factors, loadings, precision, neighbours, weights, variance, factor_noise):
        rows, species = presence.shape
        assert rows == busy * CORES * CHUNK and species == 128
        vmem = pl.BlockSpec(memory_space=pltpu.VMEM)
        hbm = pl.BlockSpec(memory_space=pltpu.HBM)
        sems = pltpu.SemaphoreType.DMA
        out_shape = (
            jax.ShapeDtypeStruct((rows, species), BF16),
            jax.ShapeDtypeStruct((K, species), F32),
            jax.ShapeDtypeStruct((K, rows), F32),
        )
        results = pl.pallas_call(
            functools.partial(kernel, n_site, n_sp),
            out_shape=tuple(pltpu.VMEM(v.shape, v.dtype) for v in out_shape),
            in_specs=[hbm] * 9,
            out_specs=(vmem,) * 3,
            scratch_shapes=[
                pltpu.VMEM((rows, species), jnp.int32),
                pltpu.VMEM((rows, species), BF16),
                pltpu.VMEM((K, rows), F32),
                pltpu.VMEM((K, species), F32),
                pltpu.VMEM((K, species), F32),
                pltpu.VMEM((NBR, CHUNK), jnp.int32),
                pltpu.VMEM((NBR, CHUNK), F32),
                pltpu.VMEM((rows,), F32),
                pltpu.VMEM((K, CHUNK), F32),
                sems((13,)),
                pltpu.VMEM((3 * K, rows), BF16),
                pltpu.VMEM((rows, 2 * species), BF16),
                pltpu.VMEM((K, RIM + rows), F32),
                pltpu.VMEM((WINDOW, CHUNK), F32),
                pltpu.VMEM((Z, K, species), F32),
                pltpu.VMEM((nx, K, species), F32),
                pltpu.VMEM((Z, K, species), F32),
                pltpu.VMEM((nx, K, species), F32),
                pltpu.VMEM((K, species), F32),
                pltpu.VMEM((K, species), F32),
                pltpu.VMEM((ny, K, species), F32),
                pltpu.VMEM((busy, K, CHUNK), F32),
                pltpu.VMEM((busy, K, CHUNK), F32),
                pltpu.VMEM((busy, K, CHUNK), F32),
                pltpu.VMEM((ny, K, CHUNK), F32),
                sems((2, 1)),
                sems((2, Z)),
                sems((2, nx)),
                sems((2, Z)),
                sems((2, nx)),
                sems((2, 1)),
                sems((2, ny)),
                sems((2, busy)),
                sems((2, ny)),
                sems((2, ny)),
                sems((2, busy)),
            ],
            compiler_params=pltpu.CompilerParams(
                collective_id=0,
                has_side_effects=True,
                vmem_limit_bytes=60 * 1024 * 1024,
            ),
        )(presence, noise, factors, loadings, precision, neighbours, weights, variance, factor_noise)
        return pl.pallas_call(
            write_out,
            out_shape=out_shape,
            in_specs=[vmem] * 3,
            out_specs=(hbm,) * 3,
            scratch_shapes=[sems((PIECES + 2,))],
        )(*[pltpu.with_memory_space_constraint(v, pltpu.VMEM) for v in results])

    in_specs = (
        P("site", "sp"),
        P("site", "sp"),
        P(None, "site"),
        P(None, "sp"),
        P(None, "sp"),
        P(None, "site"),
        P(None, "site"),
        P("site"),
        P(None, "site"),
    )
    out_specs = (P("site", "sp"), P(None, "sp"), P(None, "site"))
    return jax.shard_map(shards, mesh=mesh, in_specs=in_specs, out_specs=out_specs, check_vma=False)
```

```python
import functools

import jax
import jax.numpy as jnp
from jax import lax
from jax.experimental import pallas as pl
from jax.experimental.pallas import tpu as pltpu
from jax.sharding import PartitionSpec as P

F32 = jnp.float32
BF16 = jnp.bfloat16
MESH = pl.DeviceIdType.MESH

Z = 8
CORES = 2
K = 16
NBR = 15
CHUNK = 256
RIM = 1536
WINDOW = RIM + CHUNK
HALF = 8
STEP = 96
PIECES = 4

N_COEF = (0.7978845828848753, 0.561783412736638, 0.19921040380039692, 0.039025408597369395, 0.0036777514496204662)
D_COEF = (1.0, 1.1595221251207712, 0.6411219754723788, 0.20649649681102156, 0.03902744122918637, 0.003677727281734947)
inv_root_two_pi = 0.3989422804014327


def poly(coef, u):
    acc = u * coef[-1] + coef[-2]
    for a in coef[-3::-1]:
        acc = acc * u + a
    return acc


def split(x):
    hi = x.astype(BF16)
    return hi, (x - hi.astype(F32)).astype(BF16)


def dot(a, b, dims):
    return lax.dot_general(a, b, (dims, ((), ())), preferred_element_type=F32)


def blocks_sum(p, rows, cols):
    return (p[:rows, :cols] + p[:rows, cols:]) + (p[rows:, :cols] + p[rows:, cols:])


def cholesky(base, extra):
    width = extra[0].shape[1]
    row = lax.broadcasted_iota(jnp.int32, (HALF, width), 0)
    top, bot = [], []
    for k in range(K):
        diag = jnp.where(row == k % HALF, extra[k], 0.0)
        column = base[:, k : k + 1]
        if k < HALF:
            top.append(column[:HALF] + diag)
            bot.append(column[HALF:] + jnp.zeros_like(diag))
        else:
            top.append(None)
            bot.append(column[HALF:] + diag)
    inv_top = [jnp.where(row == k, 1.0, 0.0) if k < HALF else jnp.zeros((HALF, width), F32) for k in range(K)]
    inv_bot = [None if k < HALF else jnp.where(row == k - HALF, 1.0, 0.0) for k in range(K)]
    pivots = []
    for j in range(K):
        d = top[j][j : j + 1] if j < HALF else bot[j][j - HALF : j - HALF + 1]
        r = lax.rsqrt(d)
        pivots.append(d * r)
        bot[j] = bot[j] * r
        inv_top[j] = inv_top[j] * r
        if j < HALF:
            top[j] = top[j] * r
        else:
            inv_bot[j] = inv_bot[j] * r
        for k in range(j + 1, K):
            if k < HALF:
                s = top[j][k : k + 1]
                top[k] = top[k] - top[j] * s
                bot[k] = bot[k] - bot[j] * s
            else:
                s = bot[j][k - HALF : k - HALF + 1]
                bot[k] = bot[k] - bot[j] * s
            inv_top[k] = inv_top[k] - inv_top[j] * s
            if j >= HALF:
                inv_bot[k] = inv_bot[k] - inv_bot[j] * s
    return inv_top, inv_bot, pivots


def apply_pivots(pivots, noise):
    row = lax.broadcasted_iota(jnp.int32, noise.shape, 0)
    acc = jnp.zeros_like(noise)
    for j in range(K):
        acc = jnp.where(row == j, pivots[j], acc)
    return acc * noise


def solve(inv_top, inv_bot, rhs):
    top, bot = rhs[:HALF], rhs[HALF:]
    x_top = x_bot = None
    for j in range(K):
        terms = inv_top[j] * top
        if j >= HALF:
            terms = terms + inv_bot[j] * bot
        y = jnp.sum(terms, axis=0, keepdims=True)
        x_top = inv_top[j] * y if x_top is None else x_top + inv_top[j] * y
        if j >= HALF:
            x_bot = inv_bot[j] * y if x_bot is None else x_bot + inv_bot[j] * y
    return jnp.concatenate([x_top, x_bot], axis=0)


def far_first(n):
    return sorted(range(1, n), key=lambda d: -min(d, n - d))


def kernel(
    n_site,
    n_sp,
    presence_hbm,
    noise_hbm,
    factors_hbm,
    loadings_hbm,
    precision_hbm,
    neighbours_hbm,
    weights_hbm,
    variance_hbm,
    factor_noise_hbm,
    utilities,
    new_loadings,
    new_factors,
    presence,
    noise,
    factors,
    loadings,
    precision,
    neighbours,
    weights,
    variance,
    factor_noise,
    in_sems,
    fs,
    draws,
    window,
    onehot,
    gram_z,
    gram_x,
    cross_z,
    cross_x,
    lgram_all,
    pull_out,
    pull_pair,
    pull_mine,
    pull_y,
    rim_sems,
    gz_sems,
    gx_sems,
    cz_sems,
    cx_sems,
    ly_sems,
    pp_sems,
    py_sems,
    fy_sems,
    fp_sems,
):
    nx = n_site // Z
    ny = n_sp // CORES
    busy = ny - 1
    rows = factors.shape[1]
    steps = rows // CHUNK
    cuts = (0, min(2, steps // 2) * CHUNK, steps // 2 * CHUNK, rows)
    species = loadings.shape[1]

    site = lax.axis_index("site")
    sp = lax.axis_index("sp")
    x, z = site // Z, site % Z
    y, core = sp // CORES, sp % CORES
    pair = y * CORES + (1 - core)
    ahead = (site + 1) % n_site
    behind = (site + n_site - 1) % n_site

    def z_peer(d):
        return x * Z + (z + d) % Z

    def sp_peer(o):
        return ((y + o // CORES) % ny) * CORES + (core + o) % CORES

    def x_peer(d):
        return ((x + d) % nx) * Z + z

    chunk = jnp.minimum(sp, CORES * busy - 1)
    c0 = pl.multiple_of(chunk * CHUNK, CHUNK)
    mine = pl.ds(c0, CHUNK)
    loads = [(factors_hbm, factors), (loadings_hbm, loadings)]
    for a, b in zip(cuts, cuts[1:]):
        loads.append((presence_hbm.at[a:b], presence.at[a:b]))
        loads.append((noise_hbm.at[a:b], noise.at[a:b]))
    loads += [
        (neighbours_hbm.at[:, mine], neighbours),
        (weights_hbm.at[:, mine], weights),
        (precision_hbm, precision),
        (variance_hbm, variance),
        (factor_noise_hbm.at[:, mine], factor_noise),
    ]
    loads = [pltpu.make_async_copy(a, b, in_sems.at[i]) for i, (a, b) in enumerate(loads)]
    for load in loads:
        load.start()

    barrier = pltpu.get_barrier_semaphore()
    greeted = [{"site": z_peer(d)} for d in range(1, Z)]
    greeted += [{"site": x_peer(d)} for d in range(1, nx)]
    greeted += [{"site": ahead}, {"site": behind}]
    greeted += [{"sp": sp_peer(o)} for o in range(1, n_sp)]
    for peer in greeted:
        pl.semaphore_signal(barrier, inc=1, device_id=peer, device_id_type=MESH)

    def remote(src, dst, sems, send, recv, peer):
        return pltpu.make_async_remote_copy(
            src_ref=src,
            dst_ref=dst,
            send_sem=sems.at[0, send],
            recv_sem=sems.at[1, recv],
            device_id=peer,
            device_id_type=MESH,
        )

    def spread_z(buf, sems):
        copies = []
        for d in far_first(Z):
            copy = remote(buf.at[z], buf.at[z], sems, d, d, {"site": z_peer(d)})
            copy.start()
            copies.append(copy)
        return copies

    def spread_x(buf, sems):
        copies = []
        for d in far_first(nx):
            copy = remote(buf.at[x], buf.at[x], sems, d, d, {"site": x_peer(d)})
            copy.start()
            copies.append(copy)
        return copies

    def gather_z(buf, sems):
        for d in range(1, Z):
            s = (z + Z - d) % Z
            remote(buf.at[s], buf.at[s], sems, d, d, {"site": z_peer(d)}).wait_recv()
        acc = buf[0]
        for s in range(1, Z):
            acc = acc + buf[s]
        return acc

    def gather_x(buf, sems):
        for d in range(1, nx):
            s = (x + nx - d) % nx
            remote(buf.at[s], buf.at[s], sems, d, d, {"site": x_peer(d)}).wait_recv()
        acc = buf[0]
        for s in range(1, nx):
            acc = acc + buf[s]
        return acc

    started = []

    loads[0].wait()
    loads[1].wait()
    f = factors[...]
    hi, lo = split(f)
    fs[0:16, :] = hi
    fs[16:32, :] = lo
    fs[32:48, :] = hi
    window[:, RIM:] = f
    l_hi, l_lo = split(loadings[...])
    ls = jnp.concatenate([l_hi, l_hi, l_lo], axis=0)

    def draw_step(i, acc):
        r0 = pl.multiple_of(i * CHUNK, CHUNK)
        mean = dot(fs[:, pl.ds(r0, CHUNK)], ls, ((0,), (0,)))
        there = presence[pl.ds(r0, CHUNK), :] > 0
        t = jnp.where(there, mean, -mean)
        u = jnp.abs(t)
        density = jnp.exp(-0.5 * t * t) * inv_root_two_pi
        num = poly(N_COEF, u)
        den = poly(D_COEF, u)
        full = u * den + num
        negative = t < 0.0
        v = jnp.where(negative, num, density * full) / jnp.where(negative, den, full - density * den)
        s = v + jnp.maximum(t, 0.0)
        spread = jnp.maximum(1.0 - v * (v + u), 1e-30)
        draw = jnp.where(there, s, -s) + spread * lax.rsqrt(spread) * noise[pl.ds(r0, CHUNK), :].astype(F32)
        d_hi, d_lo = split(draw)
        utilities[pl.ds(r0, CHUNK), :] = d_hi
        pieces = jnp.concatenate([d_hi, d_lo], axis=1)
        draws[pl.ds(r0, CHUNK), :] = pieces
        return acc + dot(fs[0:32, pl.ds(r0, CHUNK)], pieces, ((1,), (0,)))

    acc = jnp.zeros((2 * K, 2 * species), F32)
    for piece in range(2):
        loads[2 + 2 * piece].wait()
        loads[3 + 2 * piece].wait()
        acc = lax.fori_loop(cuts[piece] // CHUNK, cuts[piece + 1] // CHUNK, draw_step, acc, unroll=True)

    products = dot(fs[0:32, :], fs[0:32, :], ((1,), (1,)))
    gram_part = blocks_sum(products, K, K)
    zeros = jnp.zeros((K, species), F32)
    gram_z[z] = zeros
    gram_z[z, :, 0:K] = gram_part

    pl.semaphore_wait(barrier, len(greeted))

    rim = remote(
        factors.at[:, rows - RIM : rows],
        window.at[:, 0:RIM],
        rim_sems,
        0,
        0,
        {"site": ahead},
    )
    started += spread_z(gram_z, gz_sems)
    rim.start()
    started.append(rim)

    loads[6].wait()
    loads[7].wait()
    acc = lax.fori_loop(cuts[2] // CHUNK, steps, draw_step, acc, unroll=True)
    cross_z[z] = blocks_sum(acc, K, species)
    started += spread_z(cross_z, cz_sems)
    gram_x[x] = gather_z(gram_z, gz_sems)
    started += spread_x(gram_x, gx_sems)

    for load in loads[8:]:
        load.wait()
    base = site * rows + chunk * CHUNK - RIM
    onehot[...] = jnp.zeros_like(onehot)
    iota = lax.broadcasted_iota(jnp.int32, (224, 128), 0)

    def mark(k, carry):
        ids = neighbours[pl.ds(k, 1), :]
        w = jnp.where(ids >= 0, weights[pl.ds(k, 1), :], 0.0)
        for q in range(CHUNK // 128):
            first = pl.multiple_of(RIM - STEP + 128 * q - STEP * k, 32)
            lanes = slice(128 * q, 128 * (q + 1))
            hit = iota == ids[:, lanes] - (base + first)
            onehot[pl.ds(first, 224), lanes] += jnp.where(hit, w[:, lanes], 0.0)
        return carry

    lax.fori_loop(0, NBR, mark, 0)
    rim.wait_recv()

    def gather_step(b, acc):
        r0 = pl.multiple_of(b * 256, 256)
        m_hi, m_lo = split(onehot[pl.ds(r0, 256), :])
        w_hi, w_lo = split(window[:, pl.ds(pl.multiple_of(c0 + r0, 256), 256)])
        return acc + dot(
            jnp.concatenate([w_hi, w_lo], axis=0),
            jnp.concatenate([m_hi, m_lo], axis=1),
            ((1,), (0,)),
        )

    prior = lax.fori_loop(0, WINDOW // 256, gather_step, jnp.zeros((2 * K, 2 * CHUNK), F32))
    prior = blocks_sum(prior, K, CHUNK)
    inverse = 1.0 / variance[pl.ds(c0, CHUNK)].reshape(1, CHUNK)
    shift = prior * inverse

    cross_x[x] = gather_z(cross_z, cz_sems)
    started += spread_x(cross_x, cx_sems)

    gram = gather_x(gram_x, gx_sems)[:, 0:K]
    inv_top, inv_bot, _ = cholesky(gram, [precision[k : k + 1, :] for k in range(K)])

    cross = gather_x(cross_x, cx_sems)
    fresh = solve(inv_top, inv_bot, cross)
    new_loadings[...] = fresh

    n_hi, n_lo = split(fresh)
    narrow = jnp.concatenate([n_hi, n_lo], axis=0)
    lgram_part = blocks_sum(dot(narrow, narrow, ((1,), (1,))), K, K)
    lgram_all[sp] = zeros
    lgram_all[sp, :, 0:K] = lgram_part
    for o in sorted(range(1, n_sp), key=lambda o: -min(o // CORES, ny - o // CORES)):
        copy = remote(lgram_all.at[sp], lgram_all.at[sp], ly_sems, o, o, {"sp": sp_peer(o)})
        copy.start()
        started.append(copy)

    zero = jnp.zeros_like(n_hi)
    wide = jnp.concatenate(
        [jnp.concatenate([n_hi, n_hi], axis=1), jnp.concatenate([n_lo, zero], axis=1)],
        axis=0,
    )

    def pull_of(t, c):
        r0 = pl.multiple_of((t * CORES + c) * CHUNK, CHUNK)
        p = dot(wide, draws[pl.ds(r0, CHUNK), :], ((1,), (1,)))
        return p[:K] + p[K:]

    order = far_first(ny)
    order.remove(busy)
    order.append(busy)
    for e in order:
        pull_out[e - 1] = pull_of((y + e) % busy, 1 - core)
    for e in order:
        copy = remote(pull_out.at[e - 1], pull_pair.at[e - 1], pp_sems, e - 1, e - 1, {"sp": pair})
        copy.start()
        started.append(copy)

    for e in order:
        pull_mine[e - 1] = pull_of((y + e) % busy, core)
    for e in order:
        t = (y + e) % busy
        remote(pull_out.at[e - 1], pull_pair.at[e - 1], pp_sems, e - 1, e - 1, {"sp": pair}).wait_recv()
        pull_mine[e - 1] += pull_pair[e - 1]
        copy = remote(pull_mine.at[e - 1], pull_y.at[y], py_sems, e, y, {"sp": t * CORES + core})
        if e < busy:
            copy.start()
            started.append(copy)
        else:

            @pl.when(y == busy)
            def _():
                copy.start()

            last_pull = copy

    for o in range(1, n_sp):
        s = ((y + ny - o // CORES) % ny) * CORES + (core + o) % CORES
        remote(lgram_all.at[s], lgram_all.at[s], ly_sems, o, o, {"sp": s}).wait_recv()

    def factors_to(sems, send, recv, index, peer):
        lanes = pl.ds(pl.multiple_of(index * CHUNK, CHUNK), CHUNK)
        return remote(new_factors.at[:, lanes], new_factors.at[:, lanes], sems, send, recv, peer)

    @pl.when(y < busy)
    def _():
        lgram = lgram_all[0]
        for s in range(1, n_sp):
            lgram = lgram + lgram_all[s]
        site_top, site_bot, pivots = cholesky(lgram[:, 0:K], [inverse] * K)
        total = pull_mine[busy - 1] + (shift + apply_pivots(pivots, factor_noise[...]))
        for d in range(1, ny):
            s = (y + d) % ny
            remote(pull_y.at[s], pull_y.at[s], py_sems, 0, s, {"sp": s * CORES + core}).wait_recv()
            total = total + pull_y[s]
        result = solve(site_top, site_bot, total)
        new_factors[:, pl.ds(c0, CHUNK)] = result
        for d in far_first(ny):
            t = (y + d) % ny
            factors_to(fy_sems, d, y, y * CORES + core, {"sp": t * CORES + core}).start()
        factors_to(fp_sems, y, y, y * CORES + core, {"sp": pair}).start()

    for copy in started:
        copy.wait_send()

    for e in order[busy - 2 :: -1] + [busy]:
        s = (y + busy - e) % busy

        def hand_on():
            factors_to(fy_sems, 0, s, s * CORES + core, {"sp": s * CORES + core}).wait_recv()
            factors_to(fp_sems, s, s, s * CORES + core, {"sp": pair}).start()

        if e < busy:
            hand_on()
        else:
            pl.when(y == busy)(hand_on)

    for s in range(busy):
        factors_to(fp_sems, s, s, s * CORES + (1 - core), {"sp": pair}).wait_recv()

    for s in range(busy):
        factors_to(fp_sems, s, s, s * CORES + core, {"sp": pair}).wait_send()

    @pl.when(y == busy)
    def _():
        last_pull.wait_send()

    @pl.when(y < busy)
    def _():
        for d in range(1, ny):
            t = (y + d) % ny
            factors_to(fy_sems, d, y, y * CORES + core, {"sp": t * CORES + core}).wait_send()


def write_out(a, b, c, a_out, b_out, c_out, sems):
    cut = a.shape[0] // PIECES
    rows = [slice(i * cut, (i + 1) * cut) for i in range(PIECES)]
    pairs = [(c, c_out), (b, b_out)] + [(a.at[r], a_out.at[r]) for r in rows]
    writes = [pltpu.make_async_copy(src, dst, sems.at[i]) for i, (src, dst) in enumerate(pairs)]
    for write in writes:
        write.start()
    for write in writes:
        write.wait()


def solution(mesh):
    n_site, n_sp = mesh.shape["site"], mesh.shape["sp"]
    nx, ny = n_site // Z, n_sp // CORES
    busy = ny - 1

    def shards(presence, noise, factors, loadings, precision, neighbours, weights, variance, factor_noise):
        rows, species = presence.shape
        assert rows == busy * CORES * CHUNK and species == 128
        vmem = pl.BlockSpec(memory_space=pltpu.VMEM)
        hbm = pl.BlockSpec(memory_space=pltpu.HBM)
        sems = pltpu.SemaphoreType.DMA
        out_shape = (
            jax.ShapeDtypeStruct((rows, species), BF16),
            jax.ShapeDtypeStruct((K, species), F32),
            jax.ShapeDtypeStruct((K, rows), F32),
        )
        results = pl.pallas_call(
            functools.partial(kernel, n_site, n_sp),
            out_shape=tuple(pltpu.VMEM(v.shape, v.dtype) for v in out_shape),
            in_specs=[hbm] * 9,
            out_specs=(vmem,) * 3,
            scratch_shapes=[
                pltpu.VMEM((rows, species), jnp.int32),
                pltpu.VMEM((rows, species), BF16),
                pltpu.VMEM((K, rows), F32),
                pltpu.VMEM((K, species), F32),
                pltpu.VMEM((K, species), F32),
                pltpu.VMEM((NBR, CHUNK), jnp.int32),
                pltpu.VMEM((NBR, CHUNK), F32),
                pltpu.VMEM((rows,), F32),
                pltpu.VMEM((K, CHUNK), F32),
                sems((13,)),
                pltpu.VMEM((3 * K, rows), BF16),
                pltpu.VMEM((rows, 2 * species), BF16),
                pltpu.VMEM((K, RIM + rows), F32),
                pltpu.VMEM((WINDOW, CHUNK), F32),
                pltpu.VMEM((Z, K, species), F32),
                pltpu.VMEM((nx, K, species), F32),
                pltpu.VMEM((Z, K, species), F32),
                pltpu.VMEM((nx, K, species), F32),
                pltpu.VMEM((n_sp, K, species), F32),
                pltpu.VMEM((busy, K, CHUNK), F32),
                pltpu.VMEM((busy, K, CHUNK), F32),
                pltpu.VMEM((busy, K, CHUNK), F32),
                pltpu.VMEM((ny, K, CHUNK), F32),
                sems((2, 1)),
                sems((2, Z)),
                sems((2, nx)),
                sems((2, Z)),
                sems((2, nx)),
                sems((2, n_sp)),
                sems((2, busy)),
                sems((2, ny)),
                sems((2, ny)),
                sems((2, busy)),
            ],
            compiler_params=pltpu.CompilerParams(
                collective_id=0,
                has_side_effects=True,
                vmem_limit_bytes=60 * 1024 * 1024,
            ),
        )(presence, noise, factors, loadings, precision, neighbours, weights, variance, factor_noise)
        return pl.pallas_call(
            write_out,
            out_shape=out_shape,
            in_specs=[vmem] * 3,
            out_specs=(hbm,) * 3,
            scratch_shapes=[sems((PIECES + 2,))],
        )(*[pltpu.with_memory_space_constraint(v, pltpu.VMEM) for v in results])

    in_specs = (
        P("site", "sp"),
        P("site", "sp"),
        P(None, "site"),
        P(None, "sp"),
        P(None, "sp"),
        P(None, "site"),
        P(None, "site"),
        P("site"),
        P(None, "site"),
    )
    out_specs = (P("site", "sp"), P(None, "sp"), P(None, "site"))
    return jax.shard_map(shards, mesh=mesh, in_specs=in_specs, out_specs=out_specs, check_vma=False)
```

```python
import functools

import jax
import jax.numpy as jnp
from jax import lax
from jax.experimental import pallas as pl
from jax.experimental.pallas import tpu as pltpu
from jax.sharding import PartitionSpec as P

F32 = jnp.float32
BF16 = jnp.bfloat16
MESH = pl.DeviceIdType.MESH

Z = 8
CORES = 2
K = 16
NBR = 15
CHUNK = 256
RIM = 1536
WINDOW = RIM + CHUNK
HALF = 8
STEP = 96
PIECES = 4

N_COEF = (0.7978845828848753, 0.561783412736638, 0.19921040380039692, 0.039025408597369395, 0.0036777514496204662)
D_COEF = (1.0, 1.1595221251207712, 0.6411219754723788, 0.20649649681102156, 0.03902744122918637, 0.003677727281734947)
inv_root_two_pi = 0.3989422804014327


def poly(coef, u):
    acc = u * coef[-1] + coef[-2]
    for a in coef[-3::-1]:
        acc = acc * u + a
    return acc


def split(x):
    hi = x.astype(BF16)
    return hi, (x - hi.astype(F32)).astype(BF16)


def dot(a, b, dims):
    return lax.dot_general(a, b, (dims, ((), ())), preferred_element_type=F32)


def blocks_sum(p, rows, cols):
    return (p[:rows, :cols] + p[:rows, cols:]) + (p[rows:, :cols] + p[rows:, cols:])


def cholesky(base, extra):
    width = extra[0].shape[1]
    row = lax.broadcasted_iota(jnp.int32, (HALF, width), 0)
    top, bot = [], []
    for k in range(K):
        diag = jnp.where(row == k % HALF, extra[k], 0.0)
        column = base[:, k : k + 1]
        if k < HALF:
            top.append(column[:HALF] + diag)
            bot.append(column[HALF:] + jnp.zeros_like(diag))
        else:
            top.append(None)
            bot.append(column[HALF:] + diag)
    inv_top = [jnp.where(row == k, 1.0, 0.0) if k < HALF else jnp.zeros((HALF, width), F32) for k in range(K)]
    inv_bot = [None if k < HALF else jnp.where(row == k - HALF, 1.0, 0.0) for k in range(K)]
    pivots = []
    for j in range(K):
        d = top[j][j : j + 1] if j < HALF else bot[j][j - HALF : j - HALF + 1]
        r = lax.rsqrt(d)
        pivots.append(d * r)
        bot[j] = bot[j] * r
        inv_top[j] = inv_top[j] * r
        if j < HALF:
            top[j] = top[j] * r
        else:
            inv_bot[j] = inv_bot[j] * r
        for k in range(j + 1, K):
            if k < HALF:
                s = top[j][k : k + 1]
                top[k] = top[k] - top[j] * s
                bot[k] = bot[k] - bot[j] * s
            else:
                s = bot[j][k - HALF : k - HALF + 1]
                bot[k] = bot[k] - bot[j] * s
            inv_top[k] = inv_top[k] - inv_top[j] * s
            if j >= HALF:
                inv_bot[k] = inv_bot[k] - inv_bot[j] * s
    return inv_top, inv_bot, pivots


def apply_pivots(pivots, noise):
    row = lax.broadcasted_iota(jnp.int32, noise.shape, 0)
    acc = jnp.zeros_like(noise)
    for j in range(K):
        acc = jnp.where(row == j, pivots[j], acc)
    return acc * noise


def solve(inv_top, inv_bot, rhs):
    top, bot = rhs[:HALF], rhs[HALF:]
    x_top = x_bot = None
    for j in range(K):
        terms = inv_top[j] * top
        if j >= HALF:
            terms = terms + inv_bot[j] * bot
        y = jnp.sum(terms, axis=0, keepdims=True)
        x_top = inv_top[j] * y if x_top is None else x_top + inv_top[j] * y
        if j >= HALF:
            x_bot = inv_bot[j] * y if x_bot is None else x_bot + inv_bot[j] * y
    return jnp.concatenate([x_top, x_bot], axis=0)


def total_of(ref, count):
    parts = [ref[i] for i in range(count)]
    while len(parts) > 1:
        parts = [a + b for a, b in zip(parts[::2], parts[1::2])] + parts[len(parts) // 2 * 2 :]
    return parts[0]


def far_first(n):
    return sorted(range(1, n), key=lambda d: -min(d, n - d))


def kernel(
    n_site,
    n_sp,
    presence_hbm,
    noise_hbm,
    factors_hbm,
    loadings_hbm,
    precision_hbm,
    neighbours_hbm,
    weights_hbm,
    variance_hbm,
    factor_noise_hbm,
    utilities,
    new_loadings,
    new_factors,
    presence,
    noise,
    factors,
    loadings,
    precision,
    neighbours,
    weights,
    variance,
    factor_noise,
    in_sems,
    fs,
    draws,
    window,
    onehot,
    gram_z,
    gram_x,
    cross_all,
    lgram_all,
    pull_out,
    pull_pair,
    pull_mine,
    pull_y,
    rim_sems,
    gz_sems,
    gx_sems,
    cross_sems,
    ly_sems,
    pp_sems,
    py_sems,
    fy_sems,
    fp_sems,
):
    nx = n_site // Z
    ny = n_sp // CORES
    busy = ny - 1
    rows = factors.shape[1]
    steps = rows // CHUNK
    cuts = (0, min(2, steps // 2) * CHUNK, steps // 2 * CHUNK, rows)
    species = loadings.shape[1]

    site = lax.axis_index("site")
    sp = lax.axis_index("sp")
    x, z = site // Z, site % Z
    y, core = sp // CORES, sp % CORES
    pair = y * CORES + (1 - core)
    ahead = (site + 1) % n_site

    def z_peer(d):
        return x * Z + (z + d) % Z

    def site_peer(o, sign=1):
        return ((x + nx + sign * (o // Z)) % nx) * Z + (z + Z + sign * (o % Z)) % Z

    def hops(o):
        dx, dz = o // Z, o % Z
        return min(dx, nx - dx) + min(dz, Z - dz)

    def sp_peer(o):
        return ((y + o // CORES) % ny) * CORES + (core + o) % CORES

    def x_peer(d):
        return ((x + d) % nx) * Z + z

    chunk = jnp.minimum(sp, CORES * busy - 1)
    c0 = pl.multiple_of(chunk * CHUNK, CHUNK)
    mine = pl.ds(c0, CHUNK)
    loads = [(factors_hbm, factors), (loadings_hbm, loadings)]
    for a, b in zip(cuts, cuts[1:]):
        loads.append((presence_hbm.at[a:b], presence.at[a:b]))
        loads.append((noise_hbm.at[a:b], noise.at[a:b]))
    loads += [
        (neighbours_hbm.at[:, mine], neighbours),
        (weights_hbm.at[:, mine], weights),
        (precision_hbm, precision),
        (variance_hbm, variance),
        (factor_noise_hbm.at[:, mine], factor_noise),
    ]
    loads = [pltpu.make_async_copy(a, b, in_sems.at[i]) for i, (a, b) in enumerate(loads)]
    for load in loads:
        load.start()

    barrier = pltpu.get_barrier_semaphore()
    greeted = [{"site": (site + d) % n_site} for d in range(1, n_site)]
    greeted += [{"sp": sp_peer(o)} for o in range(1, n_sp)]
    for peer in greeted:
        pl.semaphore_signal(barrier, inc=1, device_id=peer, device_id_type=MESH)

    def remote(src, dst, sems, send, recv, peer):
        return pltpu.make_async_remote_copy(
            src_ref=src,
            dst_ref=dst,
            send_sem=sems.at[0, send],
            recv_sem=sems.at[1, recv],
            device_id=peer,
            device_id_type=MESH,
        )

    def spread_z(buf, sems):
        copies = []
        for d in far_first(Z):
            copy = remote(buf.at[z], buf.at[z], sems, d, d, {"site": z_peer(d)})
            copy.start()
            copies.append(copy)
        return copies

    def spread_x(buf, sems):
        copies = []
        for d in far_first(nx):
            copy = remote(buf.at[x], buf.at[x], sems, d, d, {"site": x_peer(d)})
            copy.start()
            copies.append(copy)
        return copies

    def gather_z(buf, sems):
        for d in range(1, Z):
            s = (z + Z - d) % Z
            remote(buf.at[s], buf.at[s], sems, d, d, {"site": z_peer(d)}).wait_recv()
        acc = buf[0]
        for s in range(1, Z):
            acc = acc + buf[s]
        return acc

    def gather_x(buf, sems):
        for d in range(1, nx):
            s = (x + nx - d) % nx
            remote(buf.at[s], buf.at[s], sems, d, d, {"site": x_peer(d)}).wait_recv()
        acc = buf[0]
        for s in range(1, nx):
            acc = acc + buf[s]
        return acc

    started = []

    loads[0].wait()
    loads[1].wait()
    f = factors[...]
    hi, lo = split(f)
    fs[0:16, :] = hi
    fs[16:32, :] = lo
    fs[32:48, :] = hi
    window[:, RIM:] = f
    l_hi, l_lo = split(loadings[...])
    ls = jnp.concatenate([l_hi, l_hi, l_lo], axis=0)

    def draw_step(i, acc):
        r0 = pl.multiple_of(i * CHUNK, CHUNK)
        mean = dot(fs[:, pl.ds(r0, CHUNK)], ls, ((0,), (0,)))
        there = presence[pl.ds(r0, CHUNK), :] > 0
        t = jnp.where(there, mean, -mean)
        u = jnp.abs(t)
        density = jnp.exp(-0.5 * t * t) * inv_root_two_pi
        num = poly(N_COEF, u)
        den = poly(D_COEF, u)
        full = u * den + num
        negative = t < 0.0
        v = jnp.where(negative, num, density * full) / jnp.where(negative, den, full - density * den)
        s = v + jnp.maximum(t, 0.0)
        spread = jnp.maximum(1.0 - v * (v + u), 1e-30)
        draw = jnp.where(there, s, -s) + spread * lax.rsqrt(spread) * noise[pl.ds(r0, CHUNK), :].astype(F32)
        d_hi, d_lo = split(draw)
        utilities[pl.ds(r0, CHUNK), :] = d_hi
        pieces = jnp.concatenate([d_hi, d_lo], axis=1)
        draws[pl.ds(r0, CHUNK), :] = pieces
        return acc + dot(fs[0:32, pl.ds(r0, CHUNK)], pieces, ((1,), (0,)))

    acc = jnp.zeros((2 * K, 2 * species), F32)
    for piece in range(2):
        loads[2 + 2 * piece].wait()
        loads[3 + 2 * piece].wait()
        acc = lax.fori_loop(cuts[piece] // CHUNK, cuts[piece + 1] // CHUNK, draw_step, acc, unroll=True)

    products = dot(fs[0:32, :], fs[0:32, :], ((1,), (1,)))
    gram_part = blocks_sum(products, K, K)
    zeros = jnp.zeros((K, species), F32)
    gram_z[z] = zeros
    gram_z[z, :, 0:K] = gram_part

    pl.semaphore_wait(barrier, len(greeted))

    rim = remote(
        factors.at[:, rows - RIM : rows],
        window.at[:, 0:RIM],
        rim_sems,
        0,
        0,
        {"site": ahead},
    )
    started += spread_z(gram_z, gz_sems)
    rim.start()
    started.append(rim)

    loads[6].wait()
    loads[7].wait()
    acc = lax.fori_loop(cuts[2] // CHUNK, steps, draw_step, acc, unroll=True)
    cross_all[site] = blocks_sum(acc, K, species)
    for o in sorted(range(1, n_site), key=lambda o: -hops(o)):
        copy = remote(cross_all.at[site], cross_all.at[site], cross_sems, o, o, {"site": site_peer(o)})
        copy.start()
        started.append(copy)
    gram_x[x] = gather_z(gram_z, gz_sems)
    started += spread_x(gram_x, gx_sems)

    for load in loads[8:]:
        load.wait()
    base = site * rows + chunk * CHUNK - RIM
    onehot[...] = jnp.zeros_like(onehot)
    iota = lax.broadcasted_iota(jnp.int32, (224, 128), 0)

    def mark(k, carry):
        ids = neighbours[pl.ds(k, 1), :]
        w = jnp.where(ids >= 0, weights[pl.ds(k, 1), :], 0.0)
        for q in range(CHUNK // 128):
            first = pl.multiple_of(RIM - STEP + 128 * q - STEP * k, 32)
            lanes = slice(128 * q, 128 * (q + 1))
            hit = iota == ids[:, lanes] - (base + first)
            onehot[pl.ds(first, 224), lanes] += jnp.where(hit, w[:, lanes], 0.0)
        return carry

    lax.fori_loop(0, NBR, mark, 0)
    rim.wait_recv()

    def gather_step(b, acc):
        r0 = pl.multiple_of(b * 256, 256)
        m_hi, m_lo = split(onehot[pl.ds(r0, 256), :])
        w_hi, w_lo = split(window[:, pl.ds(pl.multiple_of(c0 + r0, 256), 256)])
        return acc + dot(
            jnp.concatenate([w_hi, w_lo], axis=0),
            jnp.concatenate([m_hi, m_lo], axis=1),
            ((1,), (0,)),
        )

    prior = lax.fori_loop(0, WINDOW // 256, gather_step, jnp.zeros((2 * K, 2 * CHUNK), F32))
    prior = blocks_sum(prior, K, CHUNK)
    inverse = 1.0 / variance[pl.ds(c0, CHUNK)].reshape(1, CHUNK)
    shift = prior * inverse

    gram = gather_x(gram_x, gx_sems)[:, 0:K]
    inv_top, inv_bot, _ = cholesky(gram, [precision[k : k + 1, :] for k in range(K)])

    for o in sorted(range(1, n_site), key=hops):
        s = site_peer(o, -1)
        remote(cross_all.at[s], cross_all.at[s], cross_sems, o, o, {"site": s}).wait_recv()
    cross = total_of(cross_all, n_site)
    fresh = solve(inv_top, inv_bot, cross)
    new_loadings[...] = fresh

    n_hi, n_lo = split(fresh)
    narrow = jnp.concatenate([n_hi, n_lo], axis=0)
    lgram_part = blocks_sum(dot(narrow, narrow, ((1,), (1,))), K, K)
    lgram_all[sp] = zeros
    lgram_all[sp, :, 0:K] = lgram_part
    for o in sorted(range(1, n_sp), key=lambda o: -min(o // CORES, ny - o // CORES)):
        copy = remote(lgram_all.at[sp], lgram_all.at[sp], ly_sems, o, o, {"sp": sp_peer(o)})
        copy.start()
        started.append(copy)

    zero = jnp.zeros_like(n_hi)
    wide = jnp.concatenate(
        [jnp.concatenate([n_hi, n_hi], axis=1), jnp.concatenate([n_lo, zero], axis=1)],
        axis=0,
    )

    def pull_of(t, c):
        r0 = pl.multiple_of((t * CORES + c) * CHUNK, CHUNK)
        p = dot(wide, draws[pl.ds(r0, CHUNK), :], ((1,), (1,)))
        return p[:K] + p[K:]

    order = far_first(ny)
    order.remove(busy)
    order.append(busy)
    for e in order:
        pull_out[e - 1] = pull_of((y + e) % busy, 1 - core)
    for e in order:
        copy = remote(pull_out.at[e - 1], pull_pair.at[e - 1], pp_sems, e - 1, e - 1, {"sp": pair})
        copy.start()
        started.append(copy)

    for e in order:
        pull_mine[e - 1] = pull_of((y + e) % busy, core)
    for e in order:
        t = (y + e) % busy
        remote(pull_out.at[e - 1], pull_pair.at[e - 1], pp_sems, e - 1, e - 1, {"sp": pair}).wait_recv()
        pull_mine[e - 1] += pull_pair[e - 1]
        copy = remote(pull_mine.at[e - 1], pull_y.at[y], py_sems, e, y, {"sp": t * CORES + core})
        if e < busy:
            copy.start()
            started.append(copy)
        else:

            @pl.when(y == busy)
            def _():
                copy.start()

            last_pull = copy

    for o in range(1, n_sp):
        s = ((y + ny - o // CORES) % ny) * CORES + (core + o) % CORES
        remote(lgram_all.at[s], lgram_all.at[s], ly_sems, o, o, {"sp": s}).wait_recv()

    def factors_to(sems, send, recv, index, peer):
        lanes = pl.ds(pl.multiple_of(index * CHUNK, CHUNK), CHUNK)
        return remote(new_factors.at[:, lanes], new_factors.at[:, lanes], sems, send, recv, peer)

    @pl.when(y < busy)
    def _():
        lgram = total_of(lgram_all, n_sp)
        site_top, site_bot, pivots = cholesky(lgram[:, 0:K], [inverse] * K)
        total = pull_mine[busy - 1] + (shift + apply_pivots(pivots, factor_noise[...]))
        for d in range(1, ny):
            s = (y + d) % ny
            remote(pull_y.at[s], pull_y.at[s], py_sems, 0, s, {"sp": s * CORES + core}).wait_recv()
            total = total + pull_y[s]
        result = solve(site_top, site_bot, total)
        new_factors[:, pl.ds(c0, CHUNK)] = result
        for d in far_first(ny):
            t = (y + d) % ny
            factors_to(fy_sems, d, y, y * CORES + core, {"sp": t * CORES + core}).start()
        factors_to(fp_sems, y, y, y * CORES + core, {"sp": pair}).start()

    for copy in started:
        copy.wait_send()

    for e in order[busy - 2 :: -1] + [busy]:
        s = (y + busy - e) % busy

        def hand_on():
            factors_to(fy_sems, 0, s, s * CORES + core, {"sp": s * CORES + core}).wait_recv()
            factors_to(fp_sems, s, s, s * CORES + core, {"sp": pair}).start()

        if e < busy:
            hand_on()
        else:
            pl.when(y == busy)(hand_on)

    for s in range(busy):
        factors_to(fp_sems, s, s, s * CORES + (1 - core), {"sp": pair}).wait_recv()

    for s in range(busy):
        factors_to(fp_sems, s, s, s * CORES + core, {"sp": pair}).wait_send()

    @pl.when(y == busy)
    def _():
        last_pull.wait_send()

    @pl.when(y < busy)
    def _():
        for d in range(1, ny):
            t = (y + d) % ny
            factors_to(fy_sems, d, y, y * CORES + core, {"sp": t * CORES + core}).wait_send()


def write_out(a, b, c, a_out, b_out, c_out, sems):
    cut = a.shape[0] // PIECES
    rows = [slice(i * cut, (i + 1) * cut) for i in range(PIECES)]
    pairs = [(c, c_out), (b, b_out)] + [(a.at[r], a_out.at[r]) for r in rows]
    writes = [pltpu.make_async_copy(src, dst, sems.at[i]) for i, (src, dst) in enumerate(pairs)]
    for write in writes:
        write.start()
    for write in writes:
        write.wait()


def solution(mesh):
    n_site, n_sp = mesh.shape["site"], mesh.shape["sp"]
    nx, ny = n_site // Z, n_sp // CORES
    busy = ny - 1

    def shards(presence, noise, factors, loadings, precision, neighbours, weights, variance, factor_noise):
        rows, species = presence.shape
        assert rows == busy * CORES * CHUNK and species == 128
        vmem = pl.BlockSpec(memory_space=pltpu.VMEM)
        hbm = pl.BlockSpec(memory_space=pltpu.HBM)
        sems = pltpu.SemaphoreType.DMA
        out_shape = (
            jax.ShapeDtypeStruct((rows, species), BF16),
            jax.ShapeDtypeStruct((K, species), F32),
            jax.ShapeDtypeStruct((K, rows), F32),
        )
        results = pl.pallas_call(
            functools.partial(kernel, n_site, n_sp),
            out_shape=tuple(pltpu.VMEM(v.shape, v.dtype) for v in out_shape),
            in_specs=[hbm] * 9,
            out_specs=(vmem,) * 3,
            scratch_shapes=[
                pltpu.VMEM((rows, species), jnp.int32),
                pltpu.VMEM((rows, species), BF16),
                pltpu.VMEM((K, rows), F32),
                pltpu.VMEM((K, species), F32),
                pltpu.VMEM((K, species), F32),
                pltpu.VMEM((NBR, CHUNK), jnp.int32),
                pltpu.VMEM((NBR, CHUNK), F32),
                pltpu.VMEM((rows,), F32),
                pltpu.VMEM((K, CHUNK), F32),
                sems((13,)),
                pltpu.VMEM((3 * K, rows), BF16),
                pltpu.VMEM((rows, 2 * species), BF16),
                pltpu.VMEM((K, RIM + rows), F32),
                pltpu.VMEM((WINDOW, CHUNK), F32),
                pltpu.VMEM((Z, K, species), F32),
                pltpu.VMEM((nx, K, species), F32),
                pltpu.VMEM((n_site, K, species), F32),
                pltpu.VMEM((n_sp, K, species), F32),
                pltpu.VMEM((busy, K, CHUNK), F32),
                pltpu.VMEM((busy, K, CHUNK), F32),
                pltpu.VMEM((busy, K, CHUNK), F32),
                pltpu.VMEM((ny, K, CHUNK), F32),
                sems((2, 1)),
                sems((2, Z)),
                sems((2, nx)),
                sems((2, n_site)),
                sems((2, n_sp)),
                sems((2, busy)),
                sems((2, ny)),
                sems((2, ny)),
                sems((2, busy)),
            ],
            compiler_params=pltpu.CompilerParams(
                collective_id=0,
                has_side_effects=True,
                vmem_limit_bytes=60 * 1024 * 1024,
            ),
        )(presence, noise, factors, loadings, precision, neighbours, weights, variance, factor_noise)
        return pl.pallas_call(
            write_out,
            out_shape=out_shape,
            in_specs=[vmem] * 3,
            out_specs=(hbm,) * 3,
            scratch_shapes=[sems((PIECES + 2,))],
        )(*[pltpu.with_memory_space_constraint(v, pltpu.VMEM) for v in results])

    in_specs = (
        P("site", "sp"),
        P("site", "sp"),
        P(None, "site"),
        P(None, "sp"),
        P(None, "sp"),
        P(None, "site"),
        P(None, "site"),
        P("site"),
        P(None, "site"),
    )
    out_specs = (P("site", "sp"), P(None, "sp"), P(None, "site"))
    return jax.shard_map(shards, mesh=mesh, in_specs=in_specs, out_specs=out_specs, check_vma=False)
```

```python
import functools

import jax
import jax.numpy as jnp
from jax import lax
from jax.experimental import pallas as pl
from jax.experimental.pallas import tpu as pltpu
from jax.sharding import PartitionSpec as P

F32 = jnp.float32
BF16 = jnp.bfloat16
MESH = pl.DeviceIdType.MESH

Z = 8
CORES = 2
K = 16
NBR = 15
CHUNK = 256
RIM = 1536
WINDOW = RIM + CHUNK
HALF = 8
STEP = 96
PIECES = 4

N_COEF = (0.7978845828848753, 0.561783412736638, 0.19921040380039692, 0.039025408597369395, 0.0036777514496204662)
D_COEF = (1.0, 1.1595221251207712, 0.6411219754723788, 0.20649649681102156, 0.03902744122918637, 0.003677727281734947)
inv_root_two_pi = 0.3989422804014327


def poly(coef, u):
    acc = u * coef[-1] + coef[-2]
    for a in coef[-3::-1]:
        acc = acc * u + a
    return acc


def split(x):
    hi = x.astype(BF16)
    return hi, (x - hi.astype(F32)).astype(BF16)


def dot(a, b, dims):
    return lax.dot_general(a, b, (dims, ((), ())), preferred_element_type=F32)


def blocks_sum(p, rows, cols):
    return (p[:rows, :cols] + p[:rows, cols:]) + (p[rows:, :cols] + p[rows:, cols:])


def cholesky(base, extra):
    width = extra[0].shape[1]
    row = lax.broadcasted_iota(jnp.int32, (HALF, width), 0)
    top, bot = [], []
    for k in range(K):
        diag = jnp.where(row == k % HALF, extra[k], 0.0)
        lower = base[:, K + k : K + k + 1]
        if k < HALF:
            top.append(base[:, k : k + 1] + diag)
            bot.append(lower + jnp.zeros_like(diag))
        else:
            top.append(None)
            bot.append(lower + diag)
    inv_top = [jnp.where(row == k, 1.0, 0.0) if k < HALF else jnp.zeros((HALF, width), F32) for k in range(K)]
    inv_bot = [None if k < HALF else jnp.where(row == k - HALF, 1.0, 0.0) for k in range(K)]
    pivots = []
    for j in range(K):
        d = top[j][j : j + 1] if j < HALF else bot[j][j - HALF : j - HALF + 1]
        r = lax.rsqrt(d)
        pivots.append(d * r)
        bot[j] = bot[j] * r
        inv_top[j] = inv_top[j] * r
        if j < HALF:
            top[j] = top[j] * r
        else:
            inv_bot[j] = inv_bot[j] * r
        for k in range(j + 1, K):
            if k < HALF:
                s = top[j][k : k + 1]
                top[k] = top[k] - top[j] * s
                bot[k] = bot[k] - bot[j] * s
            else:
                s = bot[j][k - HALF : k - HALF + 1]
                bot[k] = bot[k] - bot[j] * s
            inv_top[k] = inv_top[k] - inv_top[j] * s
            if j >= HALF:
                inv_bot[k] = inv_bot[k] - inv_bot[j] * s
    return inv_top, inv_bot, pivots


def apply_pivots(pivots, noise):
    row = lax.broadcasted_iota(jnp.int32, noise.shape, 0)
    acc = jnp.zeros_like(noise)
    for j in range(K):
        acc = jnp.where(row == j, pivots[j], acc)
    return acc * noise


def solve(inv_top, inv_bot, rhs):
    top, bot = rhs[:HALF], rhs[HALF:]
    x_top = x_bot = None
    for j in range(K):
        terms = inv_top[j] * top
        if j >= HALF:
            terms = terms + inv_bot[j] * bot
        y = jnp.sum(terms, axis=0, keepdims=True)
        x_top = inv_top[j] * y if x_top is None else x_top + inv_top[j] * y
        if j >= HALF:
            x_bot = inv_bot[j] * y if x_bot is None else x_bot + inv_bot[j] * y
    return jnp.concatenate([x_top, x_bot], axis=0)


def far_first(n):
    return sorted(range(1, n), key=lambda d: -min(d, n - d))


def kernel(
    n_site,
    n_sp,
    presence_hbm,
    noise_hbm,
    factors_hbm,
    loadings_hbm,
    precision_hbm,
    neighbours_hbm,
    weights_hbm,
    variance_hbm,
    factor_noise_hbm,
    utilities,
    new_loadings,
    new_factors,
    presence,
    noise,
    factors,
    loadings,
    precision,
    neighbours,
    weights,
    variance,
    factor_noise,
    in_sems,
    fs,
    draws,
    window,
    onehot,
    gram_z,
    gram_x,
    cross_z,
    cross_x,
    lgram_all,
    pull_out,
    pull_pair,
    pull_mine,
    pull_y,
    rim_sems,
    gz_sems,
    gx_sems,
    cz_sems,
    cx_sems,
    ly_sems,
    pp_sems,
    py_sems,
    fy_sems,
    fp_sems,
):
    nx = n_site // Z
    ny = n_sp // CORES
    busy = ny - 1
    rows = factors.shape[1]
    steps = rows // CHUNK
    cuts = (0, min(2, steps // 2) * CHUNK, steps // 2 * CHUNK, rows)
    species = loadings.shape[1]

    site = lax.axis_index("site")
    sp = lax.axis_index("sp")
    x, z = site // Z, site % Z
    y, core = sp // CORES, sp % CORES
    pair = y * CORES + (1 - core)
    ahead = (site + 1) % n_site
    behind = (site + n_site - 1) % n_site

    def z_peer(d):
        return x * Z + (z + d) % Z

    def sp_peer(o):
        return ((y + o // CORES) % ny) * CORES + (core + o) % CORES

    def x_peer(d):
        return ((x + d) % nx) * Z + z

    chunk = jnp.minimum(sp, CORES * busy - 1)
    c0 = pl.multiple_of(chunk * CHUNK, CHUNK)
    mine = pl.ds(c0, CHUNK)
    loads = [(factors_hbm, factors), (loadings_hbm, loadings)]
    for a, b in zip(cuts, cuts[1:]):
        loads.append((presence_hbm.at[a:b], presence.at[a:b]))
        loads.append((noise_hbm.at[a:b], noise.at[a:b]))
    loads += [
        (neighbours_hbm.at[:, mine], neighbours),
        (weights_hbm.at[:, mine], weights),
        (precision_hbm, precision),
        (variance_hbm, variance),
        (factor_noise_hbm.at[:, mine], factor_noise),
    ]
    loads = [pltpu.make_async_copy(a, b, in_sems.at[i]) for i, (a, b) in enumerate(loads)]
    for load in loads[:6]:
        load.start()

    barrier = pltpu.get_barrier_semaphore()
    greeted = [{"site": z_peer(d)} for d in range(1, Z)]
    greeted += [{"site": x_peer(d)} for d in range(1, nx)]
    greeted += [{"site": ahead}, {"site": behind}]
    greeted += [{"sp": sp_peer(o)} for o in range(1, n_sp)]
    for peer in greeted:
        pl.semaphore_signal(barrier, inc=1, device_id=peer, device_id_type=MESH)

    def remote(src, dst, sems, send, recv, peer):
        return pltpu.make_async_remote_copy(
            src_ref=src,
            dst_ref=dst,
            send_sem=sems.at[0, send],
            recv_sem=sems.at[1, recv],
            device_id=peer,
            device_id_type=MESH,
        )

    def spread_z(buf, sems):
        copies = []
        for d in far_first(Z):
            copy = remote(buf.at[z], buf.at[z], sems, d, d, {"site": z_peer(d)})
            copy.start()
            copies.append(copy)
        return copies

    def spread_x(buf, sems):
        copies = []
        for d in far_first(nx):
            copy = remote(buf.at[x], buf.at[x], sems, d, d, {"site": x_peer(d)})
            copy.start()
            copies.append(copy)
        return copies

    def gather_z(buf, sems):
        for d in range(1, Z):
            s = (z + Z - d) % Z
            remote(buf.at[s], buf.at[s], sems, d, d, {"site": z_peer(d)}).wait_recv()
        acc = buf[0]
        for s in range(1, Z):
            acc = acc + buf[s]
        return acc

    def gather_x(buf, sems):
        for d in range(1, nx):
            s = (x + nx - d) % nx
            remote(buf.at[s], buf.at[s], sems, d, d, {"site": x_peer(d)}).wait_recv()
        acc = buf[0]
        for s in range(1, nx):
            acc = acc + buf[s]
        return acc

    started = []

    loads[0].wait()
    loads[1].wait()
    for load in loads[6:]:
        load.start()
    f = factors[...]
    hi, lo = split(f)
    fs[0:16, :] = hi
    fs[16:32, :] = lo
    fs[32:48, :] = hi
    window[:, RIM:] = f
    l_hi, l_lo = split(loadings[...])
    ls = jnp.concatenate([l_hi, l_hi, l_lo], axis=0)

    def draw_step(i, acc):
        r0 = pl.multiple_of(i * CHUNK, CHUNK)
        mean = dot(fs[:, pl.ds(r0, CHUNK)], ls, ((0,), (0,)))
        there = presence[pl.ds(r0, CHUNK), :] > 0
        t = jnp.where(there, mean, -mean)
        u = jnp.abs(t)
        density = jnp.exp(-0.5 * t * t) * inv_root_two_pi
        num = poly(N_COEF, u)
        den = poly(D_COEF, u)
        full = u * den + num
        negative = t < 0.0
        v = jnp.where(negative, num, density * full) / jnp.where(negative, den, full - density * den)
        s = v + jnp.maximum(t, 0.0)
        spread = jnp.maximum(1.0 - v * (v + u), 1e-30)
        draw = jnp.where(there, s, -s) + spread * lax.rsqrt(spread) * noise[pl.ds(r0, CHUNK), :].astype(F32)
        d_hi, d_lo = split(draw)
        utilities[pl.ds(r0, CHUNK), :] = d_hi
        pieces = jnp.concatenate([d_hi, d_lo], axis=1)
        draws[pl.ds(r0, CHUNK), :] = pieces
        return acc + dot(fs[0:32, pl.ds(r0, CHUNK)], pieces, ((1,), (0,)))

    acc = jnp.zeros((2 * K, 2 * species), F32)
    for piece in range(2):
        loads[2 + 2 * piece].wait()
        loads[3 + 2 * piece].wait()
        acc = lax.fori_loop(cuts[piece] // CHUNK, cuts[piece + 1] // CHUNK, draw_step, acc, unroll=True)

    products = dot(fs[0:32, :], fs[0:32, :], ((1,), (1,)))
    gram_part = blocks_sum(products, K, K)
    zeros = jnp.zeros((HALF, 128), F32)
    gram_z[z] = zeros
    gram_z[z, :, 0:K] = gram_part[:HALF]
    gram_z[z, :, K : 2 * K] = gram_part[HALF:]

    pl.semaphore_wait(barrier, len(greeted))

    rim = remote(
        factors.at[:, rows - RIM : rows],
        window.at[:, 0:RIM],
        rim_sems,
        0,
        0,
        {"site": ahead},
    )
    started += spread_z(gram_z, gz_sems)
    reached = sp < RIM // CHUNK

    @pl.when(reached)
    def _():
        rim.start()


    loads[6].wait()
    loads[7].wait()
    acc = lax.fori_loop(cuts[2] // CHUNK, steps, draw_step, acc, unroll=True)
    cross_z[z] = blocks_sum(acc, K, species)
    started += spread_z(cross_z, cz_sems)
    gram_x[x] = gather_z(gram_z, gz_sems)
    started += spread_x(gram_x, gx_sems)

    for load in loads[8:]:
        load.wait()
    base = site * rows + chunk * CHUNK - RIM
    onehot[...] = jnp.zeros_like(onehot)
    iota = lax.broadcasted_iota(jnp.int32, (224, 128), 0)

    def mark(k, carry):
        ids = neighbours[pl.ds(k, 1), :]
        w = jnp.where(ids >= 0, weights[pl.ds(k, 1), :], 0.0)
        for q in range(CHUNK // 128):
            first = pl.multiple_of(RIM - STEP + 128 * q - STEP * k, 32)
            lanes = slice(128 * q, 128 * (q + 1))
            hit = iota == ids[:, lanes] - (base + first)
            onehot[pl.ds(first, 224), lanes] += jnp.where(hit, w[:, lanes], 0.0)
        return carry

    lax.fori_loop(0, NBR, mark, 0)

    @pl.when(reached)
    def _():
        rim.wait()


    def gather_step(b, acc):
        r0 = pl.multiple_of(b * 256, 256)
        m_hi, m_lo = split(onehot[pl.ds(r0, 256), :])
        w_hi, w_lo = split(window[:, pl.ds(pl.multiple_of(c0 + r0, 256), 256)])
        return acc + dot(
            jnp.concatenate([w_hi, w_lo], axis=0),
            jnp.concatenate([m_hi, m_lo], axis=1),
            ((1,), (0,)),
        )

    prior = lax.fori_loop(0, WINDOW // 256, gather_step, jnp.zeros((2 * K, 2 * CHUNK), F32))
    prior = blocks_sum(prior, K, CHUNK)
    inverse = 1.0 / variance[pl.ds(c0, CHUNK)].reshape(1, CHUNK)
    shift = prior * inverse

    cross_x[x] = gather_z(cross_z, cz_sems)
    started += spread_x(cross_x, cx_sems)

    gram = gather_x(gram_x, gx_sems)
    inv_top, inv_bot, _ = cholesky(gram, [precision[k : k + 1, :] for k in range(K)])

    cross = gather_x(cross_x, cx_sems)
    fresh = solve(inv_top, inv_bot, cross)
    new_loadings[...] = fresh

    n_hi, n_lo = split(fresh)
    narrow = jnp.concatenate([n_hi, n_lo], axis=0)
    lgram_part = blocks_sum(dot(narrow, narrow, ((1,), (1,))), K, K)
    zero = jnp.zeros_like(n_hi)
    wide = jnp.concatenate(
        [jnp.concatenate([n_hi, n_hi], axis=1), jnp.concatenate([n_lo, zero], axis=1)],
        axis=0,
    )

    def pull_of(t, c):
        r0 = pl.multiple_of((t * CORES + c) * CHUNK, CHUNK)
        p = dot(wide, draws[pl.ds(r0, CHUNK), :], ((1,), (1,)))
        return p[:K] + p[K:]

    order = far_first(ny)
    order.remove(busy)
    order.append(busy)
    for e in order:
        pull_out[e - 1] = pull_of((y + e) % busy, 1 - core)
    lgram_all[sp] = zeros
    lgram_all[sp, :, 0:K] = lgram_part[:HALF]
    lgram_all[sp, :, K : 2 * K] = lgram_part[HALF:]
    for e in order:
        copy = remote(pull_out.at[e - 1], pull_pair.at[e - 1], pp_sems, e - 1, e - 1, {"sp": pair})
        copy.start()
        started.append(copy)

    for o in sorted(range(1, n_sp), key=lambda o: -min(o // CORES, ny - o // CORES)):
        copy = remote(lgram_all.at[sp], lgram_all.at[sp], ly_sems, o, o, {"sp": sp_peer(o)})
        copy.start()
        started.append(copy)

    for e in order:
        pull_mine[e - 1] = pull_of((y + e) % busy, core)
    for e in order:
        t = (y + e) % busy
        remote(pull_out.at[e - 1], pull_pair.at[e - 1], pp_sems, e - 1, e - 1, {"sp": pair}).wait_recv()
        pull_mine[e - 1] += pull_pair[e - 1]
        copy = remote(pull_mine.at[e - 1], pull_y.at[y], py_sems, e, y, {"sp": t * CORES + core})
        if e < busy:
            copy.start()
            started.append(copy)
        else:

            @pl.when(y == busy)
            def _():
                copy.start()

            last_pull = copy

    for o in range(1, n_sp):
        s = ((y + ny - o // CORES) % ny) * CORES + (core + o) % CORES
        remote(lgram_all.at[s], lgram_all.at[s], ly_sems, o, o, {"sp": s}).wait_recv()

    def factors_to(sems, send, recv, index, peer):
        lanes = pl.ds(pl.multiple_of(index * CHUNK, CHUNK), CHUNK)
        return remote(new_factors.at[:, lanes], new_factors.at[:, lanes], sems, send, recv, peer)

    @pl.when(y < busy)
    def _():
        lgram = lgram_all[0]
        for s in range(1, n_sp):
            lgram = lgram + lgram_all[s]
        site_top, site_bot, pivots = cholesky(lgram, [inverse] * K)
        total = pull_mine[busy - 1] + (shift + apply_pivots(pivots, factor_noise[...]))
        for d in range(1, ny):
            s = (y + d) % ny
            remote(pull_y.at[s], pull_y.at[s], py_sems, 0, s, {"sp": s * CORES + core}).wait_recv()
            total = total + pull_y[s]
        result = solve(site_top, site_bot, total)
        new_factors[:, pl.ds(c0, CHUNK)] = result
        for d in far_first(ny):
            t = (y + d) % ny
            factors_to(fy_sems, d, y, y * CORES + core, {"sp": t * CORES + core}).start()
        factors_to(fp_sems, y, y, y * CORES + core, {"sp": pair}).start()

    for copy in started:
        copy.wait_send()

    for e in order[busy - 2 :: -1] + [busy]:
        s = (y + busy - e) % busy

        def hand_on():
            factors_to(fy_sems, 0, s, s * CORES + core, {"sp": s * CORES + core}).wait_recv()
            factors_to(fp_sems, s, s, s * CORES + core, {"sp": pair}).start()

        if e < busy:
            hand_on()
        else:
            pl.when(y == busy)(hand_on)

    for s in range(busy):
        factors_to(fp_sems, s, s, s * CORES + (1 - core), {"sp": pair}).wait_recv()

    for s in range(busy):
        factors_to(fp_sems, s, s, s * CORES + core, {"sp": pair}).wait_send()

    @pl.when(y == busy)
    def _():
        last_pull.wait_send()

    @pl.when(y < busy)
    def _():
        for d in range(1, ny):
            t = (y + d) % ny
            factors_to(fy_sems, d, y, y * CORES + core, {"sp": t * CORES + core}).wait_send()


def write_out(a, b, c, a_out, b_out, c_out, sems):
    cut = a.shape[0] // PIECES
    rows = [slice(i * cut, (i + 1) * cut) for i in range(PIECES)]
    pairs = [(c, c_out), (b, b_out)] + [(a.at[r], a_out.at[r]) for r in rows]
    writes = [pltpu.make_async_copy(src, dst, sems.at[i]) for i, (src, dst) in enumerate(pairs)]
    for write in writes:
        write.start()
    for write in writes:
        write.wait()


def solution(mesh):
    n_site, n_sp = mesh.shape["site"], mesh.shape["sp"]
    nx, ny = n_site // Z, n_sp // CORES
    busy = ny - 1

    def shards(presence, noise, factors, loadings, precision, neighbours, weights, variance, factor_noise):
        rows, species = presence.shape
        assert rows == busy * CORES * CHUNK and species == 128
        vmem = pl.BlockSpec(memory_space=pltpu.VMEM)
        hbm = pl.BlockSpec(memory_space=pltpu.HBM)
        sems = pltpu.SemaphoreType.DMA
        out_shape = (
            jax.ShapeDtypeStruct((rows, species), BF16),
            jax.ShapeDtypeStruct((K, species), F32),
            jax.ShapeDtypeStruct((K, rows), F32),
        )
        results = pl.pallas_call(
            functools.partial(kernel, n_site, n_sp),
            out_shape=tuple(pltpu.VMEM(v.shape, v.dtype) for v in out_shape),
            in_specs=[hbm] * 9,
            out_specs=(vmem,) * 3,
            scratch_shapes=[
                pltpu.VMEM((rows, species), jnp.int32),
                pltpu.VMEM((rows, species), BF16),
                pltpu.VMEM((K, rows), F32),
                pltpu.VMEM((K, species), F32),
                pltpu.VMEM((K, species), F32),
                pltpu.VMEM((NBR, CHUNK), jnp.int32),
                pltpu.VMEM((NBR, CHUNK), F32),
                pltpu.VMEM((rows,), F32),
                pltpu.VMEM((K, CHUNK), F32),
                sems((13,)),
                pltpu.VMEM((3 * K, rows), BF16),
                pltpu.VMEM((rows, 2 * species), BF16),
                pltpu.VMEM((K, RIM + rows), F32),
                pltpu.VMEM((WINDOW, CHUNK), F32),
                pltpu.VMEM((Z, HALF, 128), F32),
                pltpu.VMEM((nx, HALF, 128), F32),
                pltpu.VMEM((Z, K, species), F32),
                pltpu.VMEM((nx, K, species), F32),
                pltpu.VMEM((n_sp, HALF, 128), F32),
                pltpu.VMEM((busy, K, CHUNK), F32),
                pltpu.VMEM((busy, K, CHUNK), F32),
                pltpu.VMEM((busy, K, CHUNK), F32),
                pltpu.VMEM((ny, K, CHUNK), F32),
                sems((2, 1)),
                sems((2, Z)),
                sems((2, nx)),
                sems((2, Z)),
                sems((2, nx)),
                sems((2, n_sp)),
                sems((2, busy)),
                sems((2, ny)),
                sems((2, ny)),
                sems((2, busy)),
            ],
            compiler_params=pltpu.CompilerParams(
                collective_id=0,
                has_side_effects=True,
                vmem_limit_bytes=60 * 1024 * 1024,
            ),
        )(presence, noise, factors, loadings, precision, neighbours, weights, variance, factor_noise)
        return pl.pallas_call(
            write_out,
            out_shape=out_shape,
            in_specs=[vmem] * 3,
            out_specs=(hbm,) * 3,
            scratch_shapes=[sems((PIECES + 2,))],
        )(*[pltpu.with_memory_space_constraint(v, pltpu.VMEM) for v in results])

    in_specs = (
        P("site", "sp"),
        P("site", "sp"),
        P(None, "site"),
        P(None, "sp"),
        P(None, "sp"),
        P(None, "site"),
        P(None, "site"),
        P("site"),
        P(None, "site"),
    )
    out_specs = (P("site", "sp"), P(None, "sp"), P(None, "site"))
    return jax.shard_map(shards, mesh=mesh, in_specs=in_specs, out_specs=out_specs, check_vma=False)
```

```python
import functools

import jax
import jax.numpy as jnp
from jax import lax
from jax.experimental import pallas as pl
from jax.experimental.pallas import tpu as pltpu
from jax.sharding import PartitionSpec as P

F32 = jnp.float32
BF16 = jnp.bfloat16
MESH = pl.DeviceIdType.MESH

Z = 8
CORES = 2
K = 16
NBR = 15
CHUNK = 256
RIM = 1536
WINDOW = RIM + CHUNK
HALF = 8
STEP = 96
PIECES = 4

N_COEF = (0.7978845828848753, 0.561783412736638, 0.19921040380039692, 0.039025408597369395, 0.0036777514496204662)
D_COEF = (1.0, 1.1595221251207712, 0.6411219754723788, 0.20649649681102156, 0.03902744122918637, 0.003677727281734947)
inv_root_two_pi = 0.3989422804014327


def poly(coef, u):
    acc = u * coef[-1] + coef[-2]
    for a in coef[-3::-1]:
        acc = acc * u + a
    return acc


def split(x):
    hi = x.astype(BF16)
    return hi, (x - hi.astype(F32)).astype(BF16)


def dot(a, b, dims):
    return lax.dot_general(a, b, (dims, ((), ())), preferred_element_type=F32)


def blocks_sum(p, rows, cols):
    return (p[:rows, :cols] + p[:rows, cols:]) + (p[rows:, :cols] + p[rows:, cols:])


def cholesky(base, extra):
    width = extra[0].shape[1]
    row = lax.broadcasted_iota(jnp.int32, (HALF, width), 0)
    top, bot = [], []
    for k in range(K):
        diag = jnp.where(row == k % HALF, extra[k], 0.0)
        lower = base[:, K + k : K + k + 1]
        if k < HALF:
            top.append(base[:, k : k + 1] + diag)
            bot.append(lower + jnp.zeros_like(diag))
        else:
            top.append(None)
            bot.append(lower + diag)
    inv_top = [jnp.where(row == k, 1.0, 0.0) if k < HALF else jnp.zeros((HALF, width), F32) for k in range(K)]
    inv_bot = [None if k < HALF else jnp.where(row == k - HALF, 1.0, 0.0) for k in range(K)]
    pivots = []
    for j in range(K):
        d = top[j][j : j + 1] if j < HALF else bot[j][j - HALF : j - HALF + 1]
        r = lax.rsqrt(d)
        pivots.append(d * r)
        bot[j] = bot[j] * r
        inv_top[j] = inv_top[j] * r
        if j < HALF:
            top[j] = top[j] * r
        else:
            inv_bot[j] = inv_bot[j] * r
        for k in range(j + 1, K):
            if k < HALF:
                s = top[j][k : k + 1]
                top[k] = top[k] - top[j] * s
                bot[k] = bot[k] - bot[j] * s
            else:
                s = bot[j][k - HALF : k - HALF + 1]
                bot[k] = bot[k] - bot[j] * s
            inv_top[k] = inv_top[k] - inv_top[j] * s
            if j >= HALF:
                inv_bot[k] = inv_bot[k] - inv_bot[j] * s
    return inv_top, inv_bot, pivots


def apply_pivots(pivots, noise):
    row = lax.broadcasted_iota(jnp.int32, noise.shape, 0)
    acc = jnp.zeros_like(noise)
    for j in range(K):
        acc = jnp.where(row == j, pivots[j], acc)
    return acc * noise


def solve(inv_top, inv_bot, rhs):
    top, bot = rhs[:HALF], rhs[HALF:]
    x_top = x_bot = None
    for j in range(K):
        terms = inv_top[j] * top
        if j >= HALF:
            terms = terms + inv_bot[j] * bot
        y = jnp.sum(terms, axis=0, keepdims=True)
        x_top = inv_top[j] * y if x_top is None else x_top + inv_top[j] * y
        if j >= HALF:
            x_bot = inv_bot[j] * y if x_bot is None else x_bot + inv_bot[j] * y
    return jnp.concatenate([x_top, x_bot], axis=0)


def far_first(n):
    return sorted(range(1, n), key=lambda d: -min(d, n - d))


def kernel(
    n_site,
    n_sp,
    presence_hbm,
    noise_hbm,
    factors_hbm,
    loadings_hbm,
    precision_hbm,
    neighbours_hbm,
    weights_hbm,
    variance_hbm,
    factor_noise_hbm,
    utilities,
    new_loadings,
    new_factors,
    presence,
    noise,
    factors,
    loadings,
    precision,
    neighbours,
    weights,
    variance,
    factor_noise,
    in_sems,
    fs,
    draws,
    window,
    onehot,
    gram_z,
    gram_x,
    cross_z,
    cross_x,
    lgram_all,
    pull_out,
    pull_pair,
    pull_mine,
    pull_y,
    rim_sems,
    gz_sems,
    gx_sems,
    cz_sems,
    cx_sems,
    ly_sems,
    pp_sems,
    py_sems,
    fy_sems,
    fp_sems,
):
    nx = n_site // Z
    ny = n_sp // CORES
    busy = ny - 1
    rows = factors.shape[1]
    steps = rows // CHUNK
    cuts = [CHUNK * (steps * i // 14) for i in (0, 2, 7, 11, 14)]
    species = loadings.shape[1]

    site = lax.axis_index("site")
    sp = lax.axis_index("sp")
    x, z = site // Z, site % Z
    y, core = sp // CORES, sp % CORES
    pair = y * CORES + (1 - core)
    ahead = (site + 1) % n_site
    behind = (site + n_site - 1) % n_site

    def z_peer(d):
        return x * Z + (z + d) % Z

    def sp_peer(o):
        return ((y + o // CORES) % ny) * CORES + (core + o) % CORES

    def x_peer(d):
        return ((x + d) % nx) * Z + z

    chunk = jnp.minimum(sp, CORES * busy - 1)
    c0 = pl.multiple_of(chunk * CHUNK, CHUNK)
    mine = pl.ds(c0, CHUNK)
    loads = [(factors_hbm, factors), (loadings_hbm, loadings)]
    for a, b in zip(cuts, cuts[1:]):
        loads.append((presence_hbm.at[a:b], presence.at[a:b]))
        loads.append((noise_hbm.at[a:b], noise.at[a:b]))
    loads += [
        (neighbours_hbm.at[:, mine], neighbours),
        (weights_hbm.at[:, mine], weights),
        (precision_hbm, precision),
        (variance_hbm, variance),
        (factor_noise_hbm.at[:, mine], factor_noise),
    ]
    loads = [pltpu.make_async_copy(a, b, in_sems.at[i]) for i, (a, b) in enumerate(loads)]
    for load in loads[:6]:
        load.start()

    barrier = pltpu.get_barrier_semaphore()
    greeted = [{"site": z_peer(d)} for d in range(1, Z)]
    greeted += [{"site": x_peer(d)} for d in range(1, nx)]
    greeted += [{"site": ahead}, {"site": behind}]
    greeted += [{"sp": sp_peer(o)} for o in range(1, n_sp)]
    for peer in greeted:
        pl.semaphore_signal(barrier, inc=1, device_id=peer, device_id_type=MESH)

    def remote(src, dst, sems, send, recv, peer):
        return pltpu.make_async_remote_copy(
            src_ref=src,
            dst_ref=dst,
            send_sem=sems.at[0, send],
            recv_sem=sems.at[1, recv],
            device_id=peer,
            device_id_type=MESH,
        )

    def spread_z(buf, sems):
        copies = []
        for d in far_first(Z):
            copy = remote(buf.at[z], buf.at[z], sems, d, d, {"site": z_peer(d)})
            copy.start()
            copies.append(copy)
        return copies

    def spread_x(buf, sems):
        copies = []
        for d in far_first(nx):
            copy = remote(buf.at[x], buf.at[x], sems, d, d, {"site": x_peer(d)})
            copy.start()
            copies.append(copy)
        return copies

    def gather_z(buf, sems):
        for d in range(1, Z):
            s = (z + Z - d) % Z
            remote(buf.at[s], buf.at[s], sems, d, d, {"site": z_peer(d)}).wait_recv()
        acc = buf[0]
        for s in range(1, Z):
            acc = acc + buf[s]
        return acc

    def gather_x(buf, sems):
        for d in range(1, nx):
            s = (x + nx - d) % nx
            remote(buf.at[s], buf.at[s], sems, d, d, {"site": x_peer(d)}).wait_recv()
        acc = buf[0]
        for s in range(1, nx):
            acc = acc + buf[s]
        return acc

    started = []

    loads[0].wait()
    loads[1].wait()
    for load in loads[6:]:
        load.start()
    f = factors[...]
    hi, lo = split(f)
    fs[0:16, :] = hi
    fs[16:32, :] = lo
    fs[32:48, :] = hi
    window[:, RIM:] = f
    l_hi, l_lo = split(loadings[...])
    ls = jnp.concatenate([l_hi, l_hi, l_lo], axis=0)

    def draw_step(i, acc):
        r0 = pl.multiple_of(i * CHUNK, CHUNK)
        mean = dot(fs[:, pl.ds(r0, CHUNK)], ls, ((0,), (0,)))
        there = presence[pl.ds(r0, CHUNK), :] > 0
        t = jnp.where(there, mean, -mean)
        u = jnp.abs(t)
        density = jnp.exp(-0.5 * t * t) * inv_root_two_pi
        num = poly(N_COEF, u)
        den = poly(D_COEF, u)
        full = u * den + num
        negative = t < 0.0
        v = jnp.where(negative, num, density * full) / jnp.where(negative, den, full - density * den)
        s = v + jnp.maximum(t, 0.0)
        spread = jnp.maximum(1.0 - v * (v + u), 1e-30)
        draw = jnp.where(there, s, -s) + spread * lax.rsqrt(spread) * noise[pl.ds(r0, CHUNK), :].astype(F32)
        d_hi, d_lo = split(draw)
        utilities[pl.ds(r0, CHUNK), :] = d_hi
        pieces = jnp.concatenate([d_hi, d_lo], axis=1)
        draws[pl.ds(r0, CHUNK), :] = pieces
        return acc + dot(fs[0:32, pl.ds(r0, CHUNK)], pieces, ((1,), (0,)))

    acc = jnp.zeros((2 * K, 2 * species), F32)
    for piece in range(3):
        loads[2 + 2 * piece].wait()
        loads[3 + 2 * piece].wait()
        acc = lax.fori_loop(cuts[piece] // CHUNK, cuts[piece + 1] // CHUNK, draw_step, acc, unroll=True)

    products = dot(fs[0:32, :], fs[0:32, :], ((1,), (1,)))
    gram_part = blocks_sum(products, K, K)
    zeros = jnp.zeros((HALF, 128), F32)
    gram_z[z] = zeros
    gram_z[z, :, 0:K] = gram_part[:HALF]
    gram_z[z, :, K : 2 * K] = gram_part[HALF:]

    pl.semaphore_wait(barrier, len(greeted))

    rim = remote(
        factors.at[:, rows - RIM : rows],
        window.at[:, 0:RIM],
        rim_sems,
        0,
        0,
        {"site": ahead},
    )
    started += spread_z(gram_z, gz_sems)
    reached = sp < RIM // CHUNK

    @pl.when(reached)
    def _():
        rim.start()


    loads[8].wait()
    loads[9].wait()
    acc = lax.fori_loop(cuts[3] // CHUNK, steps, draw_step, acc, unroll=True)
    cross_z[z] = blocks_sum(acc, K, species)
    started += spread_z(cross_z, cz_sems)
    gram_x[x] = gather_z(gram_z, gz_sems)
    started += spread_x(gram_x, gx_sems)

    for load in loads[10:]:
        load.wait()
    base = site * rows + chunk * CHUNK - RIM
    onehot[...] = jnp.zeros_like(onehot)
    iota = lax.broadcasted_iota(jnp.int32, (224, 128), 0)

    def mark(k, carry):
        ids = neighbours[pl.ds(k, 1), :]
        w = jnp.where(ids >= 0, weights[pl.ds(k, 1), :], 0.0)
        for q in range(CHUNK // 128):
            first = pl.multiple_of(RIM - STEP + 128 * q - STEP * k, 32)
            lanes = slice(128 * q, 128 * (q + 1))
            hit = iota == ids[:, lanes] - (base + first)
            onehot[pl.ds(first, 224), lanes] += jnp.where(hit, w[:, lanes], 0.0)
        return carry

    lax.fori_loop(0, NBR, mark, 0)

    @pl.when(reached)
    def _():
        rim.wait()


    def gather_step(b, acc):
        r0 = pl.multiple_of(b * 256, 256)
        m_hi, m_lo = split(onehot[pl.ds(r0, 256), :])
        w_hi, w_lo = split(window[:, pl.ds(pl.multiple_of(c0 + r0, 256), 256)])
        return acc + dot(
            jnp.concatenate([w_hi, w_lo], axis=0),
            jnp.concatenate([m_hi, m_lo], axis=1),
            ((1,), (0,)),
        )

    prior = lax.fori_loop(0, WINDOW // 256, gather_step, jnp.zeros((2 * K, 2 * CHUNK), F32))
    prior = blocks_sum(prior, K, CHUNK)
    inverse = 1.0 / variance[pl.ds(c0, CHUNK)].reshape(1, CHUNK)
    shift = prior * inverse

    cross_x[x] = gather_z(cross_z, cz_sems)
    started += spread_x(cross_x, cx_sems)

    gram = gather_x(gram_x, gx_sems)
    inv_top, inv_bot, _ = cholesky(gram, [precision[k : k + 1, :] for k in range(K)])

    cross = gather_x(cross_x, cx_sems)
    fresh = solve(inv_top, inv_bot, cross)
    new_loadings[...] = fresh

    n_hi, n_lo = split(fresh)
    narrow = jnp.concatenate([n_hi, n_lo], axis=0)
    lgram_part = blocks_sum(dot(narrow, narrow, ((1,), (1,))), K, K)
    zero = jnp.zeros_like(n_hi)
    wide = jnp.concatenate(
        [jnp.concatenate([n_hi, n_hi], axis=1), jnp.concatenate([n_lo, zero], axis=1)],
        axis=0,
    )

    def pull_of(t, c):
        r0 = pl.multiple_of((t * CORES + c) * CHUNK, CHUNK)
        p = dot(wide, draws[pl.ds(r0, CHUNK), :], ((1,), (1,)))
        return p[:K] + p[K:]

    order = far_first(ny)
    order.remove(busy)
    order.append(busy)
    for e in order:
        pull_out[e - 1] = pull_of((y + e) % busy, 1 - core)
    lgram_all[sp] = zeros
    lgram_all[sp, :, 0:K] = lgram_part[:HALF]
    lgram_all[sp, :, K : 2 * K] = lgram_part[HALF:]
    for e in order:
        copy = remote(pull_out.at[e - 1], pull_pair.at[e - 1], pp_sems, e - 1, e - 1, {"sp": pair})
        copy.start()
        started.append(copy)

    for o in sorted(range(1, n_sp), key=lambda o: -min(o // CORES, ny - o // CORES)):
        copy = remote(lgram_all.at[sp], lgram_all.at[sp], ly_sems, o, o, {"sp": sp_peer(o)})
        copy.start()
        started.append(copy)

    for e in order:
        pull_mine[e - 1] = pull_of((y + e) % busy, core)
    for e in order:
        t = (y + e) % busy
        remote(pull_out.at[e - 1], pull_pair.at[e - 1], pp_sems, e - 1, e - 1, {"sp": pair}).wait_recv()
        pull_mine[e - 1] += pull_pair[e - 1]
        copy = remote(pull_mine.at[e - 1], pull_y.at[y], py_sems, e, y, {"sp": t * CORES + core})
        if e < busy:
            copy.start()
            started.append(copy)
        else:

            @pl.when(y == busy)
            def _():
                copy.start()

            last_pull = copy

    for o in range(1, n_sp):
        s = ((y + ny - o // CORES) % ny) * CORES + (core + o) % CORES
        remote(lgram_all.at[s], lgram_all.at[s], ly_sems, o, o, {"sp": s}).wait_recv()

    def factors_to(sems, send, recv, index, peer):
        lanes = pl.ds(pl.multiple_of(index * CHUNK, CHUNK), CHUNK)
        return remote(new_factors.at[:, lanes], new_factors.at[:, lanes], sems, send, recv, peer)

    @pl.when(y < busy)
    def _():
        lgram = lgram_all[0]
        for s in range(1, n_sp):
            lgram = lgram + lgram_all[s]
        site_top, site_bot, pivots = cholesky(lgram, [inverse] * K)
        total = pull_mine[busy - 1] + (shift + apply_pivots(pivots, factor_noise[...]))
        for d in range(1, ny):
            s = (y + d) % ny
            remote(pull_y.at[s], pull_y.at[s], py_sems, 0, s, {"sp": s * CORES + core}).wait_recv()
            total = total + pull_y[s]
        result = solve(site_top, site_bot, total)
        new_factors[:, pl.ds(c0, CHUNK)] = result
        for d in far_first(ny):
            t = (y + d) % ny
            factors_to(fy_sems, d, y, y * CORES + core, {"sp": t * CORES + core}).start()
        factors_to(fp_sems, y, y, y * CORES + core, {"sp": pair}).start()

    for copy in started:
        copy.wait_send()

    for e in order[busy - 2 :: -1] + [busy]:
        s = (y + busy - e) % busy

        def hand_on():
            factors_to(fy_sems, 0, s, s * CORES + core, {"sp": s * CORES + core}).wait_recv()
            factors_to(fp_sems, s, s, s * CORES + core, {"sp": pair}).start()

        if e < busy:
            hand_on()
        else:
            pl.when(y == busy)(hand_on)

    for s in range(busy):
        factors_to(fp_sems, s, s, s * CORES + (1 - core), {"sp": pair}).wait_recv()

    for s in range(busy):
        factors_to(fp_sems, s, s, s * CORES + core, {"sp": pair}).wait_send()

    @pl.when(y == busy)
    def _():
        last_pull.wait_send()

    @pl.when(y < busy)
    def _():
        for d in range(1, ny):
            t = (y + d) % ny
            factors_to(fy_sems, d, y, y * CORES + core, {"sp": t * CORES + core}).wait_send()


def write_out(a, b, c, a_out, b_out, c_out, sems):
    cut = a.shape[0] // PIECES
    rows = [slice(i * cut, (i + 1) * cut) for i in range(PIECES)]
    pairs = [(c, c_out), (b, b_out)] + [(a.at[r], a_out.at[r]) for r in rows]
    writes = [pltpu.make_async_copy(src, dst, sems.at[i]) for i, (src, dst) in enumerate(pairs)]
    for write in writes:
        write.start()
    for write in writes:
        write.wait()


def solution(mesh):
    n_site, n_sp = mesh.shape["site"], mesh.shape["sp"]
    nx, ny = n_site // Z, n_sp // CORES
    busy = ny - 1

    def shards(presence, noise, factors, loadings, precision, neighbours, weights, variance, factor_noise):
        rows, species = presence.shape
        assert rows == busy * CORES * CHUNK and species == 128
        vmem = pl.BlockSpec(memory_space=pltpu.VMEM)
        hbm = pl.BlockSpec(memory_space=pltpu.HBM)
        sems = pltpu.SemaphoreType.DMA
        out_shape = (
            jax.ShapeDtypeStruct((rows, species), BF16),
            jax.ShapeDtypeStruct((K, species), F32),
            jax.ShapeDtypeStruct((K, rows), F32),
        )
        results = pl.pallas_call(
            functools.partial(kernel, n_site, n_sp),
            out_shape=tuple(pltpu.VMEM(v.shape, v.dtype) for v in out_shape),
            in_specs=[hbm] * 9,
            out_specs=(vmem,) * 3,
            scratch_shapes=[
                pltpu.VMEM((rows, species), jnp.int32),
                pltpu.VMEM((rows, species), BF16),
                pltpu.VMEM((K, rows), F32),
                pltpu.VMEM((K, species), F32),
                pltpu.VMEM((K, species), F32),
                pltpu.VMEM((NBR, CHUNK), jnp.int32),
                pltpu.VMEM((NBR, CHUNK), F32),
                pltpu.VMEM((rows,), F32),
                pltpu.VMEM((K, CHUNK), F32),
                sems((15,)),
                pltpu.VMEM((3 * K, rows), BF16),
                pltpu.VMEM((rows, 2 * species), BF16),
                pltpu.VMEM((K, RIM + rows), F32),
                pltpu.VMEM((WINDOW, CHUNK), F32),
                pltpu.VMEM((Z, HALF, 128), F32),
                pltpu.VMEM((nx, HALF, 128), F32),
                pltpu.VMEM((Z, K, species), F32),
                pltpu.VMEM((nx, K, species), F32),
                pltpu.VMEM((n_sp, HALF, 128), F32),
                pltpu.VMEM((busy, K, CHUNK), F32),
                pltpu.VMEM((busy, K, CHUNK), F32),
                pltpu.VMEM((busy, K, CHUNK), F32),
                pltpu.VMEM((ny, K, CHUNK), F32),
                sems((2, 1)),
                sems((2, Z)),
                sems((2, nx)),
                sems((2, Z)),
                sems((2, nx)),
                sems((2, n_sp)),
                sems((2, busy)),
                sems((2, ny)),
                sems((2, ny)),
                sems((2, busy)),
            ],
            compiler_params=pltpu.CompilerParams(
                collective_id=0,
                has_side_effects=True,
                vmem_limit_bytes=60 * 1024 * 1024,
            ),
        )(presence, noise, factors, loadings, precision, neighbours, weights, variance, factor_noise)
        return pl.pallas_call(
            write_out,
            out_shape=out_shape,
            in_specs=[vmem] * 3,
            out_specs=(hbm,) * 3,
            scratch_shapes=[sems((PIECES + 2,))],
        )(*[pltpu.with_memory_space_constraint(v, pltpu.VMEM) for v in results])

    in_specs = (
        P("site", "sp"),
        P("site", "sp"),
        P(None, "site"),
        P(None, "sp"),
        P(None, "sp"),
        P(None, "site"),
        P(None, "site"),
        P("site"),
        P(None, "site"),
    )
    out_specs = (P("site", "sp"), P(None, "sp"), P(None, "site"))
    return jax.shard_map(shards, mesh=mesh, in_specs=in_specs, out_specs=out_specs, check_vma=False)
```

```python
import functools

import jax
import jax.numpy as jnp
from jax import lax
from jax.experimental import pallas as pl
from jax.experimental.pallas import tpu as pltpu
from jax.sharding import PartitionSpec as P

F32 = jnp.float32
BF16 = jnp.bfloat16
MESH = pl.DeviceIdType.MESH

Z = 8
CORES = 2
K = 16
NBR = 15
CHUNK = 256
RIM = 1536
WINDOW = RIM + CHUNK
HALF = 8
STEP = 96
PIECES = 4

N_COEF = (0.7978845828848753, 0.561783412736638, 0.19921040380039692, 0.039025408597369395, 0.0036777514496204662)
D_COEF = (1.0, 1.1595221251207712, 0.6411219754723788, 0.20649649681102156, 0.03902744122918637, 0.003677727281734947)
inv_root_two_pi = 0.3989422804014327


def poly(coef, u):
    acc = u * coef[-1] + coef[-2]
    for a in coef[-3::-1]:
        acc = acc * u + a
    return acc


def split(x):
    hi = x.astype(BF16)
    return hi, (x - hi.astype(F32)).astype(BF16)


def dot(a, b, dims):
    return lax.dot_general(a, b, (dims, ((), ())), preferred_element_type=F32)


def blocks_sum(p, rows, cols):
    return (p[:rows, :cols] + p[:rows, cols:]) + (p[rows:, :cols] + p[rows:, cols:])


def cholesky(base, extra):
    width = extra[0].shape[1]
    row = lax.broadcasted_iota(jnp.int32, (HALF, width), 0)
    top, bot = [], []
    for k in range(K):
        diag = jnp.where(row == k % HALF, extra[k], 0.0)
        lower = base[:, K + k : K + k + 1]
        if k < HALF:
            top.append(base[:, k : k + 1] + diag)
            bot.append(lower + jnp.zeros_like(diag))
        else:
            top.append(None)
            bot.append(lower + diag)
    inv_top = [jnp.where(row == k, 1.0, 0.0) if k < HALF else jnp.zeros((HALF, width), F32) for k in range(K)]
    inv_bot = [None if k < HALF else jnp.where(row == k - HALF, 1.0, 0.0) for k in range(K)]
    pivots = []
    for j in range(K):
        d = top[j][j : j + 1] if j < HALF else bot[j][j - HALF : j - HALF + 1]
        r = lax.rsqrt(d)
        pivots.append(d * r)
        bot[j] = bot[j] * r
        inv_top[j] = inv_top[j] * r
        if j < HALF:
            top[j] = top[j] * r
        else:
            inv_bot[j] = inv_bot[j] * r
        for k in range(j + 1, K):
            if k < HALF:
                s = top[j][k : k + 1]
                top[k] = top[k] - top[j] * s
                bot[k] = bot[k] - bot[j] * s
            else:
                s = bot[j][k - HALF : k - HALF + 1]
                bot[k] = bot[k] - bot[j] * s
            inv_top[k] = inv_top[k] - inv_top[j] * s
            if j >= HALF:
                inv_bot[k] = inv_bot[k] - inv_bot[j] * s
    return inv_top, inv_bot, pivots


def apply_pivots(pivots, noise):
    row = lax.broadcasted_iota(jnp.int32, noise.shape, 0)
    acc = jnp.zeros_like(noise)
    for j in range(K):
        acc = jnp.where(row == j, pivots[j], acc)
    return acc * noise


def solve(inv_top, inv_bot, rhs):
    top, bot = rhs[:HALF], rhs[HALF:]
    x_top = x_bot = None
    for j in range(K):
        terms = inv_top[j] * top
        if j >= HALF:
            terms = terms + inv_bot[j] * bot
        y = jnp.sum(terms, axis=0, keepdims=True)
        x_top = inv_top[j] * y if x_top is None else x_top + inv_top[j] * y
        if j >= HALF:
            x_bot = inv_bot[j] * y if x_bot is None else x_bot + inv_bot[j] * y
    return jnp.concatenate([x_top, x_bot], axis=0)


def far_first(n):
    return sorted(range(1, n), key=lambda d: -min(d, n - d))


def kernel(
    n_site,
    n_sp,
    presence_hbm,
    noise_hbm,
    factors_hbm,
    loadings_hbm,
    precision_hbm,
    neighbours_hbm,
    weights_hbm,
    variance_hbm,
    factor_noise_hbm,
    utilities,
    new_loadings,
    new_factors,
    presence,
    noise,
    factors,
    loadings,
    precision,
    neighbours,
    weights,
    variance,
    factor_noise,
    in_sems,
    fs,
    draws,
    window,
    onehot,
    gram_z,
    gram_x,
    cross_z,
    cross_x,
    lgram_all,
    pull_out,
    pull_pair,
    pull_mine,
    pull_y,
    rim_sems,
    gz_sems,
    gx_sems,
    cz_sems,
    cx_sems,
    ly_sems,
    pp_sems,
    py_sems,
    fy_sems,
    fp_sems,
):
    nx = n_site // Z
    ny = n_sp // CORES
    busy = ny - 1
    rows = factors.shape[1]
    steps = rows // CHUNK
    cuts = [CHUNK * (steps * i // 14) for i in (0, 1, 4, 9, 14)]
    species = loadings.shape[1]

    site = lax.axis_index("site")
    sp = lax.axis_index("sp")
    x, z = site // Z, site % Z
    y, core = sp // CORES, sp % CORES
    pair = y * CORES + (1 - core)
    ahead = (site + 1) % n_site
    behind = (site + n_site - 1) % n_site

    def z_peer(d):
        return x * Z + (z + d) % Z

    def sp_peer(o):
        return ((y + o // CORES) % ny) * CORES + (core + o) % CORES

    def x_peer(d):
        return ((x + d) % nx) * Z + z

    chunk = jnp.minimum(sp, CORES * busy - 1)
    c0 = pl.multiple_of(chunk * CHUNK, CHUNK)
    mine = pl.ds(c0, CHUNK)
    loads = [(factors_hbm, factors), (loadings_hbm, loadings)]
    for a, b in zip(cuts, cuts[1:]):
        loads.append((presence_hbm.at[a:b], presence.at[a:b]))
        loads.append((noise_hbm.at[a:b], noise.at[a:b]))
    loads += [
        (neighbours_hbm.at[:, mine], neighbours),
        (weights_hbm.at[:, mine], weights),
        (precision_hbm, precision),
        (variance_hbm, variance),
        (factor_noise_hbm.at[:, mine], factor_noise),
    ]
    loads = [pltpu.make_async_copy(a, b, in_sems.at[i]) for i, (a, b) in enumerate(loads)]
    for load in loads[:6]:
        load.start()

    barrier = pltpu.get_barrier_semaphore()
    greeted = [{"site": z_peer(d)} for d in range(1, Z)]
    greeted += [{"site": x_peer(d)} for d in range(1, nx)]
    greeted += [{"site": ahead}, {"site": behind}]
    greeted += [{"sp": sp_peer(o)} for o in range(1, n_sp)]
    for peer in greeted:
        pl.semaphore_signal(barrier, inc=1, device_id=peer, device_id_type=MESH)

    def remote(src, dst, sems, send, recv, peer):
        return pltpu.make_async_remote_copy(
            src_ref=src,
            dst_ref=dst,
            send_sem=sems.at[0, send],
            recv_sem=sems.at[1, recv],
            device_id=peer,
            device_id_type=MESH,
        )

    def spread_z(buf, sems):
        copies = []
        for d in far_first(Z):
            copy = remote(buf.at[z], buf.at[z], sems, d, d, {"site": z_peer(d)})
            copy.start()
            copies.append(copy)
        return copies

    def spread_x(buf, sems):
        copies = []
        for d in far_first(nx):
            copy = remote(buf.at[x], buf.at[x], sems, d, d, {"site": x_peer(d)})
            copy.start()
            copies.append(copy)
        return copies

    def gather_z(buf, sems):
        for d in range(1, Z):
            s = (z + Z - d) % Z
            remote(buf.at[s], buf.at[s], sems, d, d, {"site": z_peer(d)}).wait_recv()
        acc = buf[0]
        for s in range(1, Z):
            acc = acc + buf[s]
        return acc

    def gather_x(buf, sems):
        for d in range(1, nx):
            s = (x + nx - d) % nx
            remote(buf.at[s], buf.at[s], sems, d, d, {"site": x_peer(d)}).wait_recv()
        acc = buf[0]
        for s in range(1, nx):
            acc = acc + buf[s]
        return acc

    started = []

    loads[0].wait()
    loads[1].wait()
    for load in loads[6:]:
        load.start()
    f = factors[...]
    hi, lo = split(f)
    fs[0:16, :] = hi
    fs[16:32, :] = lo
    fs[32:48, :] = hi
    window[:, RIM:] = f
    l_hi, l_lo = split(loadings[...])
    ls = jnp.concatenate([l_hi, l_hi, l_lo], axis=0)

    def draw_step(i, acc):
        r0 = pl.multiple_of(i * CHUNK, CHUNK)
        mean = dot(fs[:, pl.ds(r0, CHUNK)], ls, ((0,), (0,)))
        there = presence[pl.ds(r0, CHUNK), :] > 0
        t = jnp.where(there, mean, -mean)
        u = jnp.abs(t)
        density = jnp.exp(-0.5 * t * t) * inv_root_two_pi
        num = poly(N_COEF, u)
        den = poly(D_COEF, u)
        full = u * den + num
        negative = t < 0.0
        v = jnp.where(negative, num, density * full) / jnp.where(negative, den, full - density * den)
        s = v + jnp.maximum(t, 0.0)
        spread = jnp.maximum(1.0 - v * (v + u), 1e-30)
        draw = jnp.where(there, s, -s) + spread * lax.rsqrt(spread) * noise[pl.ds(r0, CHUNK), :].astype(F32)
        d_hi, d_lo = split(draw)
        utilities[pl.ds(r0, CHUNK), :] = d_hi
        pieces = jnp.concatenate([d_hi, d_lo], axis=1)
        draws[pl.ds(r0, CHUNK), :] = pieces
        return acc + dot(fs[0:32, pl.ds(r0, CHUNK)], pieces, ((1,), (0,)))

    acc = jnp.zeros((2 * K, 2 * species), F32)
    for piece in range(3):
        loads[2 + 2 * piece].wait()
        loads[3 + 2 * piece].wait()
        acc = lax.fori_loop(cuts[piece] // CHUNK, cuts[piece + 1] // CHUNK, draw_step, acc, unroll=True)

    products = dot(fs[0:32, :], fs[0:32, :], ((1,), (1,)))
    gram_part = blocks_sum(products, K, K)
    zeros = jnp.zeros((HALF, 128), F32)
    gram_z[z] = zeros
    gram_z[z, :, 0:K] = gram_part[:HALF]
    gram_z[z, :, K : 2 * K] = gram_part[HALF:]

    pl.semaphore_wait(barrier, len(greeted))

    rim = remote(
        factors.at[:, rows - RIM : rows],
        window.at[:, 0:RIM],
        rim_sems,
        0,
        0,
        {"site": ahead},
    )
    started += spread_z(gram_z, gz_sems)
    reached = sp < RIM // CHUNK

    @pl.when(reached)
    def _():
        rim.start()


    loads[8].wait()
    loads[9].wait()
    acc = lax.fori_loop(cuts[3] // CHUNK, steps, draw_step, acc, unroll=True)
    cross_z[z] = blocks_sum(acc, K, species)
    started += spread_z(cross_z, cz_sems)
    gram_x[x] = gather_z(gram_z, gz_sems)
    started += spread_x(gram_x, gx_sems)

    for load in loads[10:]:
        load.wait()
    base = site * rows + chunk * CHUNK - RIM
    onehot[...] = jnp.zeros_like(onehot)
    iota = lax.broadcasted_iota(jnp.int32, (224, 128), 0)

    def mark(k, carry):
        ids = neighbours[pl.ds(k, 1), :]
        w = jnp.where(ids >= 0, weights[pl.ds(k, 1), :], 0.0)
        for q in range(CHUNK // 128):
            first = pl.multiple_of(RIM - STEP + 128 * q - STEP * k, 32)
            lanes = slice(128 * q, 128 * (q + 1))
            hit = iota == ids[:, lanes] - (base + first)
            onehot[pl.ds(first, 224), lanes] += jnp.where(hit, w[:, lanes], 0.0)
        return carry

    lax.fori_loop(0, NBR, mark, 0)

    @pl.when(reached)
    def _():
        rim.wait()


    def gather_step(b, acc):
        r0 = pl.multiple_of(b * 256, 256)
        m_hi, m_lo = split(onehot[pl.ds(r0, 256), :])
        w_hi, w_lo = split(window[:, pl.ds(pl.multiple_of(c0 + r0, 256), 256)])
        return acc + dot(
            jnp.concatenate([w_hi, w_lo], axis=0),
            jnp.concatenate([m_hi, m_lo], axis=1),
            ((1,), (0,)),
        )

    prior = lax.fori_loop(0, WINDOW // 256, gather_step, jnp.zeros((2 * K, 2 * CHUNK), F32))
    prior = blocks_sum(prior, K, CHUNK)
    inverse = 1.0 / variance[pl.ds(c0, CHUNK)].reshape(1, CHUNK)
    shift = prior * inverse

    cross_x[x] = gather_z(cross_z, cz_sems)
    started += spread_x(cross_x, cx_sems)

    gram = gather_x(gram_x, gx_sems)
    inv_top, inv_bot, _ = cholesky(gram, [precision[k : k + 1, :] for k in range(K)])

    cross = gather_x(cross_x, cx_sems)
    fresh = solve(inv_top, inv_bot, cross)
    new_loadings[...] = fresh

    n_hi, n_lo = split(fresh)
    narrow = jnp.concatenate([n_hi, n_lo], axis=0)
    lgram_part = blocks_sum(dot(narrow, narrow, ((1,), (1,))), K, K)
    zero = jnp.zeros_like(n_hi)
    wide = jnp.concatenate(
        [jnp.concatenate([n_hi, n_hi], axis=1), jnp.concatenate([n_lo, zero], axis=1)],
        axis=0,
    )

    def pull_of(t, c):
        r0 = pl.multiple_of((t * CORES + c) * CHUNK, CHUNK)
        p = dot(wide, draws[pl.ds(r0, CHUNK), :], ((1,), (1,)))
        return p[:K] + p[K:]

    order = far_first(ny)
    order.remove(busy)
    order.append(busy)
    for e in order:
        pull_out[e - 1] = pull_of((y + e) % busy, 1 - core)
    lgram_all[sp] = zeros
    lgram_all[sp, :, 0:K] = lgram_part[:HALF]
    lgram_all[sp, :, K : 2 * K] = lgram_part[HALF:]
    for e in order:
        copy = remote(pull_out.at[e - 1], pull_pair.at[e - 1], pp_sems, e - 1, e - 1, {"sp": pair})
        copy.start()
        started.append(copy)

    for o in sorted(range(1, n_sp), key=lambda o: -min(o // CORES, ny - o // CORES)):
        copy = remote(lgram_all.at[sp], lgram_all.at[sp], ly_sems, o, o, {"sp": sp_peer(o)})
        copy.start()
        started.append(copy)

    for e in order:
        pull_mine[e - 1] = pull_of((y + e) % busy, core)
    for e in order:
        t = (y + e) % busy
        remote(pull_out.at[e - 1], pull_pair.at[e - 1], pp_sems, e - 1, e - 1, {"sp": pair}).wait_recv()
        pull_mine[e - 1] += pull_pair[e - 1]
        copy = remote(pull_mine.at[e - 1], pull_y.at[y], py_sems, e, y, {"sp": t * CORES + core})
        if e < busy:
            copy.start()
            started.append(copy)
        else:

            @pl.when(y == busy)
            def _():
                copy.start()

            last_pull = copy

    for o in range(1, n_sp):
        s = ((y + ny - o // CORES) % ny) * CORES + (core + o) % CORES
        remote(lgram_all.at[s], lgram_all.at[s], ly_sems, o, o, {"sp": s}).wait_recv()

    far = (y + ny // 2) % ny

    def factors_to(sems, send, recv, index, peer):
        lanes = pl.ds(pl.multiple_of(index * CHUNK, CHUNK), CHUNK)
        return remote(new_factors.at[:, lanes], new_factors.at[:, lanes], sems, send, recv, peer)

    @pl.when(y < busy)
    def _():
        lgram = lgram_all[0]
        for s in range(1, n_sp):
            lgram = lgram + lgram_all[s]
        site_top, site_bot, pivots = cholesky(lgram, [inverse] * K)
        total = pull_mine[busy - 1] + (shift + apply_pivots(pivots, factor_noise[...]))
        for d in range(1, ny):
            s = (y + d) % ny
            remote(pull_y.at[s], pull_y.at[s], py_sems, 0, s, {"sp": s * CORES + core}).wait_recv()
            total = total + pull_y[s]
        result = solve(site_top, site_bot, total)
        new_factors[:, pl.ds(c0, CHUNK)] = result
        for d in far_first(ny):
            t = (y + d) % ny
            factors_to(fy_sems, d, y, y * CORES + core, {"sp": t * CORES + core}).start()
            if d == ny // 2:
                factors_to(fp_sems, far, y, y * CORES + core, {"sp": far * CORES + (1 - core)}).start()
        factors_to(fp_sems, y, y, y * CORES + core, {"sp": pair}).start()

    for copy in started:
        copy.wait_send()

    for e in order[busy - 2 :: -1] + [busy]:
        s = (y + busy - e) % busy

        def hand_on():
            factors_to(fy_sems, 0, s, s * CORES + core, {"sp": s * CORES + core}).wait_recv()

            @pl.when(s != far)
            def _():
                factors_to(fp_sems, s, s, s * CORES + core, {"sp": pair}).start()

        if e < busy:
            hand_on()
        else:
            pl.when(y == busy)(hand_on)

    for s in range(busy):
        factors_to(fp_sems, s, s, s * CORES + (1 - core), {"sp": pair}).wait_recv()

    for s in range(busy):

        @pl.when((s != far) | (y < busy))
        def _():
            factors_to(fp_sems, s, s, s * CORES + core, {"sp": pair}).wait_send()

    @pl.when(far == busy)
    def _():
        factors_to(fp_sems, far, y, y * CORES + core, {"sp": pair}).wait_send()

    @pl.when(y == busy)
    def _():
        last_pull.wait_send()

    @pl.when(y < busy)
    def _():
        for d in range(1, ny):
            t = (y + d) % ny
            factors_to(fy_sems, d, y, y * CORES + core, {"sp": t * CORES + core}).wait_send()


def write_out(a, b, c, a_out, b_out, c_out, sems):
    cut = a.shape[0] // PIECES
    rows = [slice(i * cut, (i + 1) * cut) for i in range(PIECES)]
    pairs = [(c, c_out), (b, b_out)] + [(a.at[r], a_out.at[r]) for r in rows]
    writes = [pltpu.make_async_copy(src, dst, sems.at[i]) for i, (src, dst) in enumerate(pairs)]
    for write in writes:
        write.start()
    for write in writes:
        write.wait()


def solution(mesh):
    n_site, n_sp = mesh.shape["site"], mesh.shape["sp"]
    nx, ny = n_site // Z, n_sp // CORES
    busy = ny - 1

    def shards(presence, noise, factors, loadings, precision, neighbours, weights, variance, factor_noise):
        rows, species = presence.shape
        assert rows == busy * CORES * CHUNK and species == 128
        vmem = pl.BlockSpec(memory_space=pltpu.VMEM)
        hbm = pl.BlockSpec(memory_space=pltpu.HBM)
        sems = pltpu.SemaphoreType.DMA
        out_shape = (
            jax.ShapeDtypeStruct((rows, species), BF16),
            jax.ShapeDtypeStruct((K, species), F32),
            jax.ShapeDtypeStruct((K, rows), F32),
        )
        results = pl.pallas_call(
            functools.partial(kernel, n_site, n_sp),
            out_shape=tuple(pltpu.VMEM(v.shape, v.dtype) for v in out_shape),
            in_specs=[hbm] * 9,
            out_specs=(vmem,) * 3,
            scratch_shapes=[
                pltpu.VMEM((rows, species), jnp.int32),
                pltpu.VMEM((rows, species), BF16),
                pltpu.VMEM((K, rows), F32),
                pltpu.VMEM((K, species), F32),
                pltpu.VMEM((K, species), F32),
                pltpu.VMEM((NBR, CHUNK), jnp.int32),
                pltpu.VMEM((NBR, CHUNK), F32),
                pltpu.VMEM((rows,), F32),
                pltpu.VMEM((K, CHUNK), F32),
                sems((15,)),
                pltpu.VMEM((3 * K, rows), BF16),
                pltpu.VMEM((rows, 2 * species), BF16),
                pltpu.VMEM((K, RIM + rows), F32),
                pltpu.VMEM((WINDOW, CHUNK), F32),
                pltpu.VMEM((Z, HALF, 128), F32),
                pltpu.VMEM((nx, HALF, 128), F32),
                pltpu.VMEM((Z, K, species), F32),
                pltpu.VMEM((nx, K, species), F32),
                pltpu.VMEM((n_sp, HALF, 128), F32),
                pltpu.VMEM((busy, K, CHUNK), F32),
                pltpu.VMEM((busy, K, CHUNK), F32),
                pltpu.VMEM((busy, K, CHUNK), F32),
                pltpu.VMEM((ny, K, CHUNK), F32),
                sems((2, 1)),
                sems((2, Z)),
                sems((2, nx)),
                sems((2, Z)),
                sems((2, nx)),
                sems((2, n_sp)),
                sems((2, busy)),
                sems((2, ny)),
                sems((2, ny)),
                sems((2, ny)),
            ],
            compiler_params=pltpu.CompilerParams(
                collective_id=0,
                has_side_effects=True,
                vmem_limit_bytes=60 * 1024 * 1024,
            ),
        )(presence, noise, factors, loadings, precision, neighbours, weights, variance, factor_noise)
        return pl.pallas_call(
            write_out,
            out_shape=out_shape,
            in_specs=[vmem] * 3,
            out_specs=(hbm,) * 3,
            scratch_shapes=[sems((PIECES + 2,))],
        )(*[pltpu.with_memory_space_constraint(v, pltpu.VMEM) for v in results])

    in_specs = (
        P("site", "sp"),
        P("site", "sp"),
        P(None, "site"),
        P(None, "sp"),
        P(None, "sp"),
        P(None, "site"),
        P(None, "site"),
        P("site"),
        P(None, "site"),
    )
    out_specs = (P("site", "sp"), P(None, "sp"), P(None, "site"))
    return jax.shard_map(shards, mesh=mesh, in_specs=in_specs, out_specs=out_specs, check_vma=False)
```
